256 devices in a mesh: lat: 8 (over z), lon: 16 (over x, y_hi, core), batch: 2 (over y_lo).
Axes of the slice: x: 4, y: 4 (y_hi: 2, y_lo: 2; y = y_hi * 2 + y_lo), z: 8, core: 2. Of those that a mesh axis runs over, the one named last changes fastest.
Arguments:
- field: bfloat16 [2, 128, 768, 256], P('batch', 'lat', 'lon'), may hold values from -6 to 6
- kernel0: bfloat16 [3, 3, 256, 256], replicated, may hold values from -0.125 to 0.125
- kernel1: bfloat16 [3, 3, 256, 256], replicated, may hold values from -0.125 to 0.125
- mixing: bfloat16 [256, 256], replicated, may hold values from -0.375 to 0.375
- gain: float32 [512, 512], replicated, may hold values from -12 to 12
- cotangent: bfloat16 [2, 128, 768, 256], P('batch', 'lat', 'lon'), may hold values from -6 to 6
Outputs:
- predicted: bfloat16 [2, 128, 768, 256], P('batch', 'lat', 'lon')
- grad_kernel0: float32 [589824], P(('lat', 'lon', 'batch'))
- grad_kernel1: float32 [589824], P(('lat', 'lon', 'batch'))
- grad_mixing: float32 [65536], P(('lat', 'lon', 'batch'))
- grad_gain: float32 [262144], P(('lat', 'lon', 'batch'))
The draws below stay inside these ranges and needn't reach their ends.
All inputs are finite; a program needn't handle non-finite values.
Results may differ from the reference program's by a relative error of at most 0.027.
Values may be sent and summed in bfloat16 or wider, within the bound.
A program may use at most 64 MiB of HBM per device.

```python
import math
import jax
import jax.numpy as jnp
from jax import lax

C = 256
BATCH = 2
LAT0 = 128
LON0 = 768
KL = 16
KM = 32


def block_scale(stream_key, dims, pieces, smallest, top_value):
    factor_of = 1.0
    for dim, shards_of in pieces:
        heights = jax.random.uniform(jax.random.fold_in(jax.random.fold_in(stream_key, 6), dim), (shards_of,), jnp.float32, smallest / len(pieces), top_value / len(pieces))
        factor_of = factor_of * jnp.repeat(jnp.exp(heights), dims[dim] // shards_of).reshape((-1,) + (1,) * (len(dims) - 1 - dim))
    return factor_of


def scatter_about(rng, shape, scale, limit, cuts=(), kind=jnp.bfloat16):
    result = scale * jax.random.normal(rng, shape, jnp.float32)
    if cuts:
        result = result * block_scale(rng, shape, cuts, -0.22, 0.18)
    return jnp.clip(result, -limit, limit).astype(kind)


def setup_inputs(seed: int = 0) -> dict:
    key_list = jax.random.split(jax.random.key(seed), 7)
    return {
        "field": scatter_about(key_list[0], (BATCH, LAT0, LON0, C), 1.0, 6.0, ((0, 2), (1, 8), (2, 16))),
        "kernel0": scatter_about(key_list[1], (3, 3, C, C), (9 * C) ** -0.5, 0.125),
        "kernel1": scatter_about(key_list[2], (3, 3, C, C), (9 * C) ** -0.5, 0.125),
        "mixing": scatter_about(key_list[3], (C, C), C ** -0.5, 0.375),
        "gain": scatter_about(key_list[4], (KL * KM, 2 * C), 3.0, 12.0, (), jnp.float32),
        "cotangent": scatter_about(key_list[5], (BATCH, LAT0, LON0, C), 1.0, 6.0, ((0, 2), (1, 8), (2, 16))),
    }


def activate(preact):
    return jax.nn.gelu(preact, approximate=True)

def activate_grad(preact, upstream):
    return jax.vjp(activate, preact)[1](upstream)[0]

def block_sum(values, factor):
    leading = values.shape[:-3]
    lat_cells, lon_cells, channels = values.shape[-3:]
    shaped = values.reshape(leading + (lat_cells // factor, factor, lon_cells // factor, factor, channels))
    return lax.optimization_barrier(jnp.sum(shaped, axis=(-4, -2)))

def spread(values, factor):
    return jnp.repeat(jnp.repeat(values, factor, axis=-3), factor, axis=-2)

def pad_sphere(values):
    wrapped = jnp.concatenate([values[:, :, -1:], values, values[:, :, :1]], axis=2)
    return jnp.pad(wrapped, ((0, 0), (1, 1), (0, 0), (0, 0)))

def conv_padded(padded, kernel):
    return lax.conv_general_dilated(padded, kernel, (1, 1), 'VALID', dimension_numbers=('NHWC', 'HWIO', 'NHWC'), preferred_element_type=jnp.float32)

def kernel_terms(padded, upstream):
    channels = upstream.shape[-1]
    lat_cells, lon_cells = (upstream.shape[1], upstream.shape[2])
    flat_up = upstream.reshape(-1, channels)
    tap_terms = []
    for row_tap in range(3):
        for col_tap in range(3):
            window = padded[:, row_tap:row_tap + lat_cells, col_tap:col_tap + lon_cells].reshape(-1, padded.shape[-1])
            tap_terms.append(jnp.dot(window.T, flat_up, preferred_element_type=jnp.float32))
    return jnp.stack(tap_terms)

def reference(field, kernel0, kernel1, mixing, gain, cotangent):
    samples, lat_cells, lon_cells, channels = field.shape
    padded0 = pad_sphere(field)
    preact0 = conv_padded(padded0, kernel0)
    level0 = (field.astype(jnp.float32) + activate(preact0)).astype(jnp.bfloat16)
    coarse1 = (block_sum(level0.astype(jnp.float32), 2) / 4.0).astype(jnp.bfloat16)
    padded1 = pad_sphere(coarse1)
    preact1 = conv_padded(padded1, kernel1)
    level1 = (coarse1.astype(jnp.float32) + activate(preact1)).astype(jnp.bfloat16)
    coarse2 = (block_sum(level1.astype(jnp.float32), 4) / 16.0).astype(jnp.bfloat16)
    lat_two = lat_cells // 8
    lon_two = lon_cells // 8
    lat_index = ((jnp.arange(KL, dtype=jnp.int32) - KL // 2) % lat_two).astype(jnp.int32)
    doubling = jnp.where(jnp.arange(KM) == 0, 1.0, 2.0).astype(jnp.float32)
    gain_re = gain[:, :channels].reshape(KL, KM, channels)
    gain_im = gain[:, channels:].reshape(KL, KM, channels)
    gain_c = lax.complex(gain_re, gain_im)
    spec = jnp.fft.rfft2(coarse2.astype(jnp.float32), axes=(1, 2), norm='ortho')[:, lat_index, :KM]
    coef = spec * gain_c[None]
    embed = jnp.zeros((samples, lat_two, lon_two // 2 + 1, channels), coef.dtype).at[:, lat_index, :KM].set(coef)
    filtered = jnp.fft.irfft2(embed, s=(lat_two, lon_two), axes=(1, 2), norm='ortho').astype(jnp.bfloat16)
    flat_filtered = filtered.reshape(-1, channels)
    mixed_pre = jnp.dot(flat_filtered, mixing, preferred_element_type=jnp.float32).reshape(filtered.shape)
    level2 = (coarse2.astype(jnp.float32) + activate(mixed_pre)).astype(jnp.bfloat16)
    decoder = level1.astype(jnp.float32) + spread(level2.astype(jnp.float32), 4)
    predicted = (level0.astype(jnp.float32) + spread(decoder, 2)).astype(jnp.bfloat16)
    upstream = cotangent.astype(jnp.float32)
    level_cells = samples * lat_cells * lon_cells
    grad_dec = block_sum(upstream, 2)
    grad_level2 = block_sum(grad_dec, 4)
    grad_mixed = activate_grad(mixed_pre, grad_level2).astype(jnp.bfloat16)
    flat_grad = grad_mixed.reshape(-1, channels)
    grad_mixing = jnp.dot(flat_filtered.T, flat_grad, preferred_element_type=jnp.float32) * (1.0 / math.sqrt(level_cells // 64))
    grad_filtered = jnp.dot(flat_grad, mixing.T, preferred_element_type=jnp.float32).reshape(filtered.shape).astype(jnp.bfloat16)
    grad_coef = jnp.fft.rfft2(grad_filtered.astype(jnp.float32), axes=(1, 2), norm='ortho')[:, lat_index, :KM] * doubling[None, None, :, None]
    gain_sum = lax.optimization_barrier(jnp.sum(jnp.conj(spec) * grad_coef, axis=0))
    grad_gain = jnp.concatenate([jnp.real(gain_sum), jnp.imag(gain_sum)], axis=-1).reshape(-1)
    back_coef = jnp.conj(gain_c)[None] * grad_coef
    full = jnp.zeros((samples, lat_two, lon_two, channels), back_coef.dtype).at[:, lat_index, :KM].set(back_coef)
    back_coarse = jnp.real(jnp.fft.ifft2(full, axes=(1, 2), norm='ortho')).astype(jnp.bfloat16)
    grad_level1 = grad_dec + spread(grad_level2 + back_coarse.astype(jnp.float32), 4) / 16.0
    grad_pre1 = activate_grad(preact1, grad_level1).astype(jnp.bfloat16)
    grad_kernel1 = kernel_terms(padded1, grad_pre1) * (1.0 / math.sqrt(level_cells // 4))
    flipped = jnp.transpose(kernel1[::-1, ::-1], (0, 1, 3, 2))
    grad_coarse1 = grad_level1 + conv_padded(pad_sphere(grad_pre1), flipped)
    grad_level0 = upstream + spread(grad_coarse1, 2) / 4.0
    grad_pre0 = activate_grad(preact0, grad_level0).astype(jnp.bfloat16)
    grad_kernel0 = kernel_terms(padded0, grad_pre0) * (1.0 / math.sqrt(level_cells))
    return (predicted, grad_kernel0.reshape(-1), grad_kernel1.reshape(-1), grad_mixing.reshape(-1), grad_gain)
```

```python
import functools
import math

import jax
import jax.numpy as jnp
import ml_dtypes
import numpy as np
from jax import lax
from jax.experimental import pallas as pl
from jax.experimental.pallas import tpu as pltpu
from jax.sharding import PartitionSpec as P

MESH = pl.DeviceIdType.MESH
F32 = jnp.float32
BF16 = jnp.bfloat16
C = 256
NLAT, NLON = 8, 16
ROWS, COLS = 16, 48
VMEM_BYTES = 56 * 2**20


def spectral_tables():
    lat_n, lon_n, kl, km = 16, 96, 16, 32
    freq = np.repeat(np.arange(kl) - kl // 2, km)
    mode = np.tile(np.arange(km), kl)
    norm = 1.0 / math.sqrt(lat_n * lon_n)

    def phase(i, j):
        whole = (freq[:, None] * i[None] * lon_n + mode[:, None] * j[None] * lat_n) % (lat_n * lon_n)
        return 2.0 * np.pi * whole / (lat_n * lon_n)

    forward = np.zeros((2, kl * km, NLON, NLAT, 2, 8))
    for lon in range(NLON):
        for lat in range(NLAT):
            for r in range(2):
                j = lon * 6 + np.arange(6)
                ph = phase(np.full(6, lat * 2 + r), j)
                forward[0, :, lon, lat, r, 1:7] = np.cos(ph) * norm
                forward[1, :, lon, lat, r, 1:7] = -np.sin(ph) * norm
    forward = forward.reshape(2 * kl * km, NLON * NLAT * 16)
    weight = np.where(mode == 0, 1.0, 2.0) * norm
    back = np.zeros((NLAT * NLON, 32, 2, kl * km))
    for lat in range(NLAT):
        for lon in range(NLON):
            i = np.repeat(lat * 2 - 1 + np.arange(4), 8)
            j = np.tile(lon * 6 - 1 + np.arange(8), 4)
            ph = phase(i, j).T
            back[lat * NLON + lon, :, 0] = np.cos(ph) * weight
            back[lat * NLON + lon, :, 1] = -np.sin(ph) * weight
    back = back.reshape(NLAT * NLON, 32, 2 * kl * km)
    return forward.astype(ml_dtypes.bfloat16), back.astype(ml_dtypes.bfloat16)


def cell_tables():
    pool2 = np.zeros((32, 2, 64))
    for j in range(32):
        pool2[j, :, 2 * j : 2 * j + 2] = 0.25
    pool4 = np.zeros((8, 4, 32))
    for j in range(1, 7):
        pool4[j, :, 4 * j : 4 * j + 4] = 1 / 16
    dec = np.zeros((4, 32, 8, 48))
    for r in range(4):
        for j in range(24):
            dec[r, 4 + j, :, 8 * (j // 4) : 8 * (j // 4) + 8] += 1 / 16
            dec[r, 4 + j, 2 * r : 2 * r + 2, 2 * j : 2 * j + 2] += 1
    sum8 = np.zeros((8, 8, 48))
    for j in range(6):
        sum8[1 + j, :, 8 * j : 8 * j + 8] = 1
    pick = np.zeros((64, 8, 32))
    for half, row, col in ((0, 0, 4), (32, 7, 27)):
        for i in range(24):
            pick[half + i, row, 4 + i] = 1
        for r in range(8):
            pick[half + 24 + r, r, col] = 1
    place = np.zeros((10, 32, 10, 16))
    for j in range(24):
        place[0, 4 + j, j // 16, j % 16] = 1
        place[9, 4 + j, 2 + j // 16, j % 16] = 1
    for r in range(8):
        place[1 + r, 3, 4, 8 + r] = 1
        place[1 + r, 28, 5, 8 + r] = 1
    place[0, 3, 6, 7] = 1
    place[0, 28, 7, 0] = 1
    place[9, 3, 8, 7] = 1
    place[9, 28, 9, 0] = 1
    up4 = np.zeros((10, 32, 4, 8))
    for r in range(10):
        for j in range(32):
            up4[r, j, (r + 3) // 4, j // 4] = 1 / 16
    up2 = np.zeros((2, 48, 32))
    up8 = np.zeros((2, 48, 8))
    for j in range(48):
        up2[:, j, 4 + j // 2] = 1
        up8[:, j, 1 + j // 8] = 1
    shapes = dict(
        pool2=(pool2, (32, 128)), pool4=(pool4, (8, 128)), dec=(dec, (128, 384)), sum8=(sum8, (8, 384)),
        pick=(pick, (64, 256)), place=(place, (320, 160)), up4=(up4, (320, 32)), up2=(up2, (96, 32)),
        up8=(up8, (96, 8)),
    )
    return {k: v.reshape(s).astype(ml_dtypes.bfloat16) for k, (v, s) in shapes.items()}


def dot(a, b):
    return jnp.dot(a, b, preferred_element_type=F32)


def dot_rows(a, b):
    return lax.dot_general(a, b, (((0,), (0,)), ((), ())), preferred_element_type=F32)


def dot_cols(a, b):
    return lax.dot_general(a, b, (((1,), (1,)), ((), ())), preferred_element_type=F32)


def gelu_both(v):
    k, q = 0.7978845608028654, 0.044715
    sq = v * v
    t = jnp.tanh(k * (v * (1.0 + q * sq)))
    half = 0.5 * (1.0 + t)
    return v * half, half + (0.5 * v) * (1.0 - t * t) * (k * (1.0 + (3.0 * q) * sq))


def place():
    return lax.axis_index("lat"), lax.axis_index("lon"), lax.axis_index("batch")


def step(pos, by, n):
    return lax.rem(pos + (by + n), n)


def signal(lat, lon, batch):
    pl.semaphore_signal(
        pltpu.get_barrier_semaphore(), inc=1, device_id={"lat": lat, "lon": lon, "batch": batch}, device_id_type=MESH
    )


def remote(src, dst, send, recv, lat, lon, batch):
    return pltpu.make_async_remote_copy(
        src_ref=src, dst_ref=dst, send_sem=send, recv_sem=recv,
        device_id={"lat": lat, "lon": lon, "batch": batch}, device_id_type=MESH,
    )


NEIGHBOURS = ((1, 0), (-1, 0), (0, 1), (0, -1), (1, 1), (1, -1), (-1, 1), (-1, -1))


def halo_copies(field, ext, send, recv):
    lat, lon, batch = place()
    rows = {1: (pl.ds(13, 3), pl.ds(0, 3)), -1: (pl.ds(0, 3), pl.ds(19, 3)), 0: (pl.ds(0, 16), pl.ds(3, 16))}
    cols = {1: (pl.ds(32, 16), pl.ds(0, 16)), -1: (pl.ds(0, 16), pl.ds(64, 16)), 0: (pl.ds(0, 48), pl.ds(16, 48))}
    copies = []
    for i, (dlat, dlon) in enumerate(NEIGHBOURS):
        (src_r, dst_r), (src_c, dst_c) = rows[dlat], cols[dlon]
        copies.append(remote(
            field.at[src_r, src_c], ext.at[dst_r, dst_c], send.at[i], recv.at[i],
            step(lat, dlat, NLAT), step(lon, dlon, NLON), batch,
        ))
    return copies


def forward_kernel(
    field, cot, k0, k1, pool2, pool4, dec, sum8, pick,
    x3c, da0, level0, x13, p1, level1, slot, a1, gl2, edges,
    ext, fs, x3, l0f, c1s, send, recv, own_sem,
):
    lat, lon, batch = place()
    for dlat, dlon in NEIGHBOURS:
        signal(step(lat, dlat, NLAT), step(lon, dlon, NLON), batch)
    own = pltpu.make_async_copy(field, ext.at[pl.ds(3, 16), pl.ds(16, 48)], own_sem)
    own.start()
    pl.semaphore_wait(pltpu.get_barrier_semaphore(), 8)
    copies = halo_copies(field, ext, send, recv)
    for copy in copies:
        copy.start()
    for half in range(2):
        part = cot[8 * half : 8 * half + 8].reshape(384, C)
        a1[4 * half : 4 * half + 4] = dot(dec[...], part).reshape(4, 32, C)
        gl2[8 * half : 8 * half + 8] = dot(sum8[...], part)
    own.wait()
    for copy in copies:
        copy.wait()

    edge_top = lat == 0
    edge_bot = lat == NLAT - 1
    fs[3:19] = ext[3:19].astype(F32)
    fs[0:3] = jnp.where(edge_top, 0.0, ext[0:3].astype(F32))
    fs[19:22] = jnp.where(edge_bot, 0.0, ext[19:22].astype(F32))
    for b in range(3):
        x3[:, :, b * C : (b + 1) * C] = fs[:, 7 + b : 71 + b, :].astype(BF16)
        x3c[:, :, b * C : (b + 1) * C] = fs[2:20, 15 + b : 63 + b, :].astype(BF16)

    def rows4(i, _):
        y = 4 * i
        acc = dot(x3[pl.ds(y, 4)].reshape(256, 3 * C), k0[0])
        acc += dot(x3[pl.ds(y + 1, 4)].reshape(256, 3 * C), k0[1])
        acc += dot(x3[pl.ds(y + 2, 4)].reshape(256, 3 * C), k0[2])
        act, slope = gelu_both(acc)
        out = fs[pl.ds(y + 1, 4), 8:72, :] + act.reshape(4, 64, C)
        l0f[pl.ds(y, 4)] = out.astype(BF16)
        level0[pl.ds(y, 4)] = out[:, 8:56].astype(BF16)
        da0[pl.ds(y, 4)] = slope.reshape(4, 64, C)[:, 8:56].astype(BF16)
        return 0

    lax.fori_loop(0, 5, rows4, 0)

    c1s[...] = jnp.zeros_like(c1s)
    for y in range(10):
        row = dot(pool2[...], l0f[2 * y : 2 * y + 2].reshape(128, C)).astype(BF16).astype(F32)
        if y == 0:
            row = jnp.where(edge_top, 0.0, row)
        if y == 9:
            row = jnp.where(edge_bot, 0.0, row)
        c1s[y, 8:40, :] = row
    for b in range(3):
        x13[:, :, b * C : (b + 1) * C] = c1s[:, 7 + b : 39 + b, :].astype(BF16)
    pre = dot(x13[0:8].reshape(256, 3 * C), k1[0])
    pre += dot(x13[1:9].reshape(256, 3 * C), k1[1])
    pre += dot(x13[2:10].reshape(256, 3 * C), k1[2])
    act, _ = gelu_both(pre)
    col = lax.broadcasted_iota(jnp.int32, (8, 32, C), 1)
    mine = (col >= 4) & (col < 28)
    pre = jnp.where(mine, pre.reshape(8, 32, C), 0.0)
    p1[...] = pre
    lev1 = jnp.where(mine, c1s[1:9, 8:40, :] + act.reshape(8, 32, C), 0.0).astype(BF16)
    level1[...] = lev1
    for half in range(2):
        slot[8 * half : 8 * half + 8] = dot(pool4[...], lev1[4 * half : 4 * half + 4].reshape(128, C)).astype(BF16)
    edges[:, 0] = dot(pick[...], a1[...].reshape(256, C).astype(BF16)).astype(BF16).reshape(4, 16, C)
    edges[:, 1] = dot(pick[...], pre.reshape(256, C).astype(BF16)).astype(BF16).reshape(4, 16, C)


def greet_band():
    lat, lon, batch = place()
    for k in range(1, NLAT):
        signal(step(lat, k, NLAT), lon, batch)
    for k in range(1, NLON):
        signal(lat, step(lon, k, NLON), batch)


def gather_cells(slot, cells, own_sem, send1, recv1, send2, recv2):
    lat, lon, batch = place()
    own = pltpu.make_async_copy(slot, cells.at[lon, lat], own_sem)
    own.start()
    first = [
        remote(slot, cells.at[lon, lat], send1.at[k - 1], recv1.at[k - 1], step(lat, k, NLAT), lon, batch)
        for k in range(1, NLAT)
    ]
    for copy in first:
        copy.start()
    own.wait()
    for copy in first:
        copy.wait()
    second = [
        remote(cells.at[lon], cells.at[lon], send2.at[k - 1], recv2.at[k - 1], lat, step(lon, k, NLON), batch)
        for k in range(1, NLON)
    ]
    for copy in second:
        copy.start()
    return second


EDGE_SENDS = (
    ((1, 0), 2, 2, 0), ((-1, 0), 0, 2, 2), ((0, 1), 3, 1, 4), ((0, -1), 1, 1, 5),
    ((1, 1), 3, 1, 6), ((1, -1), 2, 1, 7), ((-1, 1), 1, 1, 8), ((-1, -1), 0, 1, 9),
)


def spectral_kernel(
    slot, edges, table, synth, gain, mixing, gl2,
    ring, slot2, spec_own, level2, mix_grad,
    cells, coef, synth_own, own_sem, send1, recv1, send2, recv2, send3, recv3, synth_sem,
):
    lat, lon, batch = place()
    fetch = pltpu.make_async_copy(synth.at[lat * NLON + lon], synth_own, synth_sem)
    fetch.start()
    greet_band()
    for dlat, dlon in NEIGHBOURS[4:]:
        signal(step(lat, dlat, NLAT), step(lon, dlon, NLON), batch)
    pl.semaphore_wait(pltpu.get_barrier_semaphore(), NLAT + NLON - 2 + 4)
    second = gather_cells(slot, cells, own_sem, send1, recv1, send2, recv2)
    edge = []
    for i, ((dlat, dlon), seg, n, at) in enumerate(EDGE_SENDS):
        edge.append(remote(
            edges.at[pl.ds(seg, n)], ring.at[pl.ds(at, n)], send3.at[i], recv3.at[i],
            step(lat, dlat, NLAT), step(lon, dlon, NLON), batch,
        ))
    for copy in edge:
        copy.start()
    for copy in second:
        copy.wait()
    spec = dot(table[...], cells[...].reshape(NLON * NLAT * 16, C))
    sr, si = spec[:512], spec[512:]
    gr, gi = gain[:, :C], gain[:, C:]
    coef[0:512] = (gr * sr - gi * si).astype(BF16)
    coef[512:1024] = (gr * si + gi * sr).astype(BF16)
    fetch.wait()
    filt = dot(synth_own[8:24], coef[...]).astype(BF16)
    mixed = dot(filt, mixing[...])
    act, slope = gelu_both(mixed)
    level2[...] = (slot[...].astype(F32) + act).astype(BF16)
    col = lax.rem(lax.broadcasted_iota(jnp.int32, (16, C), 0), 8)
    gm = jnp.where((col >= 1) & (col < 7), gl2[...] * slope, 0.0).astype(BF16)
    mix_grad[...] = dot_rows(filt, gm).astype(BF16)
    slot2[...] = dot_cols(gm, mixing[...]).astype(BF16)
    rows = lax.broadcasted_iota(jnp.int32, (8, 512), 0)
    row_at = lax.broadcasted_iota(jnp.int32, (8, 512), 1)
    sel = jnp.where(row_at == rows + 8 * ((lat * NLON + lon) // 2), 1.0, 0.0)
    spec_own[:, :C] = jnp.dot(sel, sr, preferred_element_type=F32, precision=lax.Precision.HIGHEST)
    spec_own[:, C:] = jnp.dot(sel, si, preferred_element_type=F32, precision=lax.Precision.HIGHEST)
    for copy in edge:
        copy.wait()


def store_rows(parts, block, first, offset):
    n = block.shape[0]
    at = 0
    while at < n:
        chunk, inside = divmod(first + at, 144)
        size = min(n - at, 144 - inside)
        parts[chunk, offset + inside : offset + inside + size, :] = block[at : at + size].astype(BF16)
        at += size


def backward_kernel(
    slot2, ring, table, synth, gain, spec_own, mix_grad, a1, p1, x13, k1, x3c, cot, da0, level0, level1, level2,
    place_m, up4, up2, up8,
    predicted, parts, gain_grad,
    cells, coef, synth_own, sc, g1s, xg, gp0, own_sem, send1, recv1, send2, recv2, synth_sem,
):
    lat, lon, batch = place()
    fetch = pltpu.make_async_copy(synth.at[lat * NLON + lon], synth_own, synth_sem)
    fetch.start()
    greet_band()
    pl.semaphore_wait(pltpu.get_barrier_semaphore(), NLAT + NLON - 2)
    second = gather_cells(slot2, cells, own_sem, send1, recv1, send2, recv2)
    for r in range(8):
        low = dot(up2[...], level1[r]) + dot(up8[...], level2[8 * (r // 4) : 8 * (r // 4) + 8])
        high = level0[2 * r + 2 : 2 * r + 4].astype(F32) + low.reshape(2, 48, C)
        predicted[2 * r : 2 * r + 2] = high.astype(BF16)
    for s in range(16):
        parts[s, 288:304, :] = mix_grad[16 * s : 16 * s + 16]
    a1f = dot(place_m[...], ring[:, 0].reshape(160, C)).reshape(10, 32, C)
    p1f = dot(place_m[...], ring[:, 1].reshape(160, C)).reshape(10, 32, C)
    g1s[...] = jnp.zeros_like(g1s)
    g1s[:, 8:40, :] = a1f
    g1s[1:9, 8:40, :] += a1[...]
    xg[...] = p1f
    xg[1:9] += p1[...]
    _, slope1 = gelu_both(xg[...])
    xg[...] = slope1
    for copy in second:
        copy.wait()

    sc[...] = dot(table[...], cells[...].reshape(NLON * NLAT * 16, C))
    gr, gi = gain[:, :C], gain[:, C:]
    er, ei = sc[0:512], sc[512:1024]
    coef[0:512] = (gr * er + gi * ei).astype(BF16)
    coef[512:1024] = (gr * ei - gi * er).astype(BF16)
    fetch.wait()
    back = dot(synth_own[...], coef[...]).astype(BF16)
    gl1 = g1s[:, 8:40, :] + dot(up4[...], back).reshape(10, 32, C)
    col = lax.broadcasted_iota(jnp.int32, (10, 32, C), 1)
    row = lax.broadcasted_iota(jnp.int32, (10, 32, C), 0)
    first = jnp.where(lat == 0, 1, 0)
    last = jnp.where(lat == NLAT - 1, 9, 10)
    valid = (col >= 3) & (col < 29) & (row >= first) & (row < last)
    gp1 = jnp.where(valid, gl1 * xg[...], 0.0).astype(BF16)
    g1s[:, 8:40, :] = gp1.astype(F32)
    mine = (col[1:9] >= 4) & (col[1:9] < 28)
    gown = jnp.where(mine, gp1[1:9].astype(F32), 0.0).astype(BF16).reshape(256, C)
    gc1 = gl1[1:9].reshape(256, C)
    for b in range(3):
        shifted = g1s[:, 7 + b : 39 + b, :].astype(BF16)
        for a in range(3):
            gc1 += dot_cols(
                shifted[a : a + 8].reshape(256, C), k1[2 - a, (2 - b) * C : (3 - b) * C, :]
            )
    high = gc1.astype(BF16)
    low = (gc1 - high.astype(F32)).astype(BF16)
    for r in range(8):
        up = dot(up2[...], high[32 * r : 32 * r + 32]) + dot(up2[...], low[32 * r : 32 * r + 32])
        gl0 = cot[2 * r : 2 * r + 2].astype(F32) + 0.25 * up.reshape(2, 48, C)
        gp0[2 * r : 2 * r + 2] = (gl0 * da0[2 * r + 2 : 2 * r + 4].astype(F32)).astype(BF16)
    for a in range(3):
        store_rows(parts, dot_rows(x13[a : a + 8].reshape(256, 3 * C), gown), 768 * a, 144)
    for a in range(3):
        store_rows(parts, dot_rows(x3c[a : a + 16].reshape(768, 3 * C), gp0[...].reshape(768, C)), 768 * a, 0)

    base = 8 * ((lat * NLON + lon) // 2)
    rows = lax.broadcasted_iota(jnp.int32, (8, 512), 0)
    sel = jnp.where(lax.broadcasted_iota(jnp.int32, (8, 512), 1) == rows + base, 1.0, 0.0)
    br = jnp.dot(sel, sc[0:512], preferred_element_type=F32, precision=lax.Precision.HIGHEST)
    bi = jnp.dot(sel, sc[512:1024], preferred_element_type=F32, precision=lax.Precision.HIGHEST)
    m = lax.rem(base + lax.broadcasted_iota(jnp.int32, (8, C), 0), 32)
    weight = jnp.where(m == 0, 1.0, 2.0)
    ar, ai = spec_own[:, :C], spec_own[:, C:]
    gain_grad[:, :C] = weight * (ar * br + ai * bi)
    gain_grad[:, C:] = weight * (ar * bi - ai * br)


def reduce_kernel(
    scales, parts, gain_in, total, gain_out,
    got1, acc1, got2, acc2, got3, acc3, blocks, got4, gain_got,
    send1, recv1, send2, recv2, send3, recv3, send4, recv4, sendg, recvg,
):
    lat, lon, batch = place()
    core = lax.rem(lon, 2)
    yh = lax.rem(lon // 2, 2)
    x = lon // 4
    other = lon + 1 - 2 * core
    chunk = core * 8 + x * 2 + batch
    me = (lat * NLON + lon) * 2 + batch
    holder = lat * 2 + yh
    want = lat * 2 + lon // 8
    is_own = chunk == want
    signal(lat, other, batch)
    for k in range(1, 4):
        signal(lat, step(lon, 4 * k, NLON), batch)
    signal(lat, lon, 1 - batch)
    w_core, w_x, w_batch = want // 8, lax.rem(want // 2, 4), lax.rem(want, 2)
    for h in range(16):
        src_lon = w_x * 4 + (h % 2) * 2 + w_core

        @pl.when(jnp.logical_not(is_own & (holder == h)))
        def _():
            signal(h // 2, src_lon, w_batch)

    pl.semaphore_wait(pltpu.get_barrier_semaphore(), 21 - jnp.where(is_own, 1, 0))
    swap = remote(gain_in, gain_got, sendg, recvg, lat, lon, 1 - batch)
    swap.start()
    one = remote(parts.at[pl.ds(8 - 8 * core, 8)], got1, send1, recv1, lat, other, batch)
    one.start()
    one.wait()

    def add1(i, _):
        acc1[i] = (parts[8 * core + i].astype(F32) + got1[i].astype(F32)).astype(BF16)
        return 0

    lax.fori_loop(0, 8, add1, 0)
    two = []
    for k in range(1, 4):
        there = lax.rem(x + k, 4)
        two.append(remote(
            acc1.at[pl.ds(2 * there, 2)], got2.at[k - 1], send2.at[k - 1], recv2.at[k - 1],
            lat, step(lon, 4 * k, NLON), batch,
        ))
    for copy in two:
        copy.start()
    for copy in two:
        copy.wait()
    for i in range(2):
        acc2[i] = (
            acc1[2 * x + i].astype(F32) + got2[0, i].astype(F32) + got2[1, i].astype(F32) + got2[2, i].astype(F32)
        ).astype(BF16)
    three = remote(acc2.at[1 - batch], got3, send3, recv3, lat, lon, 1 - batch)
    three.start()
    three.wait()
    acc3[...] = acc2[batch].astype(F32) + got3[...].astype(F32)
    for e in range(16):
        block = jnp.concatenate(
            [acc3[9 * e : 9 * e + 9], acc3[144 + 9 * e : 153 + 9 * e], acc3[288 + e : 289 + e],
             jnp.zeros((13, C), F32)], axis=0
        )
        blocks[e] = block.astype(BF16)
    dest = 16 * chunk
    for e in range(16):
        to = dest + e
        copy = remote(
            blocks.at[e], got4.at[holder], send4.at[e], recv4.at[holder],
            to // 32, lax.rem(to // 2, NLON), e % 2,
        )

        @pl.when(to != me)
        def _():
            copy.start()

        @pl.when(to == me)
        def _():
            got4[holder] = blocks[e]

    for h in range(16):
        copy = remote(blocks.at[0], got4.at[h], send4.at[0], recv4.at[h], lat, other, batch)

        @pl.when(jnp.logical_not(is_own & (holder == h)))
        def _():
            copy.wait_recv()

    for e in range(16):
        copy = remote(blocks.at[e], got4.at[0], send4.at[e], recv4.at[0], lat, other, batch)

        @pl.when(dest + e != me)
        def _():
            copy.wait_send()

    acc = got4[0].astype(F32)
    for h in range(1, 16):
        acc += got4[h].astype(F32)
    s0, s1, s2 = scales
    row = lax.broadcasted_iota(jnp.int32, (32, C), 0)
    total[...] = acc * jnp.where(row < 9, s0, jnp.where(row < 18, s1, s2))
    swap.wait()
    gain_out[...] = gain_in[...] + gain_got[...]


def call(body, outs, scratch, collective, n_in, hbm=()):
    vmem = pl.BlockSpec(memory_space=pltpu.VMEM)
    anywhere = pl.BlockSpec(memory_space=pl.ANY)
    return pl.pallas_call(
        body,
        out_shape=[jax.ShapeDtypeStruct(s, d) for s, d in outs],
        in_specs=[anywhere if i in hbm else vmem for i in range(n_in)],
        out_specs=[vmem] * len(outs),
        scratch_shapes=scratch,
        compiler_params=pltpu.CompilerParams(
            collective_id=collective, has_side_effects=True, vmem_limit_bytes=VMEM_BYTES
        ),
    )


def dma(*n):
    return pltpu.SemaphoreType.DMA(n)


def on_device(tables, field, kernel0, kernel1, mixing, gain, cotangent):
    table, synth, small = tables
    small = {k: jnp.asarray(v) for k, v in small.items()}
    table, synth = jnp.asarray(table), jnp.asarray(synth)
    k0 = kernel0.reshape(3, 3 * C, C)
    k1 = kernel1.reshape(3, 3 * C, C)
    field, cot = field[0], cotangent[0]
    x3c, da0, level0, x13, p1, level1, slot, a1, gl2, edges = call(
        forward_kernel,
        [((18, 48, 3 * C), BF16), ((20, 48, C), BF16), ((20, 48, C), BF16), ((10, 32, 3 * C), BF16),
         ((8, 32, C), F32), ((8, 32, C), BF16), ((16, C), BF16), ((8, 32, C), F32), ((16, C), F32),
         ((4, 2, 16, C), BF16)],
        [pltpu.VMEM((22, 80, C), BF16), pltpu.VMEM((22, 80, C), F32), pltpu.VMEM((22, 64, 3 * C), BF16),
         pltpu.VMEM((20, 64, C), BF16), pltpu.VMEM((10, 48, C), F32), dma(8), dma(8), dma()],
        0, 9,
    )(field, cot, k0, k1, small["pool2"], small["pool4"], small["dec"], small["sum8"], small["pick"])
    ring, slot2, spec_own, level2, mix_grad = call(
        spectral_kernel,
        [((10, 2, 16, C), BF16), ((16, C), BF16), ((8, 2 * C), F32), ((16, C), BF16), ((C, C), BF16)],
        [pltpu.VMEM((NLON, NLAT, 16, C), BF16), pltpu.VMEM((1024, C), BF16), pltpu.VMEM((32, 1024), BF16),
         dma(), dma(7), dma(7), dma(15), dma(15), dma(8), dma(8), dma()],
        1, 7, hbm=(3,),
    )(slot, edges, table, synth, gain, mixing, gl2)
    predicted, parts, gain_grad = call(
        backward_kernel,
        [((ROWS, COLS, C), BF16), ((16, 304, C), BF16), ((8, 2 * C), F32)],
        [pltpu.VMEM((NLON, NLAT, 16, C), BF16), pltpu.VMEM((1024, C), BF16), pltpu.VMEM((32, 1024), BF16),
         pltpu.VMEM((1024, C), F32), pltpu.VMEM((10, 48, C), F32), pltpu.VMEM((10, 32, C), F32),
         pltpu.VMEM((16, 48, C), BF16), dma(), dma(7), dma(7), dma(15), dma(15), dma()],
        2, 21, hbm=(3,),
    )(slot2, ring, table, synth, gain, spec_own, mix_grad, a1, p1, x13, k1, x3c, cot, da0, level0, level1, level2,
      small["place"], small["up4"], small["up2"], small["up8"])
    cells0 = 2 * 128 * 768
    scales = (1.0 / math.sqrt(cells0), 1.0 / math.sqrt(cells0 // 4), 1.0 / math.sqrt(cells0 // 64))
    total, gain_sum = call(
        functools.partial(reduce_kernel, scales),
        [((32, C), F32), ((8, 2 * C), F32)],
        [pltpu.VMEM((8, 304, C), BF16), pltpu.VMEM((8, 304, C), BF16), pltpu.VMEM((3, 2, 304, C), BF16),
         pltpu.VMEM((2, 304, C), BF16), pltpu.VMEM((304, C), BF16), pltpu.VMEM((304, C), F32),
         pltpu.VMEM((16, 32, C), BF16), pltpu.VMEM((16, 32, C), BF16), pltpu.VMEM((8, 2 * C), F32),
         dma(), dma(), dma(3), dma(3), dma(), dma(), dma(16), dma(16), dma(), dma()],
        3, 2,
    )(parts, gain_grad)
    lat, lon, batch = place()
    at = 4 * lax.rem(lon, 2) + 2 * batch
    gain_rows = lax.dynamic_slice_in_dim(gain_sum, at, 2, 0)
    return (
        predicted[None], total[:9].reshape(-1), total[9:18].reshape(-1), total[18].reshape(-1),
        gain_rows.reshape(-1),
    )


def solution(mesh):
    tables = (*spectral_tables(), cell_tables())
    tile = P("batch", "lat", "lon", None)
    split = P(("lat", "lon", "batch"))
    return jax.shard_map(
        functools.partial(on_device, tables), mesh=mesh, in_specs=(tile, P(), P(), P(), P(), tile),
        out_specs=(tile, split, split, split, split), check_vma=False,
    )
```

```python
import functools
import math

import jax
import jax.numpy as jnp
import ml_dtypes
import numpy as np
from jax import lax
from jax.experimental import pallas as pl
from jax.experimental.pallas import tpu as pltpu
from jax.sharding import PartitionSpec as P

MESH = pl.DeviceIdType.MESH
F32 = jnp.float32
BF16 = jnp.bfloat16
C = 256
NLAT, NLON = 8, 16
ROWS, COLS = 16, 48
VMEM_BYTES = 56 * 2**20


def spectral_tables():
    lat_n, lon_n, kl, km = 16, 96, 16, 32
    freq = np.repeat(np.arange(kl) - kl // 2, km)
    mode = np.tile(np.arange(km), kl)
    norm = 1.0 / math.sqrt(lat_n * lon_n)

    def phase(i, j):
        whole = (freq[:, None] * i[None] * lon_n + mode[:, None] * j[None] * lat_n) % (lat_n * lon_n)
        return 2.0 * np.pi * whole / (lat_n * lon_n)

    forward = np.zeros((2, kl * km, NLON, NLAT, 2, 8))
    for lon in range(NLON):
        for lat in range(NLAT):
            for r in range(2):
                j = lon * 6 + np.arange(6)
                ph = phase(np.full(6, lat * 2 + r), j)
                forward[0, :, lon, lat, r, 1:7] = np.cos(ph) * norm
                forward[1, :, lon, lat, r, 1:7] = -np.sin(ph) * norm
    forward = forward.reshape(2 * kl * km, NLON * NLAT * 16)
    weight = np.where(mode == 0, 1.0, 2.0) * norm
    back = np.zeros((NLAT * NLON, 32, 2, kl * km))
    for lat in range(NLAT):
        for lon in range(NLON):
            i = np.repeat(lat * 2 - 1 + np.arange(4), 8)
            j = np.tile(lon * 6 - 1 + np.arange(8), 4)
            ph = phase(i, j).T
            back[lat * NLON + lon, :, 0] = np.cos(ph) * weight
            back[lat * NLON + lon, :, 1] = -np.sin(ph) * weight
    back = back.reshape(NLAT * NLON, 32, 2 * kl * km)
    forward = forward.reshape(2 * kl * km, 8, 256).transpose(1, 0, 2)
    return forward.astype(ml_dtypes.bfloat16), back.astype(ml_dtypes.bfloat16)


def cell_tables():
    pool2 = np.zeros((32, 2, 64))
    for j in range(32):
        pool2[j, :, 2 * j : 2 * j + 2] = 0.25
    pool4 = np.zeros((8, 4, 32))
    for j in range(1, 7):
        pool4[j, :, 4 * j : 4 * j + 4] = 1 / 16
    dec = np.zeros((4, 32, 8, 48))
    for r in range(4):
        for j in range(24):
            dec[r, 4 + j, :, 8 * (j // 4) : 8 * (j // 4) + 8] += 1 / 16
            dec[r, 4 + j, 2 * r : 2 * r + 2, 2 * j : 2 * j + 2] += 1
    sum8 = np.zeros((8, 8, 48))
    for j in range(6):
        sum8[1 + j, :, 8 * j : 8 * j + 8] = 1
    pick = np.zeros((64, 8, 32))
    for half, row, col in ((0, 0, 4), (32, 7, 27)):
        for i in range(24):
            pick[half + i, row, 4 + i] = 1
        for r in range(8):
            pick[half + 24 + r, r, col] = 1
    place = np.zeros((10, 32, 10, 16))
    for j in range(24):
        place[0, 4 + j, j // 16, j % 16] = 1
        place[9, 4 + j, 2 + j // 16, j % 16] = 1
    for r in range(8):
        place[1 + r, 3, 4, 8 + r] = 1
        place[1 + r, 28, 5, 8 + r] = 1
    place[0, 3, 6, 7] = 1
    place[0, 28, 7, 0] = 1
    place[9, 3, 8, 7] = 1
    place[9, 28, 9, 0] = 1
    up4 = np.zeros((10, 32, 4, 8))
    for r in range(10):
        for j in range(32):
            up4[r, j, (r + 3) // 4, j // 4] = 1 / 16
    up2 = np.zeros((2, 48, 32))
    up8 = np.zeros((2, 48, 8))
    for j in range(48):
        up2[:, j, 4 + j // 2] = 1
        up8[:, j, 1 + j // 8] = 1
    shapes = dict(
        pool2=(pool2, (32, 128)), pool4=(pool4, (8, 128)), dec=(dec, (128, 384)), sum8=(sum8, (8, 384)),
        pick=(pick, (64, 256)), place=(place, (320, 160)), up4=(up4, (320, 32)), up2=(up2, (96, 32)),
        up8=(up8, (96, 8)),
    )
    return {k: v.reshape(s).astype(ml_dtypes.bfloat16) for k, (v, s) in shapes.items()}


def dot(a, b):
    return jnp.dot(a, b, preferred_element_type=F32)


def dot_rows(a, b):
    return lax.dot_general(a, b, (((0,), (0,)), ((), ())), preferred_element_type=F32)


def dot_cols(a, b):
    return lax.dot_general(a, b, (((1,), (1,)), ((), ())), preferred_element_type=F32)


def gelu_both(v):
    k, q = 0.7978845608028654, 0.044715
    sq = v * v
    t = jnp.tanh(k * (v * (1.0 + q * sq)))
    half = 0.5 * (1.0 + t)
    return v * half, half + (0.5 * v) * (1.0 - t * t) * (k * (1.0 + (3.0 * q) * sq))


def place():
    return lax.axis_index("lat"), lax.axis_index("lon"), lax.axis_index("batch")


def step(pos, by, n):
    return lax.rem(pos + (by + n), n)


def signal(lat, lon, batch):
    pl.semaphore_signal(
        pltpu.get_barrier_semaphore(), inc=1, device_id={"lat": lat, "lon": lon, "batch": batch}, device_id_type=MESH
    )


def remote(src, dst, send, recv, lat, lon, batch):
    return pltpu.make_async_remote_copy(
        src_ref=src, dst_ref=dst, send_sem=send, recv_sem=recv,
        device_id={"lat": lat, "lon": lon, "batch": batch}, device_id_type=MESH,
    )


NEIGHBOURS = ((1, 0), (-1, 0), (0, 1), (0, -1), (1, 1), (1, -1), (-1, 1), (-1, -1))


def halo_copies(field, ext, send, recv):
    lat, lon, batch = place()
    rows = {1: (pl.ds(13, 3), pl.ds(0, 3)), -1: (pl.ds(0, 3), pl.ds(19, 3)), 0: (pl.ds(0, 16), pl.ds(3, 16))}
    cols = {1: (pl.ds(32, 16), pl.ds(0, 16)), -1: (pl.ds(0, 16), pl.ds(64, 16)), 0: (pl.ds(0, 48), pl.ds(16, 48))}
    copies = []
    for i, (dlat, dlon) in enumerate(NEIGHBOURS):
        (src_r, dst_r), (src_c, dst_c) = rows[dlat], cols[dlon]
        copies.append(remote(
            field.at[src_r, src_c], ext.at[dst_r, dst_c], send.at[i], recv.at[i],
            step(lat, dlat, NLAT), step(lon, dlon, NLON), batch,
        ))
    return copies


EDGE_SENDS = (
    ((1, 0), 2, 2, 0), ((-1, 0), 0, 2, 2), ((0, 1), 3, 1, 4), ((0, -1), 1, 1, 5),
    ((1, 1), 3, 1, 6), ((1, -1), 2, 1, 7), ((-1, 1), 1, 1, 8), ((-1, -1), 0, 1, 9),
)


def edge_copies(edges, ring, send, recv):
    lat, lon, batch = place()
    return [
        remote(
            edges.at[pl.ds(seg, n)], ring.at[pl.ds(at, n)], send.at[i], recv.at[i],
            step(lat, dlat, NLAT), step(lon, dlon, NLON), batch,
        )
        for i, ((dlat, dlon), seg, n, at) in enumerate(EDGE_SENDS)
    ]


def greet_all():
    lat, lon, batch = place()
    for k in range(1, NLAT):
        signal(step(lat, k, NLAT), lon, batch)
    for k in (1, -1):
        signal(lat, step(lon, k, NLON), batch)
    for dlat, dlon in NEIGHBOURS[4:]:
        signal(step(lat, dlat, NLAT), step(lon, dlon, NLON), batch)
    for k in range(1, 8):
        signal(lat, step(lon, 2 * k, NLON), batch)
    signal(lat, lon, 1 - batch)
    signal(lat, lon + 2 - 4 * lax.rem(lon // 2, 2), 1 - batch)
    return 22


class Gather:
    def __init__(self, slot, cells, own, send1, recv1, send2, recv2, send3, recv3):
        lat, lon, batch = place()
        self.q, self.core, self.cells = lon // 2, lax.rem(lon, 2), cells
        other = lon + 1 - 2 * self.core
        here = cells.at[self.q, self.core]
        self.own = pltpu.make_async_copy(slot, here.at[lat], own)
        self.first = [
            remote(slot, here.at[lat], send1.at[k - 1], recv1.at[k - 1], step(lat, k, NLAT), lon, batch)
            for k in range(1, NLAT)
        ]
        self.second = {
            k: remote(here, here, send2.at[k - 1], recv2.at[k - 1], lat, step(lon, 2 * k, NLON), batch)
            for k in range(1, 8)
        }
        self.third = {}
        for k in range(8):
            block = cells.at[lax.rem(self.q + 8 - k, 8), self.core]
            self.third[k] = remote(block, block, send3.at[k], recv3.at[k], lat, other, batch)

    def begin(self):
        for k in (4, 3, 5, 2, 6, 1, 7):
            self.first[k - 1].start()
        self.own.start()

    def middle(self):
        self.own.wait()
        for copy in self.first:
            copy.wait()
        for k in (3, 5, 1, 7, 4, 2, 6):
            self.second[k].start()
        self.third[0].start()

    def end(self, table, total):
        order = (0, 2, 6, 4, 1, 7, 3, 5)
        for i, k in enumerate(order):
            if i + 1 < 8:
                ahead = order[i + 1]
                self.second[ahead].wait()
                self.third[ahead].start()
            self.third[k].wait()
            at = lax.rem(self.q + 8 - k, 8)
            part = dot(table[at], self.cells[at].reshape(256, C))
            if i == 0:
                total[...] = part
            else:
                total[...] += part


def store_rows(parts, block, first):
    n, at = block.shape[0], 0
    while at < n:
        g, inside = divmod(first + at, 72)
        size = min(n - at, 72 - inside)
        parts[g // 16, (g // 4) % 4, g % 4, inside : inside + size, :] = block[at : at + size].astype(BF16)
        at += size


class Reduce:
    def __init__(self, x_first, parts, got1, acc1, got2, acc2, got3, blocks, got4, sems):
        s1, r1, s2, r2, s3, r3, s4, r4 = sems
        self.bufs = parts, got1, acc1, got2, acc2, got3, blocks, got4
        self.x_first = x_first
        lat, lon, batch = place()
        self.lat, self.core = lat, lax.rem(lon, 2)
        self.x = lon // 4
        self.y = lax.rem(lon // 2, 2) * 2 + batch
        core, x, y = self.core, self.x, self.y
        self.one = remote(parts.at[1 - core], got1, s1, r1, lat, lon + 1 - 2 * core, batch)

        def peer(along_x, k):
            if along_x:
                return lax.rem(x + k, 4), (lat, step(lon, 4 * k, NLON), batch)
            to = lax.rem(y + k, 4)
            return to, (lat, x * 4 + (to // 2) * 2 + core, lax.rem(to, 2))

        self.two, self.three = [], []
        for k in range(1, 4):
            to, device = peer(x_first, k)
            src = acc1.at[:, to] if x_first else acc1.at[to]
            self.two.append(remote(src, got2.at[k - 1], s2.at[k - 1], r2.at[k - 1], *device))
            to, device = peer(not x_first, k)
            self.three.append(remote(acc2.at[to], got3.at[k - 1], s3.at[k - 1], r3.at[k - 1], *device))
        to_lat = core * 4 + y
        self.is_own = to_lat == lat
        self.e_own = lax.rem(lon, 4) * 2 + batch
        self.four = [
            remote(blocks.at[e], got4.at[lat], s4.at[e], r4.at[lat], to_lat, x * 4 + e // 2, e % 2) for e in range(8)
        ]
        self.arrive = [remote(blocks.at[0], got4.at[h], s4.at[0], r4.at[h], to_lat, x * 4, 0) for h in range(8)]

    def swap_cores(self):
        self.one.start()

    def first_axis(self):
        parts, got1, acc1 = self.bufs[:3]
        self.one.wait()

        def add(i, _):
            for j in range(4):
                acc1[i, j] = (parts[self.core, i, j].astype(F32) + got1[i, j].astype(F32)).astype(BF16)
            return 0

        lax.fori_loop(0, 4, add, 0)
        for copy in self.two:
            copy.start()

    def second_axis(self):
        _, _, acc1, got2, acc2 = self.bufs[:5]
        for copy in self.two:
            copy.wait()
        for i in range(4):
            mine = acc1[i, self.x] if self.x_first else acc1[self.y, i]
            acc2[i] = (
                mine.astype(F32) + got2[0, i].astype(F32) + got2[1, i].astype(F32) + got2[2, i].astype(F32)
            ).astype(BF16)
        for copy in self.three:
            copy.start()

    def to_owners(self, with_mixing):
        _, _, _, _, acc2, got3, blocks, got4 = self.bufs
        for copy in self.three:
            copy.wait()
        mine = acc2[self.y if self.x_first else self.x]
        total = mine.astype(F32) + got3[0].astype(F32) + got3[1].astype(F32) + got3[2].astype(F32)
        for e in range(8):
            rows = [total[9 * e : 9 * e + 9], total[72 + e : 73 + e], jnp.zeros((6, C), F32)]
            blocks[e] = jnp.concatenate(rows, axis=0).astype(BF16)
        for e in range(8):
            mine = self.is_own & (self.e_own == e)

            @pl.when(jnp.logical_not(mine))
            def _():
                self.four[e].start()

            @pl.when(mine)
            def _():
                got4[self.lat] = blocks[e]

    def finish(self):
        got4 = self.bufs[-1]
        total = None
        for h in range(8):

            @pl.when(jnp.logical_not(self.is_own & (self.lat == h)))
            def _():
                self.arrive[h].wait_recv()

        for h in range(8):
            total = got4[h].astype(F32) if h == 0 else total + got4[h].astype(F32)
        for e in range(8):

            @pl.when(jnp.logical_not(self.is_own & (self.e_own == e)))
            def _():
                self.four[e].wait_send()

        return total


INPUTS = (
    "field", "cot", "dec", "sum8", "k0", "pool2", "k1", "pool4", "pick", "gain", "table", "synth", "mixing", "place",
    "up4", "up2", "up8",
)


def kernel(scales, n_in, *refs):
    src = dict(zip(INPUTS, refs[:n_in]))
    out_pred, out0, out1, outm, outg = refs[n_in : n_in + 5]
    names = [n for n in INPUTS if n != "field"]
    v = dict(zip(names, refs[n_in + 5 :]))
    (
        load_sem, ext, fs, x3, x3c, l0f, c1s, x13, level0, da0, level1, a1, p1, slot, gl2, edges, ring, halo_s, halo_r,
        edge_s, edge_r, halo_own, cells1, cells2, g1sem, g2sem, sc, coef, slot2, spec_own, level2, pred, pred_sem,
        g1s, slope, xg, gp0, red0, red1, gain_in, gain_got, gain_s, gain_r,
    ) = refs[n_in + 5 + len(names) :]
    cot, k0, k1, gain, table, mixing = (v[n] for n in ("cot", "k0", "k1", "gain", "table", "mixing"))
    lat, lon, batch = place()
    mode_owner = lat * NLON + lon
    base = pl.multiple_of(8 * (mode_owner // 2), 8)

    own = pltpu.make_async_copy(src["field"], ext.at[pl.ds(3, 16), pl.ds(16, 48)], halo_own)
    own.start()
    loads = {}
    for i, n in enumerate(names):
        ref = src[n].at[mode_owner] if n == "synth" else src[n]
        loads[n] = pltpu.make_async_copy(ref, v[n], load_sem.at[i])
        loads[n].start()
    n_peers = greet_all()
    pl.semaphore_wait(pltpu.get_barrier_semaphore(), n_peers)
    halo = halo_copies(src["field"], ext, halo_s, halo_r)
    for copy in halo:
        copy.start()

    for n in ("cot", "dec", "sum8"):
        loads[n].wait()
    for half in range(2):
        part = cot[8 * half : 8 * half + 8].reshape(384, C)
        a1[4 * half : 4 * half + 4] = dot(v["dec"][...], part).reshape(4, 32, C)
        gl2[8 * half : 8 * half + 8] = dot(v["sum8"][...], part)
    c1s[...] = jnp.zeros_like(c1s)
    g1s[...] = jnp.zeros_like(g1s)
    red0[0][:, :, :, 72:80, :] = jnp.zeros((2, 4, 4, 8, C), BF16)
    own.wait()
    fs[3:19, 16:64] = ext[3:19, 16:64].astype(F32)
    for n in ("k0", "pool2", "k1", "pool4", "pick"):
        loads[n].wait()
    for copy in halo:
        copy.wait()

    edge_top = lat == 0
    edge_bot = lat == NLAT - 1
    fs[3:19, 0:16] = ext[3:19, 0:16].astype(F32)
    fs[3:19, 64:80] = ext[3:19, 64:80].astype(F32)
    fs[0:3] = jnp.where(edge_top, 0.0, ext[0:3].astype(F32))
    fs[19:22] = jnp.where(edge_bot, 0.0, ext[19:22].astype(F32))
    for b in range(3):
        x3[:, :, b * C : (b + 1) * C] = fs[:, 7 + b : 71 + b, :].astype(BF16)

    def rows4(i, _):
        y = 4 * i
        acc = dot(x3[pl.ds(y, 4)].reshape(256, 3 * C), k0[0])
        acc += dot(x3[pl.ds(y + 1, 4)].reshape(256, 3 * C), k0[1])
        acc += dot(x3[pl.ds(y + 2, 4)].reshape(256, 3 * C), k0[2])
        act, grad = gelu_both(acc)
        out = fs[pl.ds(y + 1, 4), 8:72, :] + act.reshape(4, 64, C)
        l0f[pl.ds(y, 4)] = out.astype(BF16)
        level0[pl.ds(y, 4)] = out[:, 8:56].astype(BF16)
        da0[pl.ds(y, 4)] = grad.reshape(4, 64, C)[:, 8:56].astype(BF16)
        return 0

    lax.fori_loop(0, 5, rows4, 0)

    for y in range(10):
        row = dot(v["pool2"][...], l0f[2 * y : 2 * y + 2].reshape(128, C)).astype(BF16).astype(F32)
        if y == 0:
            row = jnp.where(edge_top, 0.0, row)
        if y == 9:
            row = jnp.where(edge_bot, 0.0, row)
        c1s[y, 8:40, :] = row
    for b in range(3):
        x13[:, :, b * C : (b + 1) * C] = c1s[:, 7 + b : 39 + b, :].astype(BF16)
    pre = dot(x13[0:8].reshape(256, 3 * C), k1[0])
    pre += dot(x13[1:9].reshape(256, 3 * C), k1[1])
    pre += dot(x13[2:10].reshape(256, 3 * C), k1[2])
    act, _ = gelu_both(pre)
    col = lax.broadcasted_iota(jnp.int32, (8, 32, C), 1)
    mine = (col >= 4) & (col < 28)
    p1[...] = jnp.where(mine, pre.reshape(8, 32, C), 0.0)
    lev1 = jnp.where(mine, c1s[1:9, 8:40, :] + act.reshape(8, 32, C), 0.0).astype(BF16)
    level1[...] = lev1
    for half in range(2):
        slot[8 * half : 8 * half + 8] = dot(v["pool4"][...], lev1[4 * half : 4 * half + 4].reshape(128, C)).astype(BF16)

    gather = Gather(slot, cells1, *g1sem)
    gather.begin()
    edges[:, 0] = dot(v["pick"][...], a1[...].reshape(256, C).astype(BF16)).astype(BF16).reshape(4, 16, C)
    edges[:, 1] = dot(v["pick"][...], p1[...].reshape(256, C).astype(BF16)).astype(BF16).reshape(4, 16, C)
    edge = edge_copies(edges, ring, edge_s, edge_r)
    for copy in edge:
        copy.start()
    for b in range(3):
        x3c[:, :, b * C : (b + 1) * C] = fs[2:20, 15 + b : 63 + b, :].astype(BF16)
    for n in ("gain", "table", "synth", "mixing", "place", "up4", "up2", "up8"):
        loads[n].wait()
    gather.middle()
    for copy in edge:
        copy.wait()
    g1s[:, 8:40, :] = dot(v["place"][...], ring[:, 0].reshape(160, C)).reshape(10, 32, C)
    g1s[1:9, 8:40, :] += a1[...]
    slope[...] = dot(v["place"][...], ring[:, 1].reshape(160, C)).reshape(10, 32, C)
    slope[1:9] += p1[...]
    _, grad1 = gelu_both(slope[...])
    slope[...] = grad1
    gather.end(table, sc)

    gr, gi = gain[:, :C], gain[:, C:]
    sr, si = sc[0:512], sc[512:1024]
    coef[0:512] = (gr * sr - gi * si).astype(BF16)
    coef[512:1024] = (gr * si + gi * sr).astype(BF16)
    filt = dot(v["synth"][8:24], coef[...]).astype(BF16)
    mixed = dot(filt, mixing[...])
    act, grad = gelu_both(mixed)
    cell = lax.rem(lax.broadcasted_iota(jnp.int32, (16, C), 0), 8)
    gm = jnp.where((cell >= 1) & (cell < 7), gl2[...] * grad, 0.0).astype(BF16)
    slot2[...] = dot_cols(gm, mixing[...]).astype(BF16)

    gather = Gather(slot2, cells2, *g2sem)
    gather.begin()
    level2[...] = (slot[...].astype(F32) + act).astype(BF16)
    mix = dot_rows(filt, gm)
    for g in range(32):
        red1[0][g // 16, (g // 4) % 4, g % 4, 72:80, :] = mix[8 * g : 8 * g + 8].astype(BF16)
    spec_own[:, :C] = sc[pl.ds(base, 8), :]
    spec_own[:, C:] = sc[pl.ds(512 + base, 8), :]

    def predict(r):
        low = dot(v["up2"][...], level1[r]) + dot(v["up8"][...], level2[8 * (r // 4) : 8 * (r // 4) + 8])
        high = level0[2 * r + 2 : 2 * r + 4].astype(F32) + low.reshape(2, 48, C)
        pred[2 * r : 2 * r + 2] = high.astype(BF16)

    for r in range(4):
        predict(r)
    gather.middle()
    for r in range(4, 8):
        predict(r)
    pred_out = pltpu.make_async_copy(pred, out_pred, pred_sem)
    pred_out.start()
    gather.end(table, sc)

    er, ei = sc[0:512], sc[512:1024]
    coef[0:512] = (gr * er + gi * ei).astype(BF16)
    coef[512:1024] = (gr * ei - gi * er).astype(BF16)
    back = dot(v["synth"][...], coef[...]).astype(BF16)
    gl1 = g1s[:, 8:40, :] + dot(v["up4"][...], back).reshape(10, 32, C)
    col = lax.broadcasted_iota(jnp.int32, (10, 32, C), 1)
    row = lax.broadcasted_iota(jnp.int32, (10, 32, C), 0)
    first = jnp.where(edge_top, 1, 0)
    last = jnp.where(edge_bot, 9, 10)
    valid = (col >= 3) & (col < 29) & (row >= first) & (row < last)
    gp1 = jnp.where(valid, gl1 * slope[...], 0.0)
    g1s[:, 8:40, :] = gp1
    gown = jnp.where((col[1:9] >= 4) & (col[1:9] < 28), gp1[1:9], 0.0).astype(BF16).reshape(256, C)
    for a in range(3):
        store_rows(red1[0], dot_rows(x13[a : a + 8].reshape(256, 3 * C), gown), 768 * a)
    sum1 = Reduce(False, *red1[:8], red1[8:])
    sum1.swap_cores()

    gc1 = gl1[1:9].reshape(256, C)
    for b in range(3):
        xg[...] = g1s[:, 7 + b : 39 + b, :].astype(BF16)
        for a in range(3):
            gc1 += dot_cols(xg[a : a + 8].reshape(256, C), k1[2 - a, (2 - b) * C : (3 - b) * C, :])
    high = gc1.astype(BF16)
    low = (gc1 - high.astype(F32)).astype(BF16)
    for r in range(8):
        up = dot(v["up2"][...], high[32 * r : 32 * r + 32]) + dot(v["up2"][...], low[32 * r : 32 * r + 32])
        gl0 = cot[2 * r : 2 * r + 2].astype(F32) + 0.25 * up.reshape(2, 48, C)
        gp0[2 * r : 2 * r + 2] = (gl0 * da0[2 * r + 2 : 2 * r + 4].astype(F32)).astype(BF16)
    sum1.first_axis()
    for a in range(3):
        store_rows(red0[0], dot_rows(x3c[a : a + 16].reshape(768, 3 * C), gp0[...].reshape(768, C)), 768 * a)
    sum0 = Reduce(True, *red0[:8], red0[8:])
    sum0.swap_cores()

    br, bi = sc[pl.ds(base, 8), :], sc[pl.ds(512 + base, 8), :]
    m = lax.rem(base + lax.broadcasted_iota(jnp.int32, (8, C), 0), 32)
    weight = jnp.where(m == 0, 1.0, 2.0)
    ar, ai = spec_own[:, :C], spec_own[:, C:]
    gain_in[:, :C] = weight * (ar * br + ai * bi)
    gain_in[:, C:] = weight * (ar * bi - ai * br)
    swap = remote(gain_in, gain_got, gain_s, gain_r, lat, lon, 1 - batch)
    swap.start()

    sum0.first_axis()
    sum1.second_axis()
    swap.wait()
    gain_in[...] = gain_in[...] + gain_got[...]
    for batch_at in range(2):
        for lon_at in range(2):

            @pl.when((batch == batch_at) & (lax.rem(lon, 2) == lon_at))
            def _():
                at = 4 * lon_at + 2 * batch_at
                for i in range(2):
                    for j in range(4):
                        outg[4 * i + j : 4 * i + j + 1, :] = gain_in[at + i : at + i + 1, 128 * j : 128 * j + 128]

    sum1.to_owners(True)
    sum0.second_axis()
    sum0.to_owners(False)
    t1 = sum1.finish()
    for r in range(9):
        for j in range(2):
            out1[2 * r + j : 2 * r + j + 1, :] = scales[1] * t1[r : r + 1, 128 * j : 128 * j + 128]
    for j in range(2):
        outm[j : j + 1, :] = scales[2] * t1[9:10, 128 * j : 128 * j + 128]
    t0 = sum0.finish()
    for r in range(9):
        for j in range(2):
            out0[2 * r + j : 2 * r + j + 1, :] = scales[0] * t0[r : r + 1, 128 * j : 128 * j + 128]
    pred_out.wait()


def dma(*n):
    return pltpu.SemaphoreType.DMA(n)


def vmem(*shape, dtype=BF16):
    return pltpu.VMEM(shape, dtype)


def reduce_scratch():
    return (
        vmem(2, 4, 4, 80, C), vmem(4, 4, 80, C), vmem(4, 4, 80, C), vmem(3, 4, 80, C), vmem(4, 80, C),
        vmem(3, 80, C), vmem(8, 16, C), vmem(8, 16, C),
        dma(), dma(), dma(3), dma(3), dma(3), dma(3), dma(8), dma(8),
    )


def on_device(tables, field, kernel0, kernel1, mixing, gain, cotangent):
    table, synth, small = tables
    args = {k: jnp.asarray(a) for k, a in small.items()}
    args |= dict(
        field=field[0], cot=cotangent[0], k0=kernel0.reshape(3, 3 * C, C), k1=kernel1.reshape(3, 3 * C, C),
        mixing=mixing, gain=gain, table=jnp.asarray(table), synth=jnp.asarray(synth),
    )
    cells0 = 2 * 128 * 768
    scales = (1.0 / math.sqrt(cells0), 1.0 / math.sqrt(cells0 // 4), 1.0 / math.sqrt(cells0 // 64))
    names = [n for n in INPUTS if n != "field"]
    gathers = (dma(), dma(7), dma(7), dma(7), dma(7), dma(8), dma(8))
    scratch = [vmem(32, 1024) if n == "synth" else vmem(*args[n].shape, dtype=args[n].dtype) for n in names]
    scratch += [
        dma(len(names)), vmem(22, 80, C), vmem(22, 80, C, dtype=F32), vmem(22, 64, 3 * C), vmem(18, 48, 3 * C),
        vmem(20, 64, C), vmem(10, 48, C, dtype=F32), vmem(10, 32, 3 * C), vmem(20, 48, C), vmem(20, 48, C),
        vmem(8, 32, C), vmem(8, 32, C, dtype=F32), vmem(8, 32, C, dtype=F32), vmem(16, C), vmem(16, C, dtype=F32),
        vmem(4, 2, 16, C), vmem(10, 2, 16, C), dma(8), dma(8), dma(8), dma(8), dma(),
        vmem(8, 2, 8, 16, C), vmem(8, 2, 8, 16, C), gathers, gathers, vmem(1024, C, dtype=F32), vmem(1024, C),
        vmem(16, C), vmem(8, 2 * C, dtype=F32), vmem(16, C), vmem(ROWS, COLS, C), dma(),
        vmem(10, 48, C, dtype=F32), vmem(10, 32, C, dtype=F32), vmem(10, 32, C), vmem(16, 48, C),
        reduce_scratch(), reduce_scratch(), vmem(8, 2 * C, dtype=F32), vmem(8, 2 * C, dtype=F32), dma(), dma(),
    ]
    anywhere = pl.BlockSpec(memory_space=pl.ANY)
    here = pl.BlockSpec(memory_space=pltpu.VMEM)
    predicted, grad0, grad1, gradm, gradg = pl.pallas_call(
        functools.partial(kernel, scales, len(INPUTS)),
        out_shape=[jax.ShapeDtypeStruct((ROWS, COLS, C), BF16)]
        + [jax.ShapeDtypeStruct((n, 128), F32) for n in (18, 18, 2, 8)],
        in_specs=[anywhere] * len(INPUTS),
        out_specs=[anywhere] + [here] * 4,
        scratch_shapes=scratch,
        compiler_params=pltpu.CompilerParams(collective_id=0, has_side_effects=True, vmem_limit_bytes=VMEM_BYTES),
    )(*[args[n] for n in INPUTS])
    return predicted[None], grad0.reshape(-1), grad1.reshape(-1), gradm.reshape(-1), gradg.reshape(-1)


def solution(mesh):
    tables = (*spectral_tables(), cell_tables())
    tile = P("batch", "lat", "lon", None)
    split = P(("lat", "lon", "batch"))
    return jax.shard_map(
        functools.partial(on_device, tables), mesh=mesh, in_specs=(tile, P(), P(), P(), P(), tile),
        out_specs=(tile, split, split, split, split), check_vma=False,
    )
```

```python
import functools
import math

import jax
import jax.numpy as jnp
import ml_dtypes
import numpy as np
from jax import lax
from jax.experimental import pallas as pl
from jax.experimental.pallas import tpu as pltpu
from jax.sharding import PartitionSpec as P

MESH = pl.DeviceIdType.MESH
F32 = jnp.float32
BF16 = jnp.bfloat16
C = 256
NLAT, NLON = 8, 16
ROWS, COLS = 16, 48
VMEM_BYTES = 56 * 2**20


def spectral_tables():
    lat_n, lon_n, kl, km = 16, 96, 16, 32
    freq = np.repeat(np.arange(kl) - kl // 2, km)
    mode = np.tile(np.arange(km), kl)
    norm = 1.0 / math.sqrt(lat_n * lon_n)

    def phase(i, j):
        whole = (freq[:, None] * i[None] * lon_n + mode[:, None] * j[None] * lat_n) % (lat_n * lon_n)
        return 2.0 * np.pi * whole / (lat_n * lon_n)

    forward = np.zeros((2, kl * km, NLON, NLAT, 2, 8))
    for lon in range(NLON):
        for lat in range(NLAT):
            for r in range(2):
                j = lon * 6 + np.arange(6)
                ph = phase(np.full(6, lat * 2 + r), j)
                forward[0, :, lon, lat, r, 1:7] = np.cos(ph) * norm
                forward[1, :, lon, lat, r, 1:7] = -np.sin(ph) * norm
    forward = forward.reshape(2 * kl * km, NLON * NLAT * 16)
    weight = np.where(mode == 0, 1.0, 2.0) * norm
    back = np.zeros((NLAT * NLON, 32, 2, kl * km))
    for lat in range(NLAT):
        for lon in range(NLON):
            i = np.repeat(lat * 2 - 1 + np.arange(4), 8)
            j = np.tile(lon * 6 - 1 + np.arange(8), 4)
            ph = phase(i, j).T
            back[lat * NLON + lon, :, 0] = np.cos(ph) * weight
            back[lat * NLON + lon, :, 1] = -np.sin(ph) * weight
    back = back.reshape(NLAT * NLON, 32, 2 * kl * km)
    forward = forward.reshape(2 * kl * km, 8, 256).transpose(1, 0, 2)
    return forward.astype(ml_dtypes.bfloat16), back.astype(ml_dtypes.bfloat16)


def cell_tables():
    pool2 = np.zeros((32, 2, 64))
    for j in range(32):
        pool2[j, :, 2 * j : 2 * j + 2] = 0.25
    pool4 = np.zeros((8, 4, 32))
    for j in range(1, 7):
        pool4[j, :, 4 * j : 4 * j + 4] = 1 / 16
    dec = np.zeros((4, 32, 8, 48))
    for r in range(4):
        for j in range(24):
            dec[r, 4 + j, :, 8 * (j // 4) : 8 * (j // 4) + 8] += 1 / 16
            dec[r, 4 + j, 2 * r : 2 * r + 2, 2 * j : 2 * j + 2] += 1
    sum8 = np.zeros((8, 8, 48))
    for j in range(6):
        sum8[1 + j, :, 8 * j : 8 * j + 8] = 1
    pick = np.zeros((64, 8, 32))
    for half, row, col in ((0, 0, 4), (32, 7, 27)):
        for i in range(24):
            pick[half + i, row, 4 + i] = 1
        for r in range(8):
            pick[half + 24 + r, r, col] = 1
    place = np.zeros((10, 32, 10, 16))
    for j in range(24):
        place[0, 4 + j, j // 16, j % 16] = 1
        place[9, 4 + j, 2 + j // 16, j % 16] = 1
    for r in range(8):
        place[1 + r, 3, 4, 8 + r] = 1
        place[1 + r, 28, 5, 8 + r] = 1
    place[0, 3, 6, 7] = 1
    place[0, 28, 7, 0] = 1
    place[9, 3, 8, 7] = 1
    place[9, 28, 9, 0] = 1
    up4 = np.zeros((10, 32, 4, 8))
    for r in range(10):
        for j in range(32):
            up4[r, j, (r + 3) // 4, j // 4] = 1 / 16
    up2 = np.zeros((2, 48, 32))
    up8 = np.zeros((2, 48, 8))
    for j in range(48):
        up2[:, j, 4 + j // 2] = 1
        up8[:, j, 1 + j // 8] = 1
    hpick = np.zeros((160, 16, 48))
    hplace = np.zeros((22, 32, 160))
    for j in range(3):
        for r in range(16):
            hpick[3 * r + j, r, j] = 1
            hpick[48 + 3 * r + j, r, 45 + j] = 1
            hplace[3 + r, 16 + j, 3 * r + j] = 1
            hplace[3 + r, 13 + j, 48 + 3 * r + j] = 1
        for i in range(3):
            for seg, row, col, to_row, to_col in (
                (96, 0, 0, 19, 16), (112, 0, 45, 19, 13), (128, 13, 0, 0, 16), (144, 13, 45, 0, 13)
            ):
                hpick[seg + 3 * i + j, row + i, col + j] = 1
                hplace[to_row + i, to_col + j, seg + 3 * i + j] = 1
    shapes = dict(
        hpick=(hpick, (160, 768)), hplace=(hplace, (704, 160)),
        pool2=(pool2, (32, 128)), pool4=(pool4, (8, 128)), dec=(dec, (128, 384)), sum8=(sum8, (8, 384)),
        pick=(pick, (64, 256)), place=(place, (320, 160)), up4=(up4, (320, 32)), up2=(up2, (96, 32)),
        up8=(up8, (96, 8)),
    )
    return {k: v.reshape(s).astype(ml_dtypes.bfloat16) for k, (v, s) in shapes.items()}


def dot(a, b):
    return jnp.dot(a, b, preferred_element_type=F32)


def dot_rows(a, b):
    return lax.dot_general(a, b, (((0,), (0,)), ((), ())), preferred_element_type=F32)


def dot_cols(a, b):
    return lax.dot_general(a, b, (((1,), (1,)), ((), ())), preferred_element_type=F32)


def gelu_both(v):
    k, q = 0.7978845608028654, 0.044715
    sq = v * v
    t = jnp.tanh(k * (v * (1.0 + q * sq)))
    half = 0.5 * (1.0 + t)
    return v * half, half + (0.5 * v) * (1.0 - t * t) * (k * (1.0 + (3.0 * q) * sq))


def place():
    return lax.axis_index("lat"), lax.axis_index("lon"), lax.axis_index("batch")


def step(pos, by, n):
    return lax.rem(pos + (by + n), n)


def signal(lat, lon, batch):
    pl.semaphore_signal(
        pltpu.get_barrier_semaphore(), inc=1, device_id={"lat": lat, "lon": lon, "batch": batch}, device_id_type=MESH
    )


def remote(src, dst, send, recv, lat, lon, batch):
    return pltpu.make_async_remote_copy(
        src_ref=src, dst_ref=dst, send_sem=send, recv_sem=recv,
        device_id={"lat": lat, "lon": lon, "batch": batch}, device_id_type=MESH,
    )


NEIGHBOURS = ((1, 0), (-1, 0), (0, 1), (0, -1), (1, 1), (1, -1), (-1, 1), (-1, -1))


HALO_SENDS = (
    ((0, -1), 0, 48), ((0, 1), 48, 48), ((-1, -1), 96, 16), ((-1, 1), 112, 16), ((1, -1), 128, 16), ((1, 1), 144, 16),
)


def halo_copies(field, rows_top, rows_bot, packed, halo, send, recv):
    lat, lon, batch = place()
    copies = [
        remote(packed.at[pl.ds(at, n)], halo.at[pl.ds(at, n)], send.at[i], recv.at[i],
               step(lat, dlat, NLAT), step(lon, dlon, NLON), batch)
        for i, ((dlat, dlon), at, n) in enumerate(HALO_SENDS)
    ]
    copies.append(remote(field.at[pl.ds(13, 3)], rows_top, send.at[6], recv.at[6], step(lat, 1, NLAT), lon, batch))
    copies.append(remote(field.at[pl.ds(0, 3)], rows_bot, send.at[7], recv.at[7], step(lat, -1, NLAT), lon, batch))
    return copies


EDGE_SENDS = (
    ((1, 0), 2, 2, 0), ((-1, 0), 0, 2, 2), ((0, 1), 3, 1, 4), ((0, -1), 1, 1, 5),
    ((1, 1), 3, 1, 6), ((1, -1), 2, 1, 7), ((-1, 1), 1, 1, 8), ((-1, -1), 0, 1, 9),
)


def edge_copies(edges, ring, send, recv):
    lat, lon, batch = place()
    return [
        remote(
            edges.at[pl.ds(seg, n)], ring.at[pl.ds(at, n)], send.at[i], recv.at[i],
            step(lat, dlat, NLAT), step(lon, dlon, NLON), batch,
        )
        for i, ((dlat, dlon), seg, n, at) in enumerate(EDGE_SENDS)
    ]


def greet_all():
    lat, lon, batch = place()
    for k in range(1, NLAT):
        signal(step(lat, k, NLAT), lon, batch)
    for k in (1, -1):
        signal(lat, step(lon, k, NLON), batch)
    for dlat, dlon in NEIGHBOURS[4:]:
        signal(step(lat, dlat, NLAT), step(lon, dlon, NLON), batch)
    for k in range(1, 8):
        signal(lat, step(lon, 2 * k, NLON), batch)
    signal(lat, lon, 1 - batch)
    signal(lat, lon + 2 - 4 * lax.rem(lon // 2, 2), 1 - batch)
    return 22


class Gather:
    PAIRS = (0, 1, 3, 2)
    FAR_FIRST = (3, 5, 1, 7, 4, 2, 6)
    NEAR_FIRST = (0, 2, 6, 4, 1, 7, 3, 5)

    def __init__(self, slot, cells, send1, recv1, send2, recv2, send3, recv3):
        lat, lon, batch = place()
        self.q, self.core, self.cells, self.lat = lon // 2, lax.rem(lon, 2), cells, lat
        other = lon + 1 - 2 * self.core
        here = cells.at[self.q, self.core]
        self.own = pltpu.make_async_copy(slot, here.at[lat], recv1.at[lat])
        self.first = [
            remote(slot, here.at[lat], send1.at[k - 1], recv1.at[lat], step(lat, k, NLAT), lon, batch)
            for k in range(1, NLAT)
        ]
        self.arrived = lambda l: pltpu.make_async_copy(slot, here.at[l], recv1.at[l])
        self.second, self.third = {}, {}
        for j, off in enumerate(self.PAIRS):
            pair = pl.ds(2 * lax.rem(lat // 2 + off, 4), 2)
            for k in range(1, 8):
                self.second[k, j] = remote(
                    here.at[pair], here.at[pair], send2.at[k - 1, j], recv2.at[k - 1, j],
                    lat, step(lon, 2 * k, NLON), batch,
                )
        for k in range(8):
            block = cells.at[lax.rem(self.q + 8 - k, 8), self.core]
            self.third[k] = remote(block, block, send3.at[k], recv3.at[k], lat, other, batch)

    def begin(self):
        for k in (4, 3, 5, 2, 6, 1, 7):
            self.first[k - 1].start()
        self.own.start()

    def advance(self, j):
        pair = lax.rem(self.lat // 2 + self.PAIRS[j], 4)
        for i in range(2):
            self.arrived(2 * pair + i).wait()
        for k in self.FAR_FIRST:
            self.second[k, j].start()
        if j == 3:
            self.third[0].start()

    def end(self, table, total):
        for i, k in enumerate(self.NEAR_FIRST):
            if i + 1 < 8:
                ahead = self.NEAR_FIRST[i + 1]
                for j in range(4):
                    self.second[ahead, j].wait_recv()
                self.third[ahead].start()
            self.third[k].wait_recv()
            at = lax.rem(self.q + 8 - k, 8)
            part = dot(table[at], self.cells[at].reshape(256, C))
            if i == 0:
                total[...] = part
            else:
                total[...] += part

    def close(self):
        for copy in [*self.first, *self.second.values(), *self.third.values()]:
            copy.wait_send()


def store_rows(parts, block, first):
    n, at = block.shape[0], 0
    while at < n:
        g, inside = divmod(first + at, 72)
        size = min(n - at, 72 - inside)
        parts[g // 16, (g // 4) % 4, g % 4, inside : inside + size, :] = block[at : at + size].astype(BF16)
        at += size


class Reduce:
    def __init__(self, x_first, parts, got1, acc1, got2, acc2, got3, blocks, got4, sems):
        s1, r1, s2, r2, s3, r3, s4, r4 = sems
        self.bufs = parts, got1, acc1, got2, acc2, got3, blocks, got4
        self.x_first = x_first
        lat, lon, batch = place()
        self.lat, self.core = lat, lax.rem(lon, 2)
        self.x = lon // 4
        self.y = lax.rem(lon // 2, 2) * 2 + batch
        core, x, y = self.core, self.x, self.y
        self.one = remote(parts.at[1 - core], got1, s1, r1, lat, lon + 1 - 2 * core, batch)

        def peer(along_x, k):
            if along_x:
                return lax.rem(x + k, 4), (lat, step(lon, 4 * k, NLON), batch)
            to = lax.rem(y + k, 4)
            return to, (lat, x * 4 + (to // 2) * 2 + core, lax.rem(to, 2))

        self.two, self.three = [], []
        for k in range(1, 4):
            to, device = peer(x_first, k)
            src = acc1.at[:, to] if x_first else acc1.at[to]
            self.two.append(remote(src, got2.at[k - 1], s2.at[k - 1], r2.at[k - 1], *device))
            to, device = peer(not x_first, k)
            self.three.append(remote(acc2.at[to], got3.at[k - 1], s3.at[k - 1], r3.at[k - 1], *device))
        to_lat = core * 4 + y
        self.is_own = to_lat == lat
        self.e_own = lax.rem(lon, 4) * 2 + batch
        self.four = [
            remote(blocks.at[e], got4.at[lat], s4.at[e], r4.at[lat], to_lat, x * 4 + e // 2, e % 2) for e in range(8)
        ]
        self.arrive = [remote(blocks.at[0], got4.at[h], s4.at[0], r4.at[h], to_lat, x * 4, 0) for h in range(8)]

    def swap_cores(self):
        self.one.start()

    def first_axis(self):
        parts, got1, acc1 = self.bufs[:3]
        self.one.wait()

        def add(i, _):
            for j in range(4):
                acc1[i, j] = (parts[self.core, i, j].astype(F32) + got1[i, j].astype(F32)).astype(BF16)
            return 0

        lax.fori_loop(0, 4, add, 0)
        for copy in self.two:
            copy.start()

    def second_axis(self):
        _, _, acc1, got2, acc2 = self.bufs[:5]
        for copy in self.two:
            copy.wait()
        for i in range(4):
            mine = acc1[i, self.x] if self.x_first else acc1[self.y, i]
            acc2[i] = (
                mine.astype(F32) + got2[0, i].astype(F32) + got2[1, i].astype(F32) + got2[2, i].astype(F32)
            ).astype(BF16)
        for copy in self.three:
            copy.start()

    def to_owners(self, with_mixing):
        _, _, _, _, acc2, got3, blocks, got4 = self.bufs
        for copy in self.three:
            copy.wait()
        mine = acc2[self.y if self.x_first else self.x]
        total = mine.astype(F32) + got3[0].astype(F32) + got3[1].astype(F32) + got3[2].astype(F32)
        for e in range(8):
            rows = [total[9 * e : 9 * e + 9], total[72 + e : 73 + e], jnp.zeros((6, C), F32)]
            blocks[e] = jnp.concatenate(rows, axis=0).astype(BF16)
        for e in range(8):
            mine = self.is_own & (self.e_own == e)

            @pl.when(jnp.logical_not(mine))
            def _():
                self.four[e].start()

            @pl.when(mine)
            def _():
                got4[self.lat] = blocks[e]

    def finish(self):
        got4 = self.bufs[-1]
        total = None
        for h in range(8):

            @pl.when(jnp.logical_not(self.is_own & (self.lat == h)))
            def _():
                self.arrive[h].wait_recv()

        for h in range(8):
            total = got4[h].astype(F32) if h == 0 else total + got4[h].astype(F32)
        for e in range(8):

            @pl.when(jnp.logical_not(self.is_own & (self.e_own == e)))
            def _():
                self.four[e].wait_send()

        return total


INPUTS = (
    "field", "hpick", "cot", "dec", "sum8", "hplace", "k0", "pool2", "k1", "pool4", "pick", "gain", "table", "synth", "mixing", "place",
    "up4", "up2", "up8",
)


def kernel(scales, n_in, *refs):
    src = dict(zip(INPUTS, refs[:n_in]))
    out_pred, out0, out1, outm, outg = refs[n_in : n_in + 5]
    names = list(INPUTS)
    v = dict(zip(names, refs[n_in + 5 :]))
    (
        load_sem, packed, halo_in, rows_top, rows_bot, fs, x3, x3c, l0f, c1s, x13, level0, da0, level1, a1, p1, slot, gl2, edges, ring, halo_s, halo_r,
        edge_s, edge_r, cells1, cells2, g1sem, g2sem, sc, coef, slot2, spec_own, level2, pred, pred_sem,
        g1s, slope, xg, gp0, red0, red1, gain_in, gain_got, gain_s, gain_r,
    ) = refs[n_in + 5 + len(names) :]
    cot, k0, k1, gain, table, mixing = (v[n] for n in ("cot", "k0", "k1", "gain", "table", "mixing"))
    field = v["field"]
    lat, lon, batch = place()
    mode_owner = lat * NLON + lon
    base = pl.multiple_of(8 * (mode_owner // 2), 8)

    loads = {}
    for i, n in enumerate(names):
        ref = src[n].at[mode_owner] if n == "synth" else src[n]
        loads[n] = pltpu.make_async_copy(ref, v[n], load_sem.at[i])
        loads[n].start()
    n_peers = greet_all()
    loads["field"].wait()
    loads["hpick"].wait()
    packed[...] = dot(v["hpick"][...], field[...].reshape(768, C)).astype(BF16)
    pl.semaphore_wait(pltpu.get_barrier_semaphore(), n_peers)
    halo = halo_copies(field, rows_top, rows_bot, packed, halo_in, halo_s, halo_r)
    for copy in halo:
        copy.start()

    for n in ("cot", "dec", "sum8"):
        loads[n].wait()
    for half in range(2):
        part = cot[8 * half : 8 * half + 8].reshape(384, C)
        a1[4 * half : 4 * half + 4] = dot(v["dec"][...], part).reshape(4, 32, C)
        gl2[8 * half : 8 * half + 8] = dot(v["sum8"][...], part)
    c1s[...] = jnp.zeros_like(c1s)
    g1s[...] = jnp.zeros_like(g1s)
    red0[0][:, :, :, 72:80, :] = jnp.zeros((2, 4, 4, 8, C), BF16)
    fs[3:19, 16:64] = field[...].astype(F32)
    for n in ("hplace", "k0", "pool2", "k1", "pool4", "pick"):
        loads[n].wait()
    for copy in halo:
        copy.wait()

    edge_top = lat == 0
    edge_bot = lat == NLAT - 1
    fs[0:3, 16:64] = jnp.where(edge_top, 0.0, rows_top[...].astype(F32))
    fs[19:22, 16:64] = jnp.where(edge_bot, 0.0, rows_bot[...].astype(F32))
    sides = dot(v["hplace"][...], halo_in[...]).reshape(22, 32, C)
    for half, at in ((0, 0), (16, 64)):
        fs[0:3, at : at + 16] = jnp.where(edge_top, 0.0, sides[0:3, half : half + 16])
        fs[3:19, at : at + 16] = sides[3:19, half : half + 16]
        fs[19:22, at : at + 16] = jnp.where(edge_bot, 0.0, sides[19:22, half : half + 16])
    for b in range(3):
        x3[:, :, b * C : (b + 1) * C] = fs[:, 7 + b : 71 + b, :].astype(BF16)

    def rows4(i, _):
        y = 4 * i
        acc = dot(x3[pl.ds(y, 4)].reshape(256, 3 * C), k0[0])
        acc += dot(x3[pl.ds(y + 1, 4)].reshape(256, 3 * C), k0[1])
        acc += dot(x3[pl.ds(y + 2, 4)].reshape(256, 3 * C), k0[2])
        act, grad = gelu_both(acc)
        out = fs[pl.ds(y + 1, 4), 8:72, :] + act.reshape(4, 64, C)
        l0f[pl.ds(y, 4)] = out.astype(BF16)
        level0[pl.ds(y, 4)] = out[:, 8:56].astype(BF16)
        da0[pl.ds(y, 4)] = grad.reshape(4, 64, C)[:, 8:56].astype(BF16)
        return 0

    lax.fori_loop(0, 5, rows4, 0)

    for y in range(10):
        row = dot(v["pool2"][...], l0f[2 * y : 2 * y + 2].reshape(128, C)).astype(BF16).astype(F32)
        if y == 0:
            row = jnp.where(edge_top, 0.0, row)
        if y == 9:
            row = jnp.where(edge_bot, 0.0, row)
        c1s[y, 8:40, :] = row
    for b in range(3):
        x13[:, :, b * C : (b + 1) * C] = c1s[:, 7 + b : 39 + b, :].astype(BF16)
    pre = dot(x13[0:8].reshape(256, 3 * C), k1[0])
    pre += dot(x13[1:9].reshape(256, 3 * C), k1[1])
    pre += dot(x13[2:10].reshape(256, 3 * C), k1[2])
    act, _ = gelu_both(pre)
    col = lax.broadcasted_iota(jnp.int32, (8, 32, C), 1)
    mine = (col >= 4) & (col < 28)
    p1[...] = jnp.where(mine, pre.reshape(8, 32, C), 0.0)
    lev1 = jnp.where(mine, c1s[1:9, 8:40, :] + act.reshape(8, 32, C), 0.0).astype(BF16)
    level1[...] = lev1
    for half in range(2):
        slot[8 * half : 8 * half + 8] = dot(v["pool4"][...], lev1[4 * half : 4 * half + 4].reshape(128, C)).astype(BF16)

    gather = Gather(slot, cells1, *g1sem)
    gather.begin()
    edges[:, 0] = dot(v["pick"][...], a1[...].reshape(256, C).astype(BF16)).astype(BF16).reshape(4, 16, C)
    edges[:, 1] = dot(v["pick"][...], p1[...].reshape(256, C).astype(BF16)).astype(BF16).reshape(4, 16, C)
    edge = edge_copies(edges, ring, edge_s, edge_r)
    for copy in edge:
        copy.start()
    for n in ("gain", "table", "synth", "mixing", "place", "up4", "up2", "up8"):
        loads[n].wait()
    for b in range(3):
        gather.advance(b)
        x3c[:, :, b * C : (b + 1) * C] = fs[2:20, 15 + b : 63 + b, :].astype(BF16)
    gather.advance(3)
    for copy in edge:
        copy.wait()
    g1s[:, 8:40, :] = dot(v["place"][...], ring[:, 0].reshape(160, C)).reshape(10, 32, C)
    g1s[1:9, 8:40, :] += a1[...]
    slope[...] = dot(v["place"][...], ring[:, 1].reshape(160, C)).reshape(10, 32, C)
    slope[1:9] += p1[...]
    _, grad1 = gelu_both(slope[...])
    slope[...] = grad1
    gather.end(table, sc)
    first_gather = gather

    gr, gi = gain[:, :C], gain[:, C:]
    sr, si = sc[0:512], sc[512:1024]
    coef[0:512] = (gr * sr - gi * si).astype(BF16)
    coef[512:1024] = (gr * si + gi * sr).astype(BF16)
    filt = dot(v["synth"][8:24], coef[...]).astype(BF16)
    mixed = dot(filt, mixing[...])
    act, grad = gelu_both(mixed)
    cell = lax.rem(lax.broadcasted_iota(jnp.int32, (16, C), 0), 8)
    gm = jnp.where((cell >= 1) & (cell < 7), gl2[...] * grad, 0.0).astype(BF16)
    slot2[...] = dot_cols(gm, mixing[...]).astype(BF16)

    gather = Gather(slot2, cells2, *g2sem)
    gather.begin()
    level2[...] = (slot[...].astype(F32) + act).astype(BF16)
    mix = dot_rows(filt, gm)
    for g in range(32):
        red1[0][g // 16, (g // 4) % 4, g % 4, 72:80, :] = mix[8 * g : 8 * g + 8].astype(BF16)
    spec_own[:, :C] = sc[pl.ds(base, 8), :]
    spec_own[:, C:] = sc[pl.ds(512 + base, 8), :]

    def predict(r):
        low = dot(v["up2"][...], level1[r]) + dot(v["up8"][...], level2[8 * (r // 4) : 8 * (r // 4) + 8])
        high = level0[2 * r + 2 : 2 * r + 4].astype(F32) + low.reshape(2, 48, C)
        pred[2 * r : 2 * r + 2] = high.astype(BF16)

    for j in range(4):
        gather.advance(j)
        predict(2 * j)
        predict(2 * j + 1)
    pred_out = pltpu.make_async_copy(pred, out_pred, pred_sem)
    pred_out.start()
    gather.end(table, sc)

    er, ei = sc[0:512], sc[512:1024]
    coef[0:512] = (gr * er + gi * ei).astype(BF16)
    coef[512:1024] = (gr * ei - gi * er).astype(BF16)
    back = dot(v["synth"][...], coef[...]).astype(BF16)
    gl1 = g1s[:, 8:40, :] + dot(v["up4"][...], back).reshape(10, 32, C)
    col = lax.broadcasted_iota(jnp.int32, (10, 32, C), 1)
    row = lax.broadcasted_iota(jnp.int32, (10, 32, C), 0)
    first = jnp.where(edge_top, 1, 0)
    last = jnp.where(edge_bot, 9, 10)
    valid = (col >= 3) & (col < 29) & (row >= first) & (row < last)
    gp1 = jnp.where(valid, gl1 * slope[...], 0.0)
    g1s[:, 8:40, :] = gp1
    gown = jnp.where((col[1:9] >= 4) & (col[1:9] < 28), gp1[1:9], 0.0).astype(BF16).reshape(256, C)
    for a in range(3):
        store_rows(red1[0], dot_rows(x13[a : a + 8].reshape(256, 3 * C), gown), 768 * a)
    sum1 = Reduce(False, *red1[:8], red1[8:])
    sum1.swap_cores()

    gc1 = gl1[1:9].reshape(256, C)
    for b in range(3):
        xg[...] = g1s[:, 7 + b : 39 + b, :].astype(BF16)
        for a in range(3):
            gc1 += dot_cols(xg[a : a + 8].reshape(256, C), k1[2 - a, (2 - b) * C : (3 - b) * C, :])
    high = gc1.astype(BF16)
    low = (gc1 - high.astype(F32)).astype(BF16)
    for r in range(8):
        up = dot(v["up2"][...], high[32 * r : 32 * r + 32]) + dot(v["up2"][...], low[32 * r : 32 * r + 32])
        gl0 = cot[2 * r : 2 * r + 2].astype(F32) + 0.25 * up.reshape(2, 48, C)
        gp0[2 * r : 2 * r + 2] = (gl0 * da0[2 * r + 2 : 2 * r + 4].astype(F32)).astype(BF16)
    sum1.first_axis()
    for a in range(3):
        store_rows(red0[0], dot_rows(x3c[a : a + 16].reshape(768, 3 * C), gp0[...].reshape(768, C)), 768 * a)
    sum0 = Reduce(True, *red0[:8], red0[8:])
    sum0.swap_cores()

    br, bi = sc[pl.ds(base, 8), :], sc[pl.ds(512 + base, 8), :]
    m = lax.rem(base + lax.broadcasted_iota(jnp.int32, (8, C), 0), 32)
    weight = jnp.where(m == 0, 1.0, 2.0)
    ar, ai = spec_own[:, :C], spec_own[:, C:]
    gain_in[:, :C] = weight * (ar * br + ai * bi)
    gain_in[:, C:] = weight * (ar * bi - ai * br)
    swap = remote(gain_in, gain_got, gain_s, gain_r, lat, lon, 1 - batch)
    swap.start()

    sum0.first_axis()
    sum1.second_axis()
    swap.wait()
    gain_in[...] = gain_in[...] + gain_got[...]
    for batch_at in range(2):
        for lon_at in range(2):

            @pl.when((batch == batch_at) & (lax.rem(lon, 2) == lon_at))
            def _():
                at = 4 * lon_at + 2 * batch_at
                for i in range(2):
                    for j in range(4):
                        outg[4 * i + j : 4 * i + j + 1, :] = gain_in[at + i : at + i + 1, 128 * j : 128 * j + 128]

    sum1.to_owners(True)
    sum0.second_axis()
    sum0.to_owners(False)
    t1 = sum1.finish()
    for r in range(9):
        for j in range(2):
            out1[2 * r + j : 2 * r + j + 1, :] = scales[1] * t1[r : r + 1, 128 * j : 128 * j + 128]
    for j in range(2):
        outm[j : j + 1, :] = scales[2] * t1[9:10, 128 * j : 128 * j + 128]
    t0 = sum0.finish()
    for r in range(9):
        for j in range(2):
            out0[2 * r + j : 2 * r + j + 1, :] = scales[0] * t0[r : r + 1, 128 * j : 128 * j + 128]
    first_gather.close()
    gather.close()
    pred_out.wait()


def dma(*n):
    return pltpu.SemaphoreType.DMA(n)


def vmem(*shape, dtype=BF16):
    return pltpu.VMEM(shape, dtype)


def reduce_scratch():
    return (
        vmem(2, 4, 4, 80, C), vmem(4, 4, 80, C), vmem(4, 4, 80, C), vmem(3, 4, 80, C), vmem(4, 80, C),
        vmem(3, 80, C), vmem(8, 16, C), vmem(8, 16, C),
        dma(), dma(), dma(3), dma(3), dma(3), dma(3), dma(8), dma(8),
    )


def hand_over(*arrays):
    n = len(arrays)

    def body(*refs):
        src, dst, buf, (come, go) = refs[:n], refs[n : 2 * n], refs[2 * n : 3 * n], refs[3 * n :]
        inward = [pltpu.make_async_copy(src[i], buf[i], come.at[i]) for i in range(n)]
        outward = [pltpu.make_async_copy(buf[i], dst[i], go.at[i]) for i in range(n)]
        for copy in inward:
            copy.start()
        for i in range(n):
            inward[i].wait()
            outward[i].start()
        for copy in outward:
            copy.wait()

    anywhere = pl.BlockSpec(memory_space=pl.ANY)
    return pl.pallas_call(
        body, out_shape=[jax.ShapeDtypeStruct(a.shape, a.dtype) for a in arrays], in_specs=[anywhere] * n,
        out_specs=[anywhere] * n, scratch_shapes=[vmem(*a.shape, dtype=a.dtype) for a in arrays] + [dma(n), dma(n)],
    )(*arrays)


def on_device(tables, field, kernel0, kernel1, mixing, gain, cotangent):
    table, synth, small = tables
    args = {k: jnp.asarray(a) for k, a in small.items()}
    args |= dict(
        field=field[0], cot=cotangent[0], k0=kernel0.reshape(3, 3 * C, C), k1=kernel1.reshape(3, 3 * C, C),
        mixing=mixing, gain=gain, table=jnp.asarray(table), synth=jnp.asarray(synth),
    )
    cells0 = 2 * 128 * 768
    scales = (1.0 / math.sqrt(cells0), 1.0 / math.sqrt(cells0 // 4), 1.0 / math.sqrt(cells0 // 64))
    names = INPUTS
    gathers = (dma(7), dma(8), dma(7, 4), dma(7, 4), dma(8), dma(8))
    scratch = [vmem(32, 1024) if n == "synth" else vmem(*args[n].shape, dtype=args[n].dtype) for n in names]
    scratch += [
        dma(len(names)), vmem(160, C), vmem(160, C), vmem(3, 48, C), vmem(3, 48, C), vmem(22, 80, C, dtype=F32), vmem(22, 64, 3 * C), vmem(18, 48, 3 * C),
        vmem(20, 64, C), vmem(10, 48, C, dtype=F32), vmem(10, 32, 3 * C), vmem(20, 48, C), vmem(20, 48, C),
        vmem(8, 32, C), vmem(8, 32, C, dtype=F32), vmem(8, 32, C, dtype=F32), vmem(16, C), vmem(16, C, dtype=F32),
        vmem(4, 2, 16, C), vmem(10, 2, 16, C), dma(8), dma(8), dma(8), dma(8),
        vmem(8, 2, 8, 16, C), vmem(8, 2, 8, 16, C), gathers, gathers, vmem(1024, C, dtype=F32), vmem(1024, C),
        vmem(16, C), vmem(8, 2 * C, dtype=F32), vmem(16, C), vmem(ROWS, COLS, C), dma(),
        vmem(10, 48, C, dtype=F32), vmem(10, 32, C, dtype=F32), vmem(10, 32, C), vmem(16, 48, C),
        reduce_scratch(), reduce_scratch(), vmem(8, 2 * C, dtype=F32), vmem(8, 2 * C, dtype=F32), dma(), dma(),
    ]
    anywhere = pl.BlockSpec(memory_space=pl.ANY)
    here = pl.BlockSpec(memory_space=pltpu.VMEM)
    predicted, grad0, grad1, gradm, gradg = pl.pallas_call(
        functools.partial(kernel, scales, len(INPUTS)),
        out_shape=[jax.ShapeDtypeStruct((ROWS, COLS, C), BF16)]
        + [jax.ShapeDtypeStruct((n, 128), F32) for n in (18, 18, 2, 8)],
        in_specs=[anywhere] * len(INPUTS),
        out_specs=[anywhere] + [here] * 4,
        scratch_shapes=scratch,
        compiler_params=pltpu.CompilerParams(collective_id=0, has_side_effects=True, vmem_limit_bytes=VMEM_BYTES),
    )(*[args[n] for n in INPUTS])
    predicted, grad0, grad1, gradm, gradg = hand_over(predicted, grad0, grad1, gradm, gradg)
    return predicted[None], grad0.reshape(-1), grad1.reshape(-1), gradm.reshape(-1), gradg.reshape(-1)


def solution(mesh):
    tables = (*spectral_tables(), cell_tables())
    tile = P("batch", "lat", "lon", None)
    split = P(("lat", "lon", "batch"))
    return jax.shard_map(
        functools.partial(on_device, tables), mesh=mesh, in_specs=(tile, P(), P(), P(), P(), tile),
        out_specs=(tile, split, split, split, split), check_vma=False,
    )
```

```python
import functools
import math

import jax
import jax.numpy as jnp
import ml_dtypes
import numpy as np
from jax import lax
from jax.experimental import pallas as pl
from jax.experimental.pallas import tpu as pltpu
from jax.sharding import PartitionSpec as P

MESH = pl.DeviceIdType.MESH
F32 = jnp.float32
BF16 = jnp.bfloat16
C = 256
NLAT, NLON = 8, 16
ROWS, COLS = 16, 48
VMEM_BYTES = 56 * 2**20


def spectral_tables():
    lat_n, lon_n, kl, km = 16, 96, 16, 32
    freq = np.repeat(np.arange(kl) - kl // 2, km)
    mode = np.tile(np.arange(km), kl)
    norm = 1.0 / math.sqrt(lat_n * lon_n)

    def phase(i, j):
        whole = (freq[:, None] * i[None] * lon_n + mode[:, None] * j[None] * lat_n) % (lat_n * lon_n)
        return 2.0 * np.pi * whole / (lat_n * lon_n)

    forward = np.zeros((2, kl * km, NLON, NLAT, 2, 8))
    for lon in range(NLON):
        for lat in range(NLAT):
            for r in range(2):
                j = lon * 6 + np.arange(6)
                ph = phase(np.full(6, lat * 2 + r), j)
                forward[0, :, lon, lat, r, 1:7] = np.cos(ph) * norm
                forward[1, :, lon, lat, r, 1:7] = -np.sin(ph) * norm
    forward = forward.reshape(2 * kl * km, NLON * NLAT * 16)
    weight = np.where(mode == 0, 1.0, 2.0) * norm
    back = np.zeros((NLAT * NLON, 32, 2, kl * km))
    for lat in range(NLAT):
        for lon in range(NLON):
            i = np.repeat(lat * 2 - 1 + np.arange(4), 8)
            j = np.tile(lon * 6 - 1 + np.arange(8), 4)
            ph = phase(i, j).T
            back[lat * NLON + lon, :, 0] = np.cos(ph) * weight
            back[lat * NLON + lon, :, 1] = -np.sin(ph) * weight
    back = back.reshape(NLAT * NLON, 32, 2 * kl * km)
    forward = forward.reshape(2 * kl * km, 8, 256).transpose(1, 0, 2)
    return forward.astype(ml_dtypes.bfloat16), back.astype(ml_dtypes.bfloat16)


def cell_tables():
    pool2 = np.zeros((32, 2, 64))
    for j in range(32):
        pool2[j, :, 2 * j : 2 * j + 2] = 0.25
    pool4 = np.zeros((8, 4, 32))
    for j in range(1, 7):
        pool4[j, :, 4 * j : 4 * j + 4] = 1 / 16
    dec = np.zeros((4, 32, 8, 48))
    for r in range(4):
        for j in range(24):
            dec[r, 4 + j, :, 8 * (j // 4) : 8 * (j // 4) + 8] += 1 / 16
            dec[r, 4 + j, 2 * r : 2 * r + 2, 2 * j : 2 * j + 2] += 1
    sum8 = np.zeros((8, 8, 48))
    for j in range(6):
        sum8[1 + j, :, 8 * j : 8 * j + 8] = 1
    pick = np.zeros((64, 8, 32))
    for half, row, col in ((0, 0, 4), (32, 7, 27)):
        for i in range(24):
            pick[half + i, row, 4 + i] = 1
        for r in range(8):
            pick[half + 24 + r, r, col] = 1
    place = np.zeros((10, 32, 10, 16))
    for j in range(24):
        place[0, 4 + j, j // 16, j % 16] = 1
        place[9, 4 + j, 2 + j // 16, j % 16] = 1
    for r in range(8):
        place[1 + r, 3, 4, 8 + r] = 1
        place[1 + r, 28, 5, 8 + r] = 1
    place[0, 3, 6, 7] = 1
    place[0, 28, 7, 0] = 1
    place[9, 3, 8, 7] = 1
    place[9, 28, 9, 0] = 1
    up4 = np.zeros((10, 32, 4, 8))
    for r in range(10):
        for j in range(32):
            up4[r, j, (r + 3) // 4, j // 4] = 1 / 16
    up2 = np.zeros((2, 48, 32))
    up8 = np.zeros((2, 48, 8))
    for j in range(48):
        up2[:, j, 4 + j // 2] = 1
        up8[:, j, 1 + j // 8] = 1
    hpick = np.zeros((160, 16, 48))
    hplace = np.zeros((22, 32, 160))
    for j in range(3):
        for r in range(16):
            hpick[3 * r + j, r, j] = 1
            hpick[48 + 3 * r + j, r, 45 + j] = 1
            hplace[3 + r, 16 + j, 3 * r + j] = 1
            hplace[3 + r, 13 + j, 48 + 3 * r + j] = 1
        for i in range(3):
            for seg, row, col, to_row, to_col in (
                (96, 0, 0, 19, 16), (112, 0, 45, 19, 13), (128, 13, 0, 0, 16), (144, 13, 45, 0, 13)
            ):
                hpick[seg + 3 * i + j, row + i, col + j] = 1
                hplace[to_row + i, to_col + j, seg + 3 * i + j] = 1
    shapes = dict(
        hpick=(hpick, (160, 768)), hplace=(hplace, (704, 160)),
        pool2=(pool2, (32, 128)), pool4=(pool4, (8, 128)), dec=(dec, (128, 384)), sum8=(sum8, (8, 384)),
        pick=(pick, (64, 256)), place=(place, (320, 160)), up4=(up4, (320, 32)), up2=(up2, (96, 32)),
        up8=(up8, (96, 8)),
    )
    return {k: v.reshape(s).astype(ml_dtypes.bfloat16) for k, (v, s) in shapes.items()}


def dot(a, b):
    return jnp.dot(a, b, preferred_element_type=F32)


def dot_rows(a, b):
    return lax.dot_general(a, b, (((0,), (0,)), ((), ())), preferred_element_type=F32)


def dot_cols(a, b):
    return lax.dot_general(a, b, (((1,), (1,)), ((), ())), preferred_element_type=F32)


def gelu_both(v):
    k, q = 0.7978845608028654, 0.044715
    sq = v * v
    t = jnp.tanh(k * (v * (1.0 + q * sq)))
    half = 0.5 * (1.0 + t)
    return v * half, half + (0.5 * v) * (1.0 - t * t) * (k * (1.0 + (3.0 * q) * sq))


def place():
    return lax.axis_index("lat"), lax.axis_index("lon"), lax.axis_index("batch")


def step(pos, by, n):
    return lax.rem(pos + (by + n), n)


def signal(lat, lon, batch):
    pl.semaphore_signal(
        pltpu.get_barrier_semaphore(), inc=1, device_id={"lat": lat, "lon": lon, "batch": batch}, device_id_type=MESH
    )


def remote(src, dst, send, recv, lat, lon, batch):
    return pltpu.make_async_remote_copy(
        src_ref=src, dst_ref=dst, send_sem=send, recv_sem=recv,
        device_id={"lat": lat, "lon": lon, "batch": batch}, device_id_type=MESH,
    )


NEIGHBOURS = ((1, 0), (-1, 0), (0, 1), (0, -1), (1, 1), (1, -1), (-1, 1), (-1, -1))


HALO_SENDS = (
    ((0, -1), 0, 48), ((0, 1), 48, 48), ((-1, -1), 96, 16), ((-1, 1), 112, 16), ((1, -1), 128, 16), ((1, 1), 144, 16),
)


def halo_copies(field, rows_top, rows_bot, packed, halo, send, recv):
    lat, lon, batch = place()
    copies = [
        remote(packed.at[pl.ds(at, n)], halo.at[pl.ds(at, n)], send.at[i], recv.at[i],
               step(lat, dlat, NLAT), step(lon, dlon, NLON), batch)
        for i, ((dlat, dlon), at, n) in enumerate(HALO_SENDS)
    ]
    copies.append(remote(field.at[pl.ds(13, 3)], rows_top, send.at[6], recv.at[6], step(lat, 1, NLAT), lon, batch))
    copies.append(remote(field.at[pl.ds(0, 3)], rows_bot, send.at[7], recv.at[7], step(lat, -1, NLAT), lon, batch))
    return copies


EDGE_SENDS = (
    ((1, 0), 2, 2, 0), ((-1, 0), 0, 2, 2), ((0, 1), 3, 1, 4), ((0, -1), 1, 1, 5),
    ((1, 1), 3, 1, 6), ((1, -1), 2, 1, 7), ((-1, 1), 1, 1, 8), ((-1, -1), 0, 1, 9),
)


def edge_copies(edges, ring, send, recv):
    lat, lon, batch = place()
    return [
        remote(
            edges.at[pl.ds(seg, n)], ring.at[pl.ds(at, n)], send.at[i], recv.at[i],
            step(lat, dlat, NLAT), step(lon, dlon, NLON), batch,
        )
        for i, ((dlat, dlon), seg, n, at) in enumerate(EDGE_SENDS)
    ]


def greet_all():
    lat, lon, batch = place()
    for k in range(1, NLAT):
        signal(step(lat, k, NLAT), lon, batch)
    for k in (1, -1):
        signal(lat, step(lon, k, NLON), batch)
    for dlat, dlon in NEIGHBOURS[4:]:
        signal(step(lat, dlat, NLAT), step(lon, dlon, NLON), batch)
    for k in range(1, 8):
        signal(lat, step(lon, 2 * k, NLON), batch)
    signal(lat, lon, 1 - batch)
    signal(lat, lon + 2 - 4 * lax.rem(lon // 2, 2), 1 - batch)
    return 22


class Gather:
    PAIRS = (0, 1, 3, 2)
    FAR_FIRST = (3, 5, 1, 7, 4, 2, 6)
    NEAR_FIRST = (0, 2, 6, 4, 1, 7, 3, 5)

    def __init__(self, slot, cells, send1, recv1, send2, recv2, send3, recv3):
        lat, lon, batch = place()
        self.q, self.core, self.cells, self.lat = lon // 2, lax.rem(lon, 2), cells, lat
        other = lon + 1 - 2 * self.core
        here = cells.at[self.q, self.core]
        self.own = pltpu.make_async_copy(slot, here.at[lat], recv1.at[lat])
        self.first = [
            remote(slot, here.at[lat], send1.at[k - 1], recv1.at[lat], step(lat, k, NLAT), lon, batch)
            for k in range(1, NLAT)
        ]
        self.arrived = lambda l: pltpu.make_async_copy(slot, here.at[l], recv1.at[l])
        self.second, self.third = {}, {}
        for j, off in enumerate(self.PAIRS):
            pair = pl.ds(2 * lax.rem(lat // 2 + off, 4), 2)
            for k in range(1, 8):
                self.second[k, j] = remote(
                    here.at[pair], here.at[pair], send2.at[k - 1, j], recv2.at[k - 1, j],
                    lat, step(lon, 2 * k, NLON), batch,
                )
        for k in range(8):
            block = cells.at[lax.rem(self.q + 8 - k, 8), self.core]
            self.third[k] = remote(block, block, send3.at[k], recv3.at[k], lat, other, batch)

    def begin(self):
        for k in (4, 3, 5, 2, 6, 1, 7):
            self.first[k - 1].start()
        self.own.start()

    def advance(self, j):
        pair = lax.rem(self.lat // 2 + self.PAIRS[j], 4)
        for i in range(2):
            self.arrived(2 * pair + i).wait()
        for k in self.FAR_FIRST:
            self.second[k, j].start()
        if j == 3:
            self.third[0].start()

    def end(self, table, total):
        for i, k in enumerate(self.NEAR_FIRST):
            if i + 1 < 8:
                ahead = self.NEAR_FIRST[i + 1]
                for j in range(4):
                    self.second[ahead, j].wait_recv()
                self.third[ahead].start()
            self.third[k].wait_recv()
            at = lax.rem(self.q + 8 - k, 8)
            part = dot(table[at], self.cells[at].reshape(256, C))
            if i == 0:
                total[...] = part
            else:
                total[...] += part

    def close(self):
        for copy in [*self.first, *self.second.values(), *self.third.values()]:
            copy.wait_send()


HALF = 1152


PIECE = 384


class Reduce:
    def __init__(self, x_rows, out, got1, total1, acc1, got2x, got2y, acc2x, acc2y, got3x, got3y, blocks, got4, sems):
        s1, r1, s2, r2, s3, r3, s4, r4 = sems
        self.out, self.got1, self.total1, self.acc1 = out, got1, total1, acc1
        self.blocks, self.got4 = blocks, got4
        lat, lon, batch = place()
        self.lat, self.core = lat, lax.rem(lon, 2)
        self.x = lon // 4
        self.y = lax.rem(lon // 2, 2) * 2 + batch
        core, x, y = self.core, self.x, self.y
        self.one = []
        for i, at in enumerate(range(0, out.shape[0], PIECE)):
            part = pl.ds(at, min(PIECE, out.shape[0] - at))
            self.one.append((part, remote(out.at[part], got1.at[part], s1.at[i], r1.at[i], lat, lon + 1 - 2 * core, batch)))

        def peer(along_x, k):
            if along_x:
                return lax.rem(x + k, 4), (lat, step(lon, 4 * k, NLON), batch)
            to = lax.rem(y + k, 4)
            return to, (lat, x * 4 + (to // 2) * 2 + core, lax.rem(to, 2))

        self.ways = []
        for way, (rows, got2, acc2, got3) in enumerate((
            (pl.ds(0, x_rows), got2x, acc2x, got3x), (pl.ds(x_rows, 80 - x_rows), got2y, acc2y, got3y)
        )):
            two, three = [], []
            for k in (2, 1, 3):
                to, device = peer(way == 0, k)
                src = acc1.at[:, to, rows] if way == 0 else acc1.at[to, :, rows]
                two.append(remote(src, got2.at[k - 1], s2.at[way, k - 1], r2.at[way, k - 1], *device))
                to, device = peer(way == 1, k)
                three.append(remote(acc2.at[to], got3.at[k - 1], s3.at[way, k - 1], r3.at[way, k - 1], *device))
            self.ways.append((rows, got2, acc2, got3, two, three))
        self.is_own = lat // 4 == core
        self.e_own = lax.rem(lat, 4) * 2 + core
        self.four = [
            remote(blocks.at[e], got4.at[lat], s4.at[e], r4.at[lat], core * 4 + e // 2, lon - core + e % 2, batch)
            for e in range(8)
        ]
        self.arrive = [remote(blocks.at[0], got4.at[h], s4.at[0], r4.at[h], lat, lon + 1 - 2 * core, batch) for h in range(8)]

    def halves(self, windows, grad):
        n = grad.shape[0]
        height = n // windows.shape[1]

        def piece(i):
            tap, side = i // 2, lax.rem(i, 2)
            cols = pl.ds(pl.multiple_of(side * PIECE, 128), PIECE)
            return dot_rows(windows[pl.ds(tap, height), :, cols].reshape(n, PIECE), grad)

        for i in range(3):
            self.out[PIECE * i : PIECE * i + PIECE, :] = piece(i + 3 - 3 * self.core).astype(BF16)
            self.one[i][1].start()
        for i in range(3):
            self.total1[PIECE * i : PIECE * i + PIECE, :] = piece(i + 3 * self.core)

    def first_axis(self):
        total1, acc1 = self.total1, self.acc1
        for part, copy in self.one:
            copy.wait_recv()
            total1[part, :] += self.got1[part, :].astype(F32)
        for x in range(4):
            for y in range(4):
                pieces = []
                for e in range(8):
                    w = x * 8 + (y // 2) * 4 + (e % 2) * 2 + y % 2
                    at = 288 * (e // 2) + 9 * w
                    pieces.append(total1[at : at + 9])
                for e in range(8):
                    w = x * 8 + (y // 2) * 4 + (e % 2) * 2 + y % 2
                    at = HALF + 32 * (e // 2) + w
                    pieces.append(total1[at : at + 1] if total1.shape[0] > HALF else jnp.zeros((1, C), F32))
                acc1[y, x] = jnp.concatenate(pieces, axis=0).astype(BF16)
        for i in range(3):
            for way in range(2):
                self.ways[way][4][i].start()

    def second_axis(self):
        for way, (rows, got2, acc2, _, two, three) in enumerate(self.ways):
            for copy in two:
                copy.wait_recv()
            for i in range(4):
                mine = self.acc1[i, self.x, rows] if way == 0 else self.acc1[self.y, i, rows]
                acc2[i] = (
                    mine.astype(F32) + got2[0, i].astype(F32) + got2[1, i].astype(F32) + got2[2, i].astype(F32)
                ).astype(BF16)
            for copy in three:
                copy.start()

    def to_owners(self):
        blocks, got4 = self.blocks, self.got4
        totals = []
        for way, (_, _, acc2, got3, _, three) in enumerate(self.ways):
            for copy in three:
                copy.wait_recv()
            mine = acc2[self.y if way == 0 else self.x]
            totals.append(mine.astype(F32) + got3[0].astype(F32) + got3[1].astype(F32) + got3[2].astype(F32))
        total = jnp.concatenate(totals, axis=0)
        for e in range(8):
            rows = [total[9 * e : 9 * e + 9], total[72 + e : 73 + e], jnp.zeros((6, C), F32)]
            blocks[e] = jnp.concatenate(rows, axis=0).astype(BF16)
        for e in range(8):
            mine = self.is_own & (self.e_own == e)

            @pl.when(jnp.logical_not(mine))
            def _():
                self.four[e].start()

            @pl.when(mine)
            def _():
                got4[self.lat] = blocks[e]

    def finish(self):
        got4 = self.got4
        total = None
        for h in range(8):

            @pl.when(jnp.logical_not(self.is_own & (self.lat == h)))
            def _():
                self.arrive[h].wait_recv()

        for h in range(8):
            total = got4[h].astype(F32) if h == 0 else total + got4[h].astype(F32)
        for e in range(8):

            @pl.when(jnp.logical_not(self.is_own & (self.e_own == e)))
            def _():
                self.four[e].wait_send()

        for copy in [c for _, c in self.one] + [c for way in self.ways for c in way[4] + way[5]]:
            copy.wait_send()
        return total


INPUTS = (
    "field", "hpick", "cot", "dec", "sum8", "hplace", "k0", "pool2", "k1", "pool4", "pick", "gain", "table", "synth", "mixing", "place",
    "up4", "up2", "up8",
)


def kernel(scales, n_in, *refs):
    src = dict(zip(INPUTS, refs[:n_in]))
    out_pred, out0, out1, outm, outg = refs[n_in : n_in + 5]
    names = list(INPUTS)
    v = dict(zip(names, refs[n_in + 5 :]))
    (
        load_sem, packed, halo_in, rows_top, rows_bot, fs, x3, x3c, l0f, c1s, x13, level0, da0, level1, a1, p1, slot, gl2, edges, ring, halo_s, halo_r,
        edge_s, edge_r, cells1, cells2, g1sem, g2sem, sc, coef, slot2, spec_own, level2, pred, pred_sem,
        g1s, slope, xg, gp0, mixes, red0, red1, gain_in, gain_got, gain_s, gain_r,
    ) = refs[n_in + 5 + len(names) :]
    cot, k0, k1, gain, table, mixing = (v[n] for n in ("cot", "k0", "k1", "gain", "table", "mixing"))
    field = v["field"]
    lat, lon, batch = place()
    mode_owner = lat * NLON + lon
    base = pl.multiple_of(8 * (mode_owner // 2), 8)

    n_peers = greet_all()
    loads = {}
    for i, n in enumerate(names):
        ref = src[n].at[mode_owner] if n == "synth" else src[n]
        loads[n] = pltpu.make_async_copy(ref, v[n], load_sem.at[i])
    early = ("field", "hpick", "cot", "dec", "sum8")
    for n in early:
        loads[n].start()
    loads["field"].wait()
    loads["hpick"].wait()
    packed[...] = dot(v["hpick"][...], field[...].reshape(768, C)).astype(BF16)
    pl.semaphore_wait(pltpu.get_barrier_semaphore(), n_peers)
    halo = halo_copies(field, rows_top, rows_bot, packed, halo_in, halo_s, halo_r)
    for copy in halo:
        copy.start()
    for n in names:
        if n not in early:
            loads[n].start()

    for n in ("cot", "dec", "sum8"):
        loads[n].wait()
    for half in range(2):
        part = cot[8 * half : 8 * half + 8].reshape(384, C)
        a1[4 * half : 4 * half + 4] = dot(v["dec"][...], part).reshape(4, 32, C)
        gl2[8 * half : 8 * half + 8] = dot(v["sum8"][...], part)
    c1s[...] = jnp.zeros_like(c1s)
    g1s[...] = jnp.zeros_like(g1s)
    fs[3:19, 16:64] = field[...].astype(F32)
    for n in ("hplace", "k0", "pool2", "k1", "pool4", "pick"):
        loads[n].wait()
    for copy in halo:
        copy.wait()

    edge_top = lat == 0
    edge_bot = lat == NLAT - 1
    fs[0:3, 16:64] = jnp.where(edge_top, 0.0, rows_top[...].astype(F32))
    fs[19:22, 16:64] = jnp.where(edge_bot, 0.0, rows_bot[...].astype(F32))
    sides = dot(v["hplace"][...], halo_in[...]).reshape(22, 32, C)
    for half, at in ((0, 0), (16, 64)):
        fs[0:3, at : at + 16] = jnp.where(edge_top, 0.0, sides[0:3, half : half + 16])
        fs[3:19, at : at + 16] = sides[3:19, half : half + 16]
        fs[19:22, at : at + 16] = jnp.where(edge_bot, 0.0, sides[19:22, half : half + 16])
    for b in range(3):
        x3[:, :, b * C : (b + 1) * C] = fs[:, 7 + b : 71 + b, :].astype(BF16)

    def rows4(i, _):
        y = 4 * i
        acc = dot(x3[pl.ds(y, 4)].reshape(256, 3 * C), k0[0])
        acc += dot(x3[pl.ds(y + 1, 4)].reshape(256, 3 * C), k0[1])
        acc += dot(x3[pl.ds(y + 2, 4)].reshape(256, 3 * C), k0[2])
        act, grad = gelu_both(acc)
        out = fs[pl.ds(y + 1, 4), 8:72, :] + act.reshape(4, 64, C)
        l0f[pl.ds(y, 4)] = out.astype(BF16)
        level0[pl.ds(y, 4)] = out[:, 8:56].astype(BF16)
        da0[pl.ds(y, 4)] = grad.reshape(4, 64, C)[:, 8:56].astype(BF16)
        return 0

    lax.fori_loop(0, 5, rows4, 0)

    for y in range(10):
        row = dot(v["pool2"][...], l0f[2 * y : 2 * y + 2].reshape(128, C)).astype(BF16).astype(F32)
        if y == 0:
            row = jnp.where(edge_top, 0.0, row)
        if y == 9:
            row = jnp.where(edge_bot, 0.0, row)
        c1s[y, 8:40, :] = row
    for b in range(3):
        x13[:, :, b * C : (b + 1) * C] = c1s[:, 7 + b : 39 + b, :].astype(BF16)
    pre = dot(x13[0:8].reshape(256, 3 * C), k1[0])
    pre += dot(x13[1:9].reshape(256, 3 * C), k1[1])
    pre += dot(x13[2:10].reshape(256, 3 * C), k1[2])
    act, _ = gelu_both(pre)
    col = lax.broadcasted_iota(jnp.int32, (8, 32, C), 1)
    mine = (col >= 4) & (col < 28)
    p1[...] = jnp.where(mine, pre.reshape(8, 32, C), 0.0)
    lev1 = jnp.where(mine, c1s[1:9, 8:40, :] + act.reshape(8, 32, C), 0.0).astype(BF16)
    level1[...] = lev1
    for half in range(2):
        slot[8 * half : 8 * half + 8] = dot(v["pool4"][...], lev1[4 * half : 4 * half + 4].reshape(128, C)).astype(BF16)

    gather = Gather(slot, cells1, *g1sem)
    gather.begin()
    edges[:, 0] = dot(v["pick"][...], a1[...].reshape(256, C).astype(BF16)).astype(BF16).reshape(4, 16, C)
    edges[:, 1] = dot(v["pick"][...], p1[...].reshape(256, C).astype(BF16)).astype(BF16).reshape(4, 16, C)
    edge = edge_copies(edges, ring, edge_s, edge_r)
    for copy in edge:
        copy.start()
    for n in ("gain", "table", "synth", "mixing", "place", "up4", "up2", "up8"):
        loads[n].wait()
    for b in range(3):
        gather.advance(b)
        x3c[:, :, b * C : (b + 1) * C] = fs[2:20, 15 + b : 63 + b, :].astype(BF16)
    gather.advance(3)
    for copy in edge:
        copy.wait()
    g1s[:, 8:40, :] = dot(v["place"][...], ring[:, 0].reshape(160, C)).reshape(10, 32, C)
    g1s[1:9, 8:40, :] += a1[...]
    slope[...] = dot(v["place"][...], ring[:, 1].reshape(160, C)).reshape(10, 32, C)
    slope[1:9] += p1[...]
    _, grad1 = gelu_both(slope[...])
    slope[...] = grad1
    gather.end(table, sc)
    first_gather = gather

    gr, gi = gain[:, :C], gain[:, C:]
    sr, si = sc[0:512], sc[512:1024]
    coef[0:512] = (gr * sr - gi * si).astype(BF16)
    coef[512:1024] = (gr * si + gi * sr).astype(BF16)
    filt = dot(v["synth"][8:24], coef[...]).astype(BF16)
    mixed = dot(filt, mixing[...])
    act, grad = gelu_both(mixed)
    cell = lax.rem(lax.broadcasted_iota(jnp.int32, (16, C), 0), 8)
    gm = jnp.where((cell >= 1) & (cell < 7), gl2[...] * grad, 0.0).astype(BF16)
    slot2[...] = dot_cols(gm, mixing[...]).astype(BF16)

    sum1 = Reduce(32, *red1[:12], red1[12:])
    sum0 = Reduce(48, *red0[:12], red0[12:])

    gather = Gather(slot2, cells2, *g2sem)
    gather.begin()
    level2[...] = (slot[...].astype(F32) + act).astype(BF16)
    mix = dot_rows(filt, gm)
    mixes[...] = mix
    sum1.out[HALF : HALF + 128, :] = mixes[pl.ds(pl.multiple_of(128 - 128 * sum1.core, 128), 128), :].astype(BF16)
    sum1.total1[HALF : HALF + 128, :] = mixes[pl.ds(pl.multiple_of(128 * sum1.core, 128), 128), :]
    spec_own[:, :C] = sc[pl.ds(base, 8), :]
    spec_own[:, C:] = sc[pl.ds(512 + base, 8), :]

    def predict(r):
        low = dot(v["up2"][...], level1[r]) + dot(v["up8"][...], level2[8 * (r // 4) : 8 * (r // 4) + 8])
        high = level0[2 * r + 2 : 2 * r + 4].astype(F32) + low.reshape(2, 48, C)
        pred[2 * r : 2 * r + 2] = high.astype(BF16)

    for j in range(4):
        gather.advance(j)
        predict(2 * j)
        predict(2 * j + 1)
    pred_out = pltpu.make_async_copy(pred, out_pred, pred_sem)
    pred_out.start()
    gather.end(table, sc)

    er, ei = sc[0:512], sc[512:1024]
    coef[0:512] = (gr * er + gi * ei).astype(BF16)
    coef[512:1024] = (gr * ei - gi * er).astype(BF16)
    back = dot(v["synth"][...], coef[...]).astype(BF16)
    gl1 = g1s[:, 8:40, :] + dot(v["up4"][...], back).reshape(10, 32, C)
    col = lax.broadcasted_iota(jnp.int32, (10, 32, C), 1)
    row = lax.broadcasted_iota(jnp.int32, (10, 32, C), 0)
    first = jnp.where(edge_top, 1, 0)
    last = jnp.where(edge_bot, 9, 10)
    valid = (col >= 3) & (col < 29) & (row >= first) & (row < last)
    gp1 = jnp.where(valid, gl1 * slope[...], 0.0)
    g1s[:, 8:40, :] = gp1
    gown = jnp.where((col[1:9] >= 4) & (col[1:9] < 28), gp1[1:9], 0.0).astype(BF16).reshape(256, C)
    sum1.halves(x13, gown)
    sum1.one[3][1].start()

    gc1 = gl1[1:9].reshape(256, C)
    for b in range(3):
        xg[...] = g1s[:, 7 + b : 39 + b, :].astype(BF16)
        for a in range(3):
            gc1 += dot_cols(xg[a : a + 8].reshape(256, C), k1[2 - a, (2 - b) * C : (3 - b) * C, :])
    high = gc1.astype(BF16)
    low = (gc1 - high.astype(F32)).astype(BF16)
    for r in range(8):
        up = dot(v["up2"][...], high[32 * r : 32 * r + 32]) + dot(v["up2"][...], low[32 * r : 32 * r + 32])
        gl0 = cot[2 * r : 2 * r + 2].astype(F32) + 0.25 * up.reshape(2, 48, C)
        gp0[2 * r : 2 * r + 2] = (gl0 * da0[2 * r + 2 : 2 * r + 4].astype(F32)).astype(BF16)
    sum1.first_axis()
    sum0.halves(x3c, gp0[...].reshape(768, C))

    br, bi = sc[pl.ds(base, 8), :], sc[pl.ds(512 + base, 8), :]
    m = lax.rem(base + lax.broadcasted_iota(jnp.int32, (8, C), 0), 32)
    weight = jnp.where(m == 0, 1.0, 2.0)
    ar, ai = spec_own[:, :C], spec_own[:, C:]
    gain_in[:, :C] = weight * (ar * br + ai * bi)
    gain_in[:, C:] = weight * (ar * bi - ai * br)
    swap = remote(gain_in, gain_got, gain_s, gain_r, lat, lon, 1 - batch)
    swap.start()

    sum0.first_axis()
    sum1.second_axis()
    swap.wait()
    gain_in[...] = gain_in[...] + gain_got[...]
    for batch_at in range(2):
        for lon_at in range(2):

            @pl.when((batch == batch_at) & (lax.rem(lon, 2) == lon_at))
            def _():
                at = 4 * lon_at + 2 * batch_at
                for i in range(2):
                    for j in range(4):
                        outg[4 * i + j : 4 * i + j + 1, :] = gain_in[at + i : at + i + 1, 128 * j : 128 * j + 128]

    sum1.to_owners()
    sum0.second_axis()
    sum0.to_owners()
    t1 = sum1.finish()
    for r in range(9):
        for j in range(2):
            out1[2 * r + j : 2 * r + j + 1, :] = scales[1] * t1[r : r + 1, 128 * j : 128 * j + 128]
    for j in range(2):
        outm[j : j + 1, :] = scales[2] * t1[9:10, 128 * j : 128 * j + 128]
    t0 = sum0.finish()
    for r in range(9):
        for j in range(2):
            out0[2 * r + j : 2 * r + j + 1, :] = scales[0] * t0[r : r + 1, 128 * j : 128 * j + 128]
    first_gather.close()
    gather.close()
    pred_out.wait()


def dma(*n):
    return pltpu.SemaphoreType.DMA(n)


def vmem(*shape, dtype=BF16):
    return pltpu.VMEM(shape, dtype)


def reduce_scratch(rows, x_rows):
    y_rows = 80 - x_rows
    return (
        vmem(rows, C), vmem(rows, C), vmem(rows, C, dtype=F32), vmem(4, 4, 80, C),
        vmem(3, 4, x_rows, C), vmem(3, 4, y_rows, C), vmem(4, x_rows, C), vmem(4, y_rows, C),
        vmem(3, x_rows, C), vmem(3, y_rows, C), vmem(8, 16, C), vmem(8, 16, C),
        dma(4), dma(4), dma(2, 3), dma(2, 3), dma(2, 3), dma(2, 3), dma(8), dma(8),
    )


def hand_over(*arrays):
    n = len(arrays)

    def body(*refs):
        src, dst, buf, (come, go) = refs[:n], refs[n : 2 * n], refs[2 * n : 3 * n], refs[3 * n :]
        inward = [pltpu.make_async_copy(src[i], buf[i], come.at[i]) for i in range(n)]
        outward = [pltpu.make_async_copy(buf[i], dst[i], go.at[i]) for i in range(n)]
        for copy in inward:
            copy.start()
        for i in range(n):
            inward[i].wait()
            outward[i].start()
        for copy in outward:
            copy.wait()

    anywhere = pl.BlockSpec(memory_space=pl.ANY)
    return pl.pallas_call(
        body, out_shape=[jax.ShapeDtypeStruct(a.shape, a.dtype) for a in arrays], in_specs=[anywhere] * n,
        out_specs=[anywhere] * n, scratch_shapes=[vmem(*a.shape, dtype=a.dtype) for a in arrays] + [dma(n), dma(n)],
    )(*arrays)


def on_device(tables, field, kernel0, kernel1, mixing, gain, cotangent):
    table, synth, small = tables
    args = {k: jnp.asarray(a) for k, a in small.items()}
    args |= dict(
        field=field[0], cot=cotangent[0], k0=kernel0.reshape(3, 3 * C, C), k1=kernel1.reshape(3, 3 * C, C),
        mixing=mixing, gain=gain, table=jnp.asarray(table), synth=jnp.asarray(synth),
    )
    cells0 = 2 * 128 * 768
    scales = (1.0 / math.sqrt(cells0), 1.0 / math.sqrt(cells0 // 4), 1.0 / math.sqrt(cells0 // 64))
    names = INPUTS
    gathers = (dma(7), dma(8), dma(7, 4), dma(7, 4), dma(8), dma(8))
    scratch = [vmem(32, 1024) if n == "synth" else vmem(*args[n].shape, dtype=args[n].dtype) for n in names]
    scratch += [
        dma(len(names)), vmem(160, C), vmem(160, C), vmem(3, 48, C), vmem(3, 48, C), vmem(22, 80, C, dtype=F32), vmem(22, 64, 3 * C), vmem(18, 48, 3 * C),
        vmem(20, 64, C), vmem(10, 48, C, dtype=F32), vmem(10, 32, 3 * C), vmem(20, 48, C), vmem(20, 48, C),
        vmem(8, 32, C), vmem(8, 32, C, dtype=F32), vmem(8, 32, C, dtype=F32), vmem(16, C), vmem(16, C, dtype=F32),
        vmem(4, 2, 16, C), vmem(10, 2, 16, C), dma(8), dma(8), dma(8), dma(8),
        vmem(8, 2, 8, 16, C), vmem(8, 2, 8, 16, C), gathers, gathers, vmem(1024, C, dtype=F32), vmem(1024, C),
        vmem(16, C), vmem(8, 2 * C, dtype=F32), vmem(16, C), vmem(ROWS, COLS, C), dma(),
        vmem(10, 48, C, dtype=F32), vmem(10, 32, C, dtype=F32), vmem(10, 32, C), vmem(16, 48, C),
        vmem(C, C, dtype=F32), reduce_scratch(HALF, 48), reduce_scratch(HALF + 128, 32), vmem(8, 2 * C, dtype=F32), vmem(8, 2 * C, dtype=F32), dma(), dma(),
    ]
    anywhere = pl.BlockSpec(memory_space=pl.ANY)
    here = pl.BlockSpec(memory_space=pltpu.VMEM)
    predicted, grad0, grad1, gradm, gradg = pl.pallas_call(
        functools.partial(kernel, scales, len(INPUTS)),
        out_shape=[jax.ShapeDtypeStruct((ROWS, COLS, C), BF16)]
        + [jax.ShapeDtypeStruct((n, 128), F32) for n in (18, 18, 2, 8)],
        in_specs=[anywhere] * len(INPUTS),
        out_specs=[anywhere] + [here] * 4,
        scratch_shapes=scratch,
        compiler_params=pltpu.CompilerParams(collective_id=0, has_side_effects=True, vmem_limit_bytes=VMEM_BYTES),
    )(*[args[n] for n in INPUTS])
    predicted, grad0, grad1, gradm, gradg = hand_over(predicted, grad0, grad1, gradm, gradg)
    return predicted[None], grad0.reshape(-1), grad1.reshape(-1), gradm.reshape(-1), gradg.reshape(-1)


def solution(mesh):
    tables = (*spectral_tables(), cell_tables())
    tile = P("batch", "lat", "lon", None)
    split = P(("lat", "lon", "batch"))
    return jax.shard_map(
        functools.partial(on_device, tables), mesh=mesh, in_specs=(tile, P(), P(), P(), P(), tile),
        out_specs=(tile, split, split, split, split), check_vma=False,
    )
```

```python
import functools
import math

import jax
import jax.numpy as jnp
import ml_dtypes
import numpy as np
from jax import lax
from jax.experimental import pallas as pl
from jax.experimental.pallas import tpu as pltpu
from jax.sharding import PartitionSpec as P

MESH = pl.DeviceIdType.MESH
F32 = jnp.float32
BF16 = jnp.bfloat16
C = 256
NLAT, NLON = 8, 16
ROWS, COLS = 16, 48
VMEM_BYTES = 56 * 2**20


def spectral_tables():
    lat_n, lon_n, kl, km = 16, 96, 16, 32
    freq = np.repeat(np.arange(kl) - kl // 2, km)
    mode = np.tile(np.arange(km), kl)
    norm = 1.0 / math.sqrt(lat_n * lon_n)

    def phase(i, j):
        whole = (freq[:, None] * i[None] * lon_n + mode[:, None] * j[None] * lat_n) % (lat_n * lon_n)
        return 2.0 * np.pi * whole / (lat_n * lon_n)

    forward = np.zeros((2, kl * km, NLON, NLAT, 2, 8))
    for lon in range(NLON):
        for lat in range(NLAT):
            for r in range(2):
                j = lon * 6 + np.arange(6)
                ph = phase(np.full(6, lat * 2 + r), j)
                forward[0, :, lon, lat, r, 1:7] = np.cos(ph) * norm
                forward[1, :, lon, lat, r, 1:7] = -np.sin(ph) * norm
    forward = forward.reshape(2 * kl * km, NLON * NLAT * 16)
    weight = np.where(mode == 0, 1.0, 2.0) * norm
    back = np.zeros((NLAT * NLON, 32, 2, kl * km))
    for lat in range(NLAT):
        for lon in range(NLON):
            i = np.repeat(lat * 2 + np.array([0, 1, -1, 2]), 8)
            j = np.tile(lon * 6 - 1 + np.arange(8), 4)
            ph = phase(i, j).T
            back[lat * NLON + lon, :, 0] = np.cos(ph) * weight
            back[lat * NLON + lon, :, 1] = -np.sin(ph) * weight
    back = back.reshape(NLAT, NLON, 32, 2 * kl * km)
    forward = forward.reshape(2 * kl * km, NLON, NLAT * 16).transpose(1, 0, 2)
    return forward.astype(ml_dtypes.bfloat16), back.astype(ml_dtypes.bfloat16)


def cell_tables():
    pool2 = np.zeros((32, 2, 64))
    for j in range(32):
        pool2[j, :, 2 * j : 2 * j + 2] = 0.25
    pool4 = np.zeros((8, 4, 32))
    for j in range(1, 7):
        pool4[j, :, 4 * j : 4 * j + 4] = 1 / 16
    dec = np.zeros((4, 32, 8, 48))
    for r in range(4):
        for j in range(24):
            dec[r, 4 + j, :, 8 * (j // 4) : 8 * (j // 4) + 8] += 1 / 16
            dec[r, 4 + j, 2 * r : 2 * r + 2, 2 * j : 2 * j + 2] += 1
    sum8 = np.zeros((8, 8, 48))
    for j in range(6):
        sum8[1 + j, :, 8 * j : 8 * j + 8] = 1
    pick = np.zeros((64, 8, 32))
    for half, row, col in ((0, 0, 4), (32, 7, 27)):
        for i in range(24):
            pick[half + i, row, 4 + i] = 1
        for r in range(8):
            pick[half + 24 + r, r, col] = 1
    place = np.zeros((10, 32, 10, 16))
    for j in range(24):
        place[0, 4 + j, j // 16, j % 16] = 1
        place[9, 4 + j, 2 + j // 16, j % 16] = 1
    for r in range(8):
        place[1 + r, 3, 4, 8 + r] = 1
        place[1 + r, 28, 5, 8 + r] = 1
    place[0, 3, 6, 7] = 1
    place[0, 28, 7, 0] = 1
    place[9, 3, 8, 7] = 1
    place[9, 28, 9, 0] = 1
    up4 = np.zeros((10, 32, 4, 8))
    for r in range(10):
        for j in range(32):
            up4[r, j, (2, 0, 1, 3)[(r + 3) // 4], j // 4] = 1 / 16
    up2 = np.zeros((2, 48, 32))
    up8 = np.zeros((2, 48, 8))
    for j in range(48):
        up2[:, j, 4 + j // 2] = 1
        up8[:, j, 1 + j // 8] = 1
    hpick = np.zeros((160, 16, 48))
    hplace = np.zeros((22, 32, 160))
    for j in range(3):
        for r in range(16):
            hpick[3 * r + j, r, j] = 1
            hpick[48 + 3 * r + j, r, 45 + j] = 1
            hplace[3 + r, 16 + j, 3 * r + j] = 1
            hplace[3 + r, 13 + j, 48 + 3 * r + j] = 1
        for i in range(3):
            for seg, row, col, to_row, to_col in (
                (96, 0, 0, 19, 16), (112, 0, 45, 19, 13), (128, 13, 0, 0, 16), (144, 13, 45, 0, 13)
            ):
                hpick[seg + 3 * i + j, row + i, col + j] = 1
                hplace[to_row + i, to_col + j, seg + 3 * i + j] = 1
    shapes = dict(
        hpick=(hpick, (160, 768)), hplace=(hplace, (704, 160)),
        pool2=(pool2, (32, 128)), pool4=(pool4, (8, 128)), dec=(dec, (128, 384)), sum8=(sum8, (8, 384)),
        pick=(pick, (64, 256)), place=(place, (320, 160)), up4=(up4, (320, 32)), up2=(up2, (96, 32)),
        up8=(up8, (96, 8)),
    )
    return {k: v.reshape(s).astype(ml_dtypes.bfloat16) for k, (v, s) in shapes.items()}


def dot(a, b):
    return jnp.dot(a, b, preferred_element_type=F32)


def dot_rows(a, b):
    return lax.dot_general(a, b, (((0,), (0,)), ((), ())), preferred_element_type=F32)


def dot_cols(a, b):
    return lax.dot_general(a, b, (((1,), (1,)), ((), ())), preferred_element_type=F32)


def gelu_both(v):
    k, q = 0.7978845608028654, 0.044715
    sq = v * v
    t = jnp.tanh(k * (v * (1.0 + q * sq)))
    half = 0.5 * (1.0 + t)
    return v * half, half + (0.5 * v) * (1.0 - t * t) * (k * (1.0 + (3.0 * q) * sq))


def place():
    return lax.axis_index("lat"), lax.axis_index("lon"), lax.axis_index("batch")


def step(pos, by, n):
    return lax.rem(pos + (by + n), n)


def signal(lat, lon, batch):
    pl.semaphore_signal(
        pltpu.get_barrier_semaphore(), inc=1, device_id={"lat": lat, "lon": lon, "batch": batch}, device_id_type=MESH
    )


def remote(src, dst, send, recv, lat, lon, batch):
    return pltpu.make_async_remote_copy(
        src_ref=src, dst_ref=dst, send_sem=send, recv_sem=recv,
        device_id={"lat": lat, "lon": lon, "batch": batch}, device_id_type=MESH,
    )


NEIGHBOURS = ((1, 0), (-1, 0), (0, 1), (0, -1), (1, 1), (1, -1), (-1, 1), (-1, -1))


HALO_SENDS = (
    ((0, -1), 0, 48), ((0, 1), 48, 48), ((-1, -1), 96, 16), ((-1, 1), 112, 16), ((1, -1), 128, 16), ((1, 1), 144, 16),
)


def halo_copies(field, rows_top, rows_bot, packed, halo, send, recv):
    lat, lon, batch = place()
    copies = [
        remote(packed.at[pl.ds(at, n)], halo.at[pl.ds(at, n)], send.at[i], recv.at[i],
               step(lat, dlat, NLAT), step(lon, dlon, NLON), batch)
        for i, ((dlat, dlon), at, n) in enumerate(HALO_SENDS)
    ]
    copies.append(remote(field.at[pl.ds(13, 3)], rows_top, send.at[6], recv.at[6], step(lat, 1, NLAT), lon, batch))
    copies.append(remote(field.at[pl.ds(0, 3)], rows_bot, send.at[7], recv.at[7], step(lat, -1, NLAT), lon, batch))
    return copies


EDGE_SENDS = (
    ((1, 0), 2, 2, 0), ((-1, 0), 0, 2, 2), ((0, 1), 3, 1, 4), ((0, -1), 1, 1, 5),
    ((1, 1), 3, 1, 6), ((1, -1), 2, 1, 7), ((-1, 1), 1, 1, 8), ((-1, -1), 0, 1, 9),
)


def edge_copies(edges, ring, send, recv):
    lat, lon, batch = place()
    return [
        remote(
            edges.at[pl.ds(seg, n)], ring.at[pl.ds(at, n)], send.at[i], recv.at[i],
            step(lat, dlat, NLAT), step(lon, dlon, NLON), batch,
        )
        for i, ((dlat, dlon), seg, n, at) in enumerate(EDGE_SENDS)
    ]


def greet_all():
    lat, lon, batch = place()
    for k in range(1, NLAT):
        signal(step(lat, k, NLAT), lon, batch)
    for k in range(1, NLON):
        signal(lat, step(lon, k, NLON), batch)
    for dlat, dlon in NEIGHBOURS[4:]:
        signal(step(lat, dlat, NLAT), step(lon, dlon, NLON), batch)
    signal(lat, lon, 1 - batch)
    signal(lat, lon + 2 - 4 * lax.rem(lon // 2, 2), 1 - batch)
    return 28


class Spectral:
    FAR_FIRST = (10, 6, 9, 7, 11, 5, 8, 12, 4, 3, 13, 2, 14, 1, 15)

    def __init__(self, slot, cells, share, got, modes, got_modes, send1, recv1, send2, recv2, send3, recv3):
        lat, lon, batch = place()
        self.lat, self.lon, self.cells = lat, lon, cells
        self.share, self.got, self.modes, self.got_modes = share, got, modes, got_modes
        self.own = pltpu.make_async_copy(slot, cells.at[lat], recv1.at[lat])
        self.first = [
            remote(slot, cells.at[lat], send1.at[k - 1], recv1.at[lat], step(lat, k, NLAT), lon, batch)
            for k in range(1, NLAT)
        ]
        self.arrived = [pltpu.make_async_copy(slot, cells.at[l], recv1.at[l]) for l in range(NLAT)]
        self.second, self.third = [], []
        for k in self.FAR_FIRST:
            to = step(lon, k, NLON)
            self.second.append(remote(share.at[to], got.at[lon], send2.at[k - 1], recv2.at[k - 1], lat, to, batch))
            self.third.append(remote(modes.at[to], got_modes.at[lon], send3.at[k - 1], recv3.at[k - 1], lat, to, batch))

    def begin(self):
        for k in (4, 3, 5, 2, 6, 1, 7):
            self.first[k - 1].start()
        self.own.start()

    def spread(self, table, gain, sign, synth, sc, coef):
        for copy in self.arrived:
            copy.wait()
        sc[...] = dot(table[...], self.cells[...].reshape(NLAT * 16, C))
        gr, gi = gain[:, :C], gain[:, C:] * sign
        sr, si = sc[0:512], sc[512:1024]
        coef[0:512] = (gr * sr - gi * si).astype(BF16)
        coef[512:1024] = (gr * si + gi * sr).astype(BF16)
        rows = self.share.shape[1]
        weights = synth[:, 0:rows].reshape(NLON * rows, 1024)
        self.share[...] = dot(weights, coef[...]).astype(BF16).reshape(NLON, rows, C)
        for copy in self.second:
            copy.start()
        self.got[self.lon] = self.share[self.lon]
        re = sc[pl.ds(pl.multiple_of(64 * self.lat, 8), 64), :]
        im = sc[pl.ds(pl.multiple_of(512 + 64 * self.lat, 8), 64), :]
        for to in range(NLON):
            self.modes[to] = jnp.concatenate([re[4 * to : 4 * to + 4], im[4 * to : 4 * to + 4]], axis=0)
        for copy in self.third:
            copy.start()
        self.got_modes[self.lon] = self.modes[self.lon]

    def collect(self):
        for copy in self.second:
            copy.wait_recv()
        total = self.got[0].astype(F32)
        for h in range(1, NLON):
            total += self.got[h].astype(F32)
        return total.astype(BF16)

    def collect_modes(self):
        for copy in self.third:
            copy.wait_recv()
        total = self.got_modes[0]
        for h in range(1, NLON):
            total += self.got_modes[h]
        return total

    def close(self):
        for copy in self.first + self.second + self.third:
            copy.wait_send()


HALF = 1152


PIECE = 384


class Reduce:
    def __init__(self, x_rows, out, got1, total1, acc1, got2x, got2y, acc2x, acc2y, got3x, got3y, blocks, got4, sems):
        s1, r1, s2, r2, s3, r3, s4, r4 = sems
        self.out, self.got1, self.total1, self.acc1 = out, got1, total1, acc1
        self.blocks, self.got4 = blocks, got4
        lat, lon, batch = place()
        self.lat, self.core = lat, lax.rem(lon, 2)
        self.x = lon // 4
        self.y = lax.rem(lon // 2, 2) * 2 + batch
        core, x, y = self.core, self.x, self.y
        self.one = []
        for i, at in enumerate(range(0, out.shape[0], PIECE)):
            part = pl.ds(at, min(PIECE, out.shape[0] - at))
            self.one.append((part, remote(out.at[part], got1.at[part], s1.at[i], r1.at[i], lat, lon + 1 - 2 * core, batch)))

        def peer(along_x, k):
            if along_x:
                return lax.rem(x + k, 4), (lat, step(lon, 4 * k, NLON), batch)
            to = lax.rem(y + k, 4)
            return to, (lat, x * 4 + (to // 2) * 2 + core, lax.rem(to, 2))

        self.ways = []
        for way, (rows, got2, acc2, got3) in enumerate((
            (pl.ds(0, x_rows), got2x, acc2x, got3x), (pl.ds(x_rows, 80 - x_rows), got2y, acc2y, got3y)
        )):
            two, three = [], []
            for k in (2, 1, 3):
                to, device = peer(way == 0, k)
                src = acc1.at[:, to, rows] if way == 0 else acc1.at[to, :, rows]
                two.append(remote(src, got2.at[k - 1], s2.at[way, k - 1], r2.at[way, k - 1], *device))
                to, device = peer(way == 1, k)
                three.append(remote(acc2.at[to], got3.at[k - 1], s3.at[way, k - 1], r3.at[way, k - 1], *device))
            self.ways.append((rows, got2, acc2, got3, two, three))
        self.is_own = lat // 4 == core
        self.e_own = lax.rem(lat, 4) * 2 + core
        self.four = [
            remote(blocks.at[e], got4.at[lat], s4.at[e], r4.at[lat], core * 4 + e // 2, lon - core + e % 2, batch)
            for e in range(8)
        ]
        self.arrive = [remote(blocks.at[0], got4.at[h], s4.at[0], r4.at[h], lat, lon + 1 - 2 * core, batch) for h in range(8)]

    def halves(self, windows, grad):
        n = grad.shape[0]
        height = n // windows.shape[1]

        def piece(i):
            tap, side = i // 2, lax.rem(i, 2)
            cols = pl.ds(pl.multiple_of(side * PIECE, 128), PIECE)
            return dot_rows(windows[pl.ds(tap, height), :, cols].reshape(n, PIECE), grad)

        for i in range(3):
            self.out[PIECE * i : PIECE * i + PIECE, :] = piece(i + 3 - 3 * self.core).astype(BF16)
            self.one[i][1].start()
        for i in range(3):
            self.total1[PIECE * i : PIECE * i + PIECE, :] = piece(i + 3 * self.core)

    def first_axis(self):
        total1, acc1 = self.total1, self.acc1
        for part, copy in self.one:
            copy.wait_recv()
            total1[part, :] += self.got1[part, :].astype(F32)
        for x in range(4):
            for y in range(4):
                pieces = []
                for e in range(8):
                    w = x * 8 + (y // 2) * 4 + (e % 2) * 2 + y % 2
                    at = 288 * (e // 2) + 9 * w
                    pieces.append(total1[at : at + 9])
                for e in range(8):
                    w = x * 8 + (y // 2) * 4 + (e % 2) * 2 + y % 2
                    at = HALF + 32 * (e // 2) + w
                    pieces.append(total1[at : at + 1] if total1.shape[0] > HALF else jnp.zeros((1, C), F32))
                acc1[y, x] = jnp.concatenate(pieces, axis=0).astype(BF16)
        for i in range(3):
            for way in range(2):
                self.ways[way][4][i].start()

    def second_axis(self):
        for way, (rows, got2, acc2, _, two, three) in enumerate(self.ways):
            for copy in two:
                copy.wait_recv()
            for i in range(4):
                mine = self.acc1[i, self.x, rows] if way == 0 else self.acc1[self.y, i, rows]
                acc2[i] = (
                    mine.astype(F32) + got2[0, i].astype(F32) + got2[1, i].astype(F32) + got2[2, i].astype(F32)
                ).astype(BF16)
            for copy in three:
                copy.start()

    def to_owners(self):
        blocks, got4 = self.blocks, self.got4
        totals = []
        for way, (_, _, acc2, got3, _, three) in enumerate(self.ways):
            for copy in three:
                copy.wait_recv()
            mine = acc2[self.y if way == 0 else self.x]
            totals.append(mine.astype(F32) + got3[0].astype(F32) + got3[1].astype(F32) + got3[2].astype(F32))
        total = jnp.concatenate(totals, axis=0)
        for e in range(8):
            rows = [total[9 * e : 9 * e + 9], total[72 + e : 73 + e], jnp.zeros((6, C), F32)]
            blocks[e] = jnp.concatenate(rows, axis=0).astype(BF16)
        for e in range(8):
            mine = self.is_own & (self.e_own == e)

            @pl.when(jnp.logical_not(mine))
            def _():
                self.four[e].start()

            @pl.when(mine)
            def _():
                got4[self.lat] = blocks[e]

    def finish(self):
        got4 = self.got4
        total = None
        for h in range(8):

            @pl.when(jnp.logical_not(self.is_own & (self.lat == h)))
            def _():
                self.arrive[h].wait_recv()

        for h in range(8):
            total = got4[h].astype(F32) if h == 0 else total + got4[h].astype(F32)
        for e in range(8):

            @pl.when(jnp.logical_not(self.is_own & (self.e_own == e)))
            def _():
                self.four[e].wait_send()

        for copy in [c for _, c in self.one] + [c for way in self.ways for c in way[4] + way[5]]:
            copy.wait_send()
        return total


INPUTS = (
    "field", "hpick", "cot", "dec", "sum8", "hplace", "k0", "pool2", "k1", "pool4", "pick", "gain", "table", "synth", "mixing", "place",
    "up4", "up2", "up8",
)


def kernel(scales, n_in, *refs):
    src = dict(zip(INPUTS, refs[:n_in]))
    out_pred, out0, out1, outm, outg = refs[n_in : n_in + 5]
    names = list(INPUTS)
    v = dict(zip(names, refs[n_in + 5 :]))
    (
        load_sem, packed, halo_in, rows_top, rows_bot, fs, x3, x3c, l0f, c1s, x13, level0, da0, level1, a1, p1, slot, gl2, edges, ring, halo_s, halo_r,
        edge_s, edge_r, spec1, spec2, sc, coef, slot2, level2, pred, pred_sem,
        g1s, slope, xg, gp0, mixes, red0, red1, gain_in, gain_got, gain_s, gain_r,
    ) = refs[n_in + 5 + len(names) :]
    cot, k0, k1, gain, table, mixing = (v[n] for n in ("cot", "k0", "k1", "gain", "table", "mixing"))
    field = v["field"]
    lat, lon, batch = place()

    n_peers = greet_all()
    loads = {}
    for i, n in enumerate(names):
        ref = src[n].at[dict(synth=lat, table=lon)[n]] if n in ("synth", "table") else src[n]
        loads[n] = pltpu.make_async_copy(ref, v[n], load_sem.at[i])
    early = ("field", "hpick", "cot", "dec", "sum8")
    for n in early:
        loads[n].start()
    loads["field"].wait()
    loads["hpick"].wait()
    packed[...] = dot(v["hpick"][...], field[...].reshape(768, C)).astype(BF16)
    pl.semaphore_wait(pltpu.get_barrier_semaphore(), n_peers)
    halo = halo_copies(field, rows_top, rows_bot, packed, halo_in, halo_s, halo_r)
    for copy in halo:
        copy.start()
    for n in names:
        if n not in early:
            loads[n].start()

    for n in ("cot", "dec", "sum8"):
        loads[n].wait()
    for half in range(2):
        part = cot[8 * half : 8 * half + 8].reshape(384, C)
        a1[4 * half : 4 * half + 4] = dot(v["dec"][...], part).reshape(4, 32, C)
        gl2[8 * half : 8 * half + 8] = dot(v["sum8"][...], part)
    c1s[...] = jnp.zeros_like(c1s)
    g1s[...] = jnp.zeros_like(g1s)
    fs[3:19, 16:64] = field[...].astype(F32)
    for n in ("hplace", "k0", "pool2", "k1", "pool4", "pick"):
        loads[n].wait()
    for copy in halo:
        copy.wait()

    edge_top = lat == 0
    edge_bot = lat == NLAT - 1
    fs[0:3, 16:64] = jnp.where(edge_top, 0.0, rows_top[...].astype(F32))
    fs[19:22, 16:64] = jnp.where(edge_bot, 0.0, rows_bot[...].astype(F32))
    sides = dot(v["hplace"][...], halo_in[...]).reshape(22, 32, C)
    for half, at in ((0, 0), (16, 64)):
        fs[0:3, at : at + 16] = jnp.where(edge_top, 0.0, sides[0:3, half : half + 16])
        fs[3:19, at : at + 16] = sides[3:19, half : half + 16]
        fs[19:22, at : at + 16] = jnp.where(edge_bot, 0.0, sides[19:22, half : half + 16])
    for b in range(3):
        x3[:, :, b * C : (b + 1) * C] = fs[:, 7 + b : 71 + b, :].astype(BF16)

    def rows4(i, _):
        y = 4 * i
        acc = dot(x3[pl.ds(y, 4)].reshape(256, 3 * C), k0[0])
        acc += dot(x3[pl.ds(y + 1, 4)].reshape(256, 3 * C), k0[1])
        acc += dot(x3[pl.ds(y + 2, 4)].reshape(256, 3 * C), k0[2])
        act, grad = gelu_both(acc)
        out = fs[pl.ds(y + 1, 4), 8:72, :] + act.reshape(4, 64, C)
        l0f[pl.ds(y, 4)] = out.astype(BF16)
        level0[pl.ds(y, 4)] = out[:, 8:56].astype(BF16)
        da0[pl.ds(y, 4)] = grad.reshape(4, 64, C)[:, 8:56].astype(BF16)
        return 0

    lax.fori_loop(0, 5, rows4, 0)

    for y in range(10):
        row = dot(v["pool2"][...], l0f[2 * y : 2 * y + 2].reshape(128, C)).astype(BF16).astype(F32)
        if y == 0:
            row = jnp.where(edge_top, 0.0, row)
        if y == 9:
            row = jnp.where(edge_bot, 0.0, row)
        c1s[y, 8:40, :] = row
    for b in range(3):
        x13[:, :, b * C : (b + 1) * C] = c1s[:, 7 + b : 39 + b, :].astype(BF16)
    pre = dot(x13[0:8].reshape(256, 3 * C), k1[0])
    pre += dot(x13[1:9].reshape(256, 3 * C), k1[1])
    pre += dot(x13[2:10].reshape(256, 3 * C), k1[2])
    act, _ = gelu_both(pre)
    col = lax.broadcasted_iota(jnp.int32, (8, 32, C), 1)
    mine = (col >= 4) & (col < 28)
    p1[...] = jnp.where(mine, pre.reshape(8, 32, C), 0.0)
    lev1 = jnp.where(mine, c1s[1:9, 8:40, :] + act.reshape(8, 32, C), 0.0).astype(BF16)
    level1[...] = lev1
    for half in range(2):
        slot[8 * half : 8 * half + 8] = dot(v["pool4"][...], lev1[4 * half : 4 * half + 4].reshape(128, C)).astype(BF16)

    forth = Spectral(slot, *spec1[:5], *spec1[5:])
    forth.begin()
    edges[:, 0] = dot(v["pick"][...], a1[...].reshape(256, C).astype(BF16)).astype(BF16).reshape(4, 16, C)
    edges[:, 1] = dot(v["pick"][...], p1[...].reshape(256, C).astype(BF16)).astype(BF16).reshape(4, 16, C)
    edge = edge_copies(edges, ring, edge_s, edge_r)
    for copy in edge:
        copy.start()
    for n in ("gain", "table", "synth", "mixing", "place", "up4", "up2", "up8"):
        loads[n].wait()
    for b in range(3):
        x3c[:, :, b * C : (b + 1) * C] = fs[2:20, 15 + b : 63 + b, :].astype(BF16)
    forth.spread(table, gain, 1.0, v["synth"], sc, coef)
    for copy in edge:
        copy.wait()
    g1s[:, 8:40, :] = dot(v["place"][...], ring[:, 0].reshape(160, C)).reshape(10, 32, C)
    g1s[1:9, 8:40, :] += a1[...]
    slope[...] = dot(v["place"][...], ring[:, 1].reshape(160, C)).reshape(10, 32, C)
    slope[1:9] += p1[...]
    _, grad1 = gelu_both(slope[...])
    slope[...] = grad1
    filt = forth.collect()
    mixed = dot(filt, mixing[...])
    act, grad = gelu_both(mixed)
    cell = lax.rem(lax.broadcasted_iota(jnp.int32, (16, C), 0), 8)
    gm = jnp.where((cell >= 1) & (cell < 7), gl2[...] * grad, 0.0).astype(BF16)
    slot2[...] = dot_cols(gm, mixing[...]).astype(BF16)

    sum1 = Reduce(32, *red1[:12], red1[12:])
    sum0 = Reduce(48, *red0[:12], red0[12:])

    back_way = Spectral(slot2, *spec2[:5], *spec2[5:])
    back_way.begin()
    level2[...] = (slot[...].astype(F32) + act).astype(BF16)
    mix = dot_rows(filt, gm)
    mixes[...] = mix
    sum1.out[HALF : HALF + 128, :] = mixes[pl.ds(pl.multiple_of(128 - 128 * sum1.core, 128), 128), :].astype(BF16)
    sum1.total1[HALF : HALF + 128, :] = mixes[pl.ds(pl.multiple_of(128 * sum1.core, 128), 128), :]
    spec_own = forth.collect_modes()

    def predict(r):
        low = dot(v["up2"][...], level1[r]) + dot(v["up8"][...], level2[8 * (r // 4) : 8 * (r // 4) + 8])
        high = level0[2 * r + 2 : 2 * r + 4].astype(F32) + low.reshape(2, 48, C)
        pred[2 * r : 2 * r + 2] = high.astype(BF16)

    for r in range(4):
        predict(r)
    back_way.spread(table, gain, -1.0, v["synth"], sc, coef)
    for r in range(4, 8):
        predict(r)
    pred_out = pltpu.make_async_copy(pred, out_pred, pred_sem)
    pred_out.start()

    back = back_way.collect()
    gl1 = g1s[:, 8:40, :] + dot(v["up4"][...], back).reshape(10, 32, C)
    col = lax.broadcasted_iota(jnp.int32, (10, 32, C), 1)
    row = lax.broadcasted_iota(jnp.int32, (10, 32, C), 0)
    first = jnp.where(edge_top, 1, 0)
    last = jnp.where(edge_bot, 9, 10)
    valid = (col >= 3) & (col < 29) & (row >= first) & (row < last)
    gp1 = jnp.where(valid, gl1 * slope[...], 0.0)
    g1s[:, 8:40, :] = gp1
    gown = jnp.where((col[1:9] >= 4) & (col[1:9] < 28), gp1[1:9], 0.0).astype(BF16).reshape(256, C)
    sum1.halves(x13, gown)
    sum1.one[3][1].start()

    gc1 = gl1[1:9].reshape(256, C)
    for b in range(3):
        xg[...] = g1s[:, 7 + b : 39 + b, :].astype(BF16)
        for a in range(3):
            gc1 += dot_cols(xg[a : a + 8].reshape(256, C), k1[2 - a, (2 - b) * C : (3 - b) * C, :])
    high = gc1.astype(BF16)
    low = (gc1 - high.astype(F32)).astype(BF16)
    for r in range(8):
        up = dot(v["up2"][...], high[32 * r : 32 * r + 32]) + dot(v["up2"][...], low[32 * r : 32 * r + 32])
        gl0 = cot[2 * r : 2 * r + 2].astype(F32) + 0.25 * up.reshape(2, 48, C)
        gp0[2 * r : 2 * r + 2] = (gl0 * da0[2 * r + 2 : 2 * r + 4].astype(F32)).astype(BF16)
    sum1.first_axis()
    sum0.halves(x3c, gp0[...].reshape(768, C))

    grads = back_way.collect_modes()
    m = lax.rem(4 * lon + lax.broadcasted_iota(jnp.int32, (4, C), 0), 32)
    weight = jnp.where(m == 0, 1.0, 2.0)
    ar, ai, br, bi = spec_own[0:4], spec_own[4:8], grads[0:4], grads[4:8]
    rest = jnp.zeros((4, C), F32)
    gain_in[:, :C] = jnp.concatenate([weight * (ar * br + ai * bi), rest], axis=0)
    gain_in[:, C:] = jnp.concatenate([weight * (ar * bi - ai * br), rest], axis=0)
    swap = remote(gain_in, gain_got, gain_s, gain_r, lat, lon, 1 - batch)
    swap.start()

    sum0.first_axis()
    sum1.second_axis()
    swap.wait()
    gain_in[...] = gain_in[...] + gain_got[...]
    for batch_at in range(2):

        @pl.when(batch == batch_at)
        def _():
            for i in range(2):
                for j in range(4):
                    row = 2 * batch_at + i
                    outg[4 * i + j : 4 * i + j + 1, :] = gain_in[row : row + 1, 128 * j : 128 * j + 128]

    sum1.to_owners()
    sum0.second_axis()
    sum0.to_owners()
    t1 = sum1.finish()
    for r in range(9):
        for j in range(2):
            out1[2 * r + j : 2 * r + j + 1, :] = scales[1] * t1[r : r + 1, 128 * j : 128 * j + 128]
    for j in range(2):
        outm[j : j + 1, :] = scales[2] * t1[9:10, 128 * j : 128 * j + 128]
    t0 = sum0.finish()
    for r in range(9):
        for j in range(2):
            out0[2 * r + j : 2 * r + j + 1, :] = scales[0] * t0[r : r + 1, 128 * j : 128 * j + 128]
    forth.close()
    back_way.close()
    pred_out.wait()


def dma(*n):
    return pltpu.SemaphoreType.DMA(n)


def vmem(*shape, dtype=BF16):
    return pltpu.VMEM(shape, dtype)


def reduce_scratch(rows, x_rows):
    y_rows = 80 - x_rows
    return (
        vmem(rows, C), vmem(rows, C), vmem(rows, C, dtype=F32), vmem(4, 4, 80, C),
        vmem(3, 4, x_rows, C), vmem(3, 4, y_rows, C), vmem(4, x_rows, C), vmem(4, y_rows, C),
        vmem(3, x_rows, C), vmem(3, y_rows, C), vmem(8, 16, C), vmem(8, 16, C),
        dma(4), dma(4), dma(2, 3), dma(2, 3), dma(2, 3), dma(2, 3), dma(8), dma(8),
    )


def hand_over(*arrays):
    n = len(arrays)

    def body(*refs):
        src, dst, buf, (come, go) = refs[:n], refs[n : 2 * n], refs[2 * n : 3 * n], refs[3 * n :]
        inward = [pltpu.make_async_copy(src[i], buf[i], come.at[i]) for i in range(n)]
        outward = [pltpu.make_async_copy(buf[i], dst[i], go.at[i]) for i in range(n)]
        for copy in inward:
            copy.start()
        for i in range(n):
            inward[i].wait()
            outward[i].start()
        for copy in outward:
            copy.wait()

    anywhere = pl.BlockSpec(memory_space=pl.ANY)
    return pl.pallas_call(
        body, out_shape=[jax.ShapeDtypeStruct(a.shape, a.dtype) for a in arrays], in_specs=[anywhere] * n,
        out_specs=[anywhere] * n, scratch_shapes=[vmem(*a.shape, dtype=a.dtype) for a in arrays] + [dma(n), dma(n)],
    )(*arrays)


def on_device(tables, field, kernel0, kernel1, mixing, gain, cotangent):
    table, synth, small = tables
    args = {k: jnp.asarray(a) for k, a in small.items()}
    args |= dict(
        field=field[0], cot=cotangent[0], k0=kernel0.reshape(3, 3 * C, C), k1=kernel1.reshape(3, 3 * C, C),
        mixing=mixing, gain=gain, table=jnp.asarray(table), synth=jnp.asarray(synth),
    )
    cells0 = 2 * 128 * 768
    scales = (1.0 / math.sqrt(cells0), 1.0 / math.sqrt(cells0 // 4), 1.0 / math.sqrt(cells0 // 64))
    names = INPUTS
    scratch = [
        vmem(*args[n].shape[1:]) if n in ("synth", "table") else vmem(*args[n].shape, dtype=args[n].dtype) for n in names
    ]

    def spectral_scratch(rows):
        sems = (dma(7), dma(8), dma(15), dma(15), dma(15), dma(15))
        modes = vmem(NLON, 8, C, dtype=F32)
        return (vmem(NLAT, 16, C), vmem(NLON, rows, C), vmem(NLON, rows, C), modes, modes, *sems)

    scratch += [
        dma(len(names)), vmem(160, C), vmem(160, C), vmem(3, 48, C), vmem(3, 48, C), vmem(22, 80, C, dtype=F32), vmem(22, 64, 3 * C), vmem(18, 48, 3 * C),
        vmem(20, 64, C), vmem(10, 48, C, dtype=F32), vmem(10, 32, 3 * C), vmem(20, 48, C), vmem(20, 48, C),
        vmem(8, 32, C), vmem(8, 32, C, dtype=F32), vmem(8, 32, C, dtype=F32), vmem(16, C), vmem(16, C, dtype=F32),
        vmem(4, 2, 16, C), vmem(10, 2, 16, C), dma(8), dma(8), dma(8), dma(8),
        spectral_scratch(16), spectral_scratch(32), vmem(1024, C, dtype=F32), vmem(1024, C),
        vmem(16, C), vmem(16, C), vmem(ROWS, COLS, C), dma(),
        vmem(10, 48, C, dtype=F32), vmem(10, 32, C, dtype=F32), vmem(10, 32, C), vmem(16, 48, C),
        vmem(C, C, dtype=F32), reduce_scratch(HALF, 48), reduce_scratch(HALF + 128, 32), vmem(8, 2 * C, dtype=F32), vmem(8, 2 * C, dtype=F32), dma(), dma(),
    ]
    anywhere = pl.BlockSpec(memory_space=pl.ANY)
    here = pl.BlockSpec(memory_space=pltpu.VMEM)
    predicted, grad0, grad1, gradm, gradg = pl.pallas_call(
        functools.partial(kernel, scales, len(INPUTS)),
        out_shape=[jax.ShapeDtypeStruct((ROWS, COLS, C), BF16)]
        + [jax.ShapeDtypeStruct((n, 128), F32) for n in (18, 18, 2, 8)],
        in_specs=[anywhere] * len(INPUTS),
        out_specs=[anywhere] + [here] * 4,
        scratch_shapes=scratch,
        compiler_params=pltpu.CompilerParams(collective_id=0, has_side_effects=True, vmem_limit_bytes=VMEM_BYTES),
    )(*[args[n] for n in INPUTS])
    predicted, grad0, grad1, gradm, gradg = hand_over(predicted, grad0, grad1, gradm, gradg)
    return predicted[None], grad0.reshape(-1), grad1.reshape(-1), gradm.reshape(-1), gradg.reshape(-1)


def solution(mesh):
    tables = (*spectral_tables(), cell_tables())
    tile = P("batch", "lat", "lon", None)
    split = P(("lat", "lon", "batch"))
    return jax.shard_map(
        functools.partial(on_device, tables), mesh=mesh, in_specs=(tile, P(), P(), P(), P(), tile),
        out_specs=(tile, split, split, split, split), check_vma=False,
    )
```

```python
import functools
import math

import jax
import jax.numpy as jnp
import ml_dtypes
import numpy as np
from jax import lax
from jax.experimental import pallas as pl
from jax.experimental.pallas import tpu as pltpu
from jax.sharding import PartitionSpec as P

MESH = pl.DeviceIdType.MESH
F32 = jnp.float32
BF16 = jnp.bfloat16
C = 256
NLAT, NLON = 8, 16
ROWS, COLS = 16, 48
VMEM_BYTES = 56 * 2**20


def spectral_tables():
    lat_n, lon_n, kl, km = 16, 96, 16, 32
    freq = np.repeat(np.arange(kl) - kl // 2, km)
    mode = np.tile(np.arange(km), kl)
    norm = 1.0 / math.sqrt(lat_n * lon_n)

    def phase(i, j):
        whole = (freq[:, None] * i[None] * lon_n + mode[:, None] * j[None] * lat_n) % (lat_n * lon_n)
        return 2.0 * np.pi * whole / (lat_n * lon_n)

    forward = np.zeros((2, kl * km, NLON, NLAT, 2, 8))
    for lon in range(NLON):
        for lat in range(NLAT):
            for r in range(2):
                j = lon * 6 + np.arange(6)
                ph = phase(np.full(6, lat * 2 + r), j)
                forward[0, :, lon, lat, r, 1:7] = np.cos(ph) * norm
                forward[1, :, lon, lat, r, 1:7] = -np.sin(ph) * norm
    forward = forward.reshape(2 * kl * km, NLON * NLAT * 16)
    weight = np.where(mode == 0, 1.0, 2.0) * norm
    back = np.zeros((NLAT * NLON, 32, 2, kl * km))
    for lat in range(NLAT):
        for lon in range(NLON):
            i = np.repeat(lat * 2 + np.array([0, 1, -1, 2]), 8)
            j = np.tile(lon * 6 - 1 + np.arange(8), 4)
            ph = phase(i, j).T
            back[lat * NLON + lon, :, 0] = np.cos(ph) * weight
            back[lat * NLON + lon, :, 1] = -np.sin(ph) * weight
    back = back.reshape(NLAT, NLON, 32, 2 * kl * km)
    forward = forward.reshape(2 * kl * km, NLON, NLAT * 16).transpose(1, 0, 2)
    return forward.astype(ml_dtypes.bfloat16), back.astype(ml_dtypes.bfloat16)


def cell_tables():
    pool2 = np.zeros((32, 2, 64))
    for j in range(32):
        pool2[j, :, 2 * j : 2 * j + 2] = 0.25
    pool4 = np.zeros((8, 4, 32))
    for j in range(1, 7):
        pool4[j, :, 4 * j : 4 * j + 4] = 1 / 16
    dec = np.zeros((4, 32, 8, 48))
    for r in range(4):
        for j in range(24):
            dec[r, 4 + j, :, 8 * (j // 4) : 8 * (j // 4) + 8] += 1 / 16
            dec[r, 4 + j, 2 * r : 2 * r + 2, 2 * j : 2 * j + 2] += 1
    sum8 = np.zeros((8, 8, 48))
    for j in range(6):
        sum8[1 + j, :, 8 * j : 8 * j + 8] = 1
    pick = np.zeros((64, 8, 32))
    for half, row, col in ((0, 0, 4), (32, 7, 27)):
        for i in range(24):
            pick[half + i, row, 4 + i] = 1
        for r in range(8):
            pick[half + 24 + r, r, col] = 1
    place = np.zeros((10, 32, 10, 16))
    for j in range(24):
        place[0, 4 + j, j // 16, j % 16] = 1
        place[9, 4 + j, 2 + j // 16, j % 16] = 1
    for r in range(8):
        place[1 + r, 3, 4, 8 + r] = 1
        place[1 + r, 28, 5, 8 + r] = 1
    place[0, 3, 6, 7] = 1
    place[0, 28, 7, 0] = 1
    place[9, 3, 8, 7] = 1
    place[9, 28, 9, 0] = 1
    up4 = np.zeros((10, 32, 4, 8))
    for r in range(10):
        for j in range(32):
            up4[r, j, (2, 0, 1, 3)[(r + 3) // 4], j // 4] = 1 / 16
    up2 = np.zeros((2, 48, 32))
    up8 = np.zeros((2, 48, 8))
    for j in range(48):
        up2[:, j, 4 + j // 2] = 1
        up8[:, j, 1 + j // 8] = 1
    hpick = np.zeros((160, 16, 48))
    hplace = np.zeros((22, 32, 160))
    for j in range(3):
        for r in range(16):
            hpick[3 * r + j, r, j] = 1
            hpick[48 + 3 * r + j, r, 45 + j] = 1
            hplace[3 + r, 16 + j, 3 * r + j] = 1
            hplace[3 + r, 13 + j, 48 + 3 * r + j] = 1
        for i in range(3):
            for seg, row, col, to_row, to_col in (
                (96, 0, 0, 19, 16), (112, 0, 45, 19, 13), (128, 13, 0, 0, 16), (144, 13, 45, 0, 13)
            ):
                hpick[seg + 3 * i + j, row + i, col + j] = 1
                hplace[to_row + i, to_col + j, seg + 3 * i + j] = 1
    shapes = dict(
        hpick=(hpick, (160, 768)), hplace=(hplace, (704, 160)),
        pool2=(pool2, (32, 128)), pool4=(pool4, (8, 128)), dec=(dec, (128, 384)), sum8=(sum8, (8, 384)),
        pick=(pick, (64, 256)), place=(place, (320, 160)), up4=(up4, (320, 32)), up2=(up2, (96, 32)),
        up8=(up8, (96, 8)),
    )
    return {k: v.reshape(s).astype(ml_dtypes.bfloat16) for k, (v, s) in shapes.items()}


def dot(a, b):
    return jnp.dot(a, b, preferred_element_type=F32)


def dot_rows(a, b):
    return lax.dot_general(a, b, (((0,), (0,)), ((), ())), preferred_element_type=F32)


def dot_cols(a, b):
    return lax.dot_general(a, b, (((1,), (1,)), ((), ())), preferred_element_type=F32)


def gelu_both(v):
    k, q = 0.7978845608028654, 0.044715
    sq = v * v
    t = jnp.tanh(k * (v * (1.0 + q * sq)))
    half = 0.5 * (1.0 + t)
    return v * half, half + (0.5 * v) * (1.0 - t * t) * (k * (1.0 + (3.0 * q) * sq))


def place():
    return lax.axis_index("lat"), lax.axis_index("lon"), lax.axis_index("batch")


def step(pos, by, n):
    return lax.rem(pos + (by + n), n)


def signal(lat, lon, batch):
    pl.semaphore_signal(
        pltpu.get_barrier_semaphore(), inc=1, device_id={"lat": lat, "lon": lon, "batch": batch}, device_id_type=MESH
    )


def remote(src, dst, send, recv, lat, lon, batch):
    return pltpu.make_async_remote_copy(
        src_ref=src, dst_ref=dst, send_sem=send, recv_sem=recv,
        device_id={"lat": lat, "lon": lon, "batch": batch}, device_id_type=MESH,
    )


NEIGHBOURS = ((1, 0), (-1, 0), (0, 1), (0, -1), (1, 1), (1, -1), (-1, 1), (-1, -1))


HALO_SENDS = (
    ((0, -1), 0, 48), ((0, 1), 48, 48), ((-1, -1), 96, 16), ((-1, 1), 112, 16), ((1, -1), 128, 16), ((1, 1), 144, 16),
)


def halo_copies(field, rows_top, rows_bot, packed, halo, send, recv):
    lat, lon, batch = place()
    copies = [
        remote(packed.at[pl.ds(at, n)], halo.at[pl.ds(at, n)], send.at[i], recv.at[i],
               step(lat, dlat, NLAT), step(lon, dlon, NLON), batch)
        for i, ((dlat, dlon), at, n) in enumerate(HALO_SENDS)
    ]
    copies.append(remote(field.at[pl.ds(13, 3)], rows_top, send.at[6], recv.at[6], step(lat, 1, NLAT), lon, batch))
    copies.append(remote(field.at[pl.ds(0, 3)], rows_bot, send.at[7], recv.at[7], step(lat, -1, NLAT), lon, batch))
    return copies


EDGE_SENDS = (
    ((1, 0), 2, 2, 0), ((-1, 0), 0, 2, 2), ((0, 1), 3, 1, 4), ((0, -1), 1, 1, 5),
    ((1, 1), 3, 1, 6), ((1, -1), 2, 1, 7), ((-1, 1), 1, 1, 8), ((-1, -1), 0, 1, 9),
)


def edge_copies(edges, ring, send, recv):
    lat, lon, batch = place()
    return [
        remote(
            edges.at[pl.ds(seg, n)], ring.at[pl.ds(at, n)], send.at[i], recv.at[i],
            step(lat, dlat, NLAT), step(lon, dlon, NLON), batch,
        )
        for i, ((dlat, dlon), seg, n, at) in enumerate(EDGE_SENDS)
    ]


def greet_all():
    lat, lon, batch = place()
    for dlat, dlon in NEIGHBOURS[4:]:
        signal(step(lat, dlat, NLAT), step(lon, dlon, NLON), batch)
    for k in (4, 3, 5, 2, 6, 1, 7):
        signal(step(lat, k, NLAT), lon, batch)
    for k in Spectral.FAR_FIRST:
        signal(lat, step(lon, k, NLON), batch)
    signal(lat, lon + 2 - 4 * lax.rem(lon // 2, 2), 1 - batch)
    signal(lat, lon, 1 - batch)
    return 28


class Spectral:
    FAR_FIRST = (10, 6, 9, 7, 11, 5, 8, 12, 4, 3, 13, 2, 14, 1, 15)

    def __init__(self, slot, cells, share, got, modes, got_modes, send1, recv1, send2, recv2, send3, recv3):
        lat, lon, batch = place()
        self.lat, self.lon, self.cells = lat, lon, cells
        self.share, self.got, self.modes, self.got_modes = share, got, modes, got_modes
        self.own = pltpu.make_async_copy(slot, cells.at[lat], recv1.at[lat])
        self.first = [
            remote(slot, cells.at[lat], send1.at[k - 1], recv1.at[lat], step(lat, k, NLAT), lon, batch)
            for k in range(1, NLAT)
        ]
        self.arrived = [pltpu.make_async_copy(slot, cells.at[l], recv1.at[l]) for l in range(NLAT)]
        self.second, self.third = [], []
        for k in self.FAR_FIRST:
            to = step(lon, k, NLON)
            self.second.append(remote(share.at[to], got.at[lon], send2.at[k - 1], recv2.at[k - 1], lat, to, batch))
            self.third.append(remote(modes.at[to], got_modes.at[lon], send3.at[k - 1], recv3.at[k - 1], lat, to, batch))

    def begin(self):
        for k in (4, 3, 5, 2, 6, 1, 7):
            self.first[k - 1].start()
        self.own.start()

    def spread(self, table, gain, sign, synth, sc, coef):
        for copy in self.arrived:
            copy.wait()
        sc[...] = dot(table[...], self.cells[...].reshape(NLAT * 16, C))
        gr, gi = gain[:, :C], gain[:, C:] * sign
        sr, si = sc[0:512], sc[512:1024]
        coef[0:512] = (gr * sr - gi * si).astype(BF16)
        coef[512:1024] = (gr * si + gi * sr).astype(BF16)
        rows = self.share.shape[1]
        weights = synth[:, 0:rows].reshape(NLON * rows, 1024)
        self.share[...] = dot(weights, coef[...]).astype(BF16).reshape(NLON, rows, C)
        for copy in self.second:
            copy.start()
        self.got[self.lon] = self.share[self.lon]
        re = sc[pl.ds(pl.multiple_of(64 * self.lat, 8), 64), :]
        im = sc[pl.ds(pl.multiple_of(512 + 64 * self.lat, 8), 64), :]
        for to in range(NLON):
            self.modes[to] = jnp.concatenate([re[4 * to : 4 * to + 4], im[4 * to : 4 * to + 4]], axis=0)
        for copy in self.third:
            copy.start()
        self.got_modes[self.lon] = self.modes[self.lon]

    def collect(self):
        for copy in self.second:
            copy.wait_recv()
        total = self.got[0].astype(F32)
        for h in range(1, NLON):
            total += self.got[h].astype(F32)
        return total.astype(BF16)

    def collect_modes(self):
        for copy in self.third:
            copy.wait_recv()
        total = self.got_modes[0]
        for h in range(1, NLON):
            total += self.got_modes[h]
        return total

    def close(self):
        for copy in self.first + self.second + self.third:
            copy.wait_send()


HALF = 1152


PIECE = 384


class Reduce:
    def __init__(self, x_rows, out, got1, total1, acc1, got2x, got2y, acc2x, acc2y, got3x, got3y, blocks, got4, sems):
        s1, r1, s2, r2, s3, r3, s4, r4 = sems
        self.out, self.got1, self.total1, self.acc1 = out, got1, total1, acc1
        self.blocks, self.got4 = blocks, got4
        lat, lon, batch = place()
        self.lat, self.core = lat, lax.rem(lon, 2)
        self.x = lon // 4
        self.y = lax.rem(lon // 2, 2) * 2 + batch
        core, x, y = self.core, self.x, self.y
        self.one = []
        for i, at in enumerate(range(0, out.shape[0], PIECE)):
            part = pl.ds(at, min(PIECE, out.shape[0] - at))
            self.one.append((part, remote(out.at[part], got1.at[part], s1.at[i], r1.at[i], lat, lon + 1 - 2 * core, batch)))

        def peer(along_x, k):
            if along_x:
                return lax.rem(x + k, 4), (lat, step(lon, 4 * k, NLON), batch)
            to = lax.rem(y + k, 4)
            return to, (lat, x * 4 + (to // 2) * 2 + core, lax.rem(to, 2))

        self.ways = []
        for way, (rows, got2, acc2, got3) in enumerate((
            (pl.ds(0, x_rows), got2x, acc2x, got3x), (pl.ds(x_rows, 80 - x_rows), got2y, acc2y, got3y)
        )):
            two, three = [], []
            for k in (2, 1, 3):
                to, device = peer(way == 0, k)
                src = acc1.at[:, to, rows] if way == 0 else acc1.at[to, :, rows]
                two.append(remote(src, got2.at[k - 1], s2.at[way, k - 1], r2.at[way, k - 1], *device))
                to, device = peer(way == 1, k)
                three.append(remote(acc2.at[to], got3.at[k - 1], s3.at[way, k - 1], r3.at[way, k - 1], *device))
            self.ways.append((rows, got2, acc2, got3, two, three))
        self.is_own = lat // 4 == core
        self.e_own = lax.rem(lat, 4) * 2 + core
        self.four = [
            remote(blocks.at[e], got4.at[lat], s4.at[e], r4.at[lat], core * 4 + e // 2, lon - core + e % 2, batch)
            for e in range(8)
        ]
        self.arrive = [remote(blocks.at[0], got4.at[h], s4.at[0], r4.at[h], lat, lon + 1 - 2 * core, batch) for h in range(8)]

    def halves(self, windows, grad):
        n = grad.shape[0]
        height = n // windows.shape[1]

        def piece(i):
            tap, side = i // 2, lax.rem(i, 2)
            cols = pl.ds(pl.multiple_of(side * PIECE, 128), PIECE)
            return dot_rows(windows[pl.ds(tap, height), :, cols].reshape(n, PIECE), grad)

        for i in range(3):
            self.out[PIECE * i : PIECE * i + PIECE, :] = piece(i + 3 - 3 * self.core).astype(BF16)
            self.one[i][1].start()
        for i in range(3):
            self.total1[PIECE * i : PIECE * i + PIECE, :] = piece(i + 3 * self.core)

    def first_axis(self):
        total1, acc1 = self.total1, self.acc1
        for part, copy in self.one:
            copy.wait_recv()
            total1[part, :] += self.got1[part, :].astype(F32)
        for x in range(4):
            for y in range(4):
                pieces = []
                for e in range(8):
                    w = x * 8 + (y // 2) * 4 + (e % 2) * 2 + y % 2
                    at = 288 * (e // 2) + 9 * w
                    pieces.append(total1[at : at + 9])
                for e in range(8):
                    w = x * 8 + (y // 2) * 4 + (e % 2) * 2 + y % 2
                    at = HALF + 32 * (e // 2) + w
                    pieces.append(total1[at : at + 1] if total1.shape[0] > HALF else jnp.zeros((1, C), F32))
                acc1[y, x] = jnp.concatenate(pieces, axis=0).astype(BF16)
        for i in range(3):
            for way in range(2):
                self.ways[way][4][i].start()

    def second_axis(self):
        for way, (rows, got2, acc2, _, two, three) in enumerate(self.ways):
            for copy in two:
                copy.wait_recv()
            for i in range(4):
                mine = self.acc1[i, self.x, rows] if way == 0 else self.acc1[self.y, i, rows]
                acc2[i] = (
                    mine.astype(F32) + got2[0, i].astype(F32) + got2[1, i].astype(F32) + got2[2, i].astype(F32)
                ).astype(BF16)
            for copy in three:
                copy.start()

    def to_owners(self):
        blocks, got4 = self.blocks, self.got4
        totals = []
        for way, (_, _, acc2, got3, _, three) in enumerate(self.ways):
            for copy in three:
                copy.wait_recv()
            mine = acc2[self.y if way == 0 else self.x]
            totals.append(mine.astype(F32) + got3[0].astype(F32) + got3[1].astype(F32) + got3[2].astype(F32))
        total = jnp.concatenate(totals, axis=0)
        for e in range(8):
            rows = [total[9 * e : 9 * e + 9], total[72 + e : 73 + e], jnp.zeros((6, C), F32)]
            blocks[e] = jnp.concatenate(rows, axis=0).astype(BF16)
        for e in range(8):
            mine = self.is_own & (self.e_own == e)

            @pl.when(jnp.logical_not(mine))
            def _():
                self.four[e].start()

            @pl.when(mine)
            def _():
                got4[self.lat] = blocks[e]

    def finish(self):
        got4 = self.got4
        total = None
        for h in range(8):

            @pl.when(jnp.logical_not(self.is_own & (self.lat == h)))
            def _():
                self.arrive[h].wait_recv()

        for h in range(8):
            total = got4[h].astype(F32) if h == 0 else total + got4[h].astype(F32)
        for e in range(8):

            @pl.when(jnp.logical_not(self.is_own & (self.e_own == e)))
            def _():
                self.four[e].wait_send()

        for copy in [c for _, c in self.one] + [c for way in self.ways for c in way[4] + way[5]]:
            copy.wait_send()
        return total


INPUTS = (
    "field", "hpick", "cot", "dec", "sum8", "hplace", "k0", "pool2", "k1", "pool4", "pick", "gain", "table", "synth", "mixing", "place",
    "up4", "up2", "up8",
)


def kernel(scales, n_in, *refs):
    src = dict(zip(INPUTS, refs[:n_in]))
    out_pred, out0, out1, outm, outg = refs[n_in : n_in + 5]
    names = list(INPUTS)
    v = dict(zip(names, refs[n_in + 5 :]))
    (
        load_sem, packed, halo_in, rows_top, rows_bot, fs, x3, x3c, l0f, c1s, x13, level0, da0, level1, a1, p1, slot, gl2, edges, ring, halo_s, halo_r,
        edge_s, edge_r, spec1, spec2, sc, coef, slot2, level2, pred, pred_sem,
        g1s, slope, xg, gp0, mixes, red0, red1, gain_in, gain_got, gain_s, gain_r,
    ) = refs[n_in + 5 + len(names) :]
    cot, k0, k1, gain, table, mixing = (v[n] for n in ("cot", "k0", "k1", "gain", "table", "mixing"))
    field = v["field"]
    lat, lon, batch = place()

    n_peers = greet_all()
    loads = {}
    for i, n in enumerate(names):
        ref = src[n].at[dict(synth=lat, table=lon)[n]] if n in ("synth", "table") else src[n]
        loads[n] = pltpu.make_async_copy(ref, v[n], load_sem.at[i])
    early = ("field", "hpick", "k0", "cot", "dec", "sum8")
    for n in early:
        loads[n].start()
    loads["field"].wait()
    loads["hpick"].wait()
    packed[...] = dot(v["hpick"][...], field[...].reshape(768, C)).astype(BF16)
    fs[3:19, 16:64] = field[...].astype(F32)
    loads["k0"].wait()

    def level_rows(y, n, c0, c1):
        size = n * (c1 - c0)
        acc = dot(x3[pl.ds(y, n), c0:c1].reshape(size, 3 * C), k0[0])
        acc += dot(x3[pl.ds(y + 1, n), c0:c1].reshape(size, 3 * C), k0[1])
        acc += dot(x3[pl.ds(y + 2, n), c0:c1].reshape(size, 3 * C), k0[2])
        act, grad = gelu_both(acc)
        out = fs[pl.ds(y + 1, n), 8 + c0 : 8 + c1, :] + act.reshape(n, c1 - c0, C)
        l0f[pl.ds(y, n), c0:c1] = out.astype(BF16)
        a, b = max(c0, 8), min(c1, 56)
        level0[pl.ds(y, n), a - 8 : b - 8] = out[:, a - c0 : b - c0].astype(BF16)
        da0[pl.ds(y, n), a - 8 : b - 8] = grad.reshape(n, c1 - c0, C)[:, a - c0 : b - c0].astype(BF16)

    for b in range(3):
        x3[3:19, 16:48, b * C : (b + 1) * C] = fs[3:19, 23 + b : 55 + b, :].astype(BF16)
    lax.fori_loop(0, 2, lambda i, _: (level_rows(4 + 6 * i, 6, 16, 48), 0)[1], 0)
    pl.semaphore_wait(pltpu.get_barrier_semaphore(), n_peers)
    halo = halo_copies(field, rows_top, rows_bot, packed, halo_in, halo_s, halo_r)
    for copy in halo:
        copy.start()
    for n in names:
        if n not in early:
            loads[n].start()

    for n in ("cot", "dec", "sum8"):
        loads[n].wait()
    for half in range(2):
        part = cot[8 * half : 8 * half + 8].reshape(384, C)
        a1[4 * half : 4 * half + 4] = dot(v["dec"][...], part).reshape(4, 32, C)
        gl2[8 * half : 8 * half + 8] = dot(v["sum8"][...], part)
    c1s[...] = jnp.zeros_like(c1s)
    g1s[...] = jnp.zeros_like(g1s)
    for n in ("hplace", "pool2", "k1", "pool4", "pick"):
        loads[n].wait()

    for copy in halo:
        copy.wait()

    edge_top = lat == 0
    edge_bot = lat == NLAT - 1
    fs[0:3, 16:64] = jnp.where(edge_top, 0.0, rows_top[...].astype(F32))
    fs[19:22, 16:64] = jnp.where(edge_bot, 0.0, rows_bot[...].astype(F32))
    sides = dot(v["hplace"][...], halo_in[...]).reshape(22, 32, C)
    for half, at in ((0, 0), (16, 64)):
        fs[0:3, at : at + 16] = jnp.where(edge_top, 0.0, sides[0:3, half : half + 16])
        fs[3:19, at : at + 16] = sides[3:19, half : half + 16]
        fs[19:22, at : at + 16] = jnp.where(edge_bot, 0.0, sides[19:22, half : half + 16])
    for b in range(3):
        lane = slice(b * C, (b + 1) * C)
        x3[0:3, :, lane] = fs[0:3, 7 + b : 71 + b, :].astype(BF16)
        x3[19:22, :, lane] = fs[19:22, 7 + b : 71 + b, :].astype(BF16)
        x3[3:19, 0:16, lane] = fs[3:19, 7 + b : 23 + b, :].astype(BF16)
        x3[3:19, 48:64, lane] = fs[3:19, 55 + b : 71 + b, :].astype(BF16)
    lax.fori_loop(0, 2, lambda i, _: (level_rows(16 * i, 4, 0, 64), 0)[1], 0)
    level_rows(4, 12, 0, 16)
    level_rows(4, 12, 48, 64)

    for y in range(10):
        row = dot(v["pool2"][...], l0f[2 * y : 2 * y + 2].reshape(128, C)).astype(BF16).astype(F32)
        if y == 0:
            row = jnp.where(edge_top, 0.0, row)
        if y == 9:
            row = jnp.where(edge_bot, 0.0, row)
        c1s[y, 8:40, :] = row
    for b in range(3):
        x13[:, :, b * C : (b + 1) * C] = c1s[:, 7 + b : 39 + b, :].astype(BF16)
    pre = dot(x13[0:8].reshape(256, 3 * C), k1[0])
    pre += dot(x13[1:9].reshape(256, 3 * C), k1[1])
    pre += dot(x13[2:10].reshape(256, 3 * C), k1[2])
    act, _ = gelu_both(pre)
    col = lax.broadcasted_iota(jnp.int32, (8, 32, C), 1)
    mine = (col >= 4) & (col < 28)
    p1[...] = jnp.where(mine, pre.reshape(8, 32, C), 0.0)
    lev1 = jnp.where(mine, c1s[1:9, 8:40, :] + act.reshape(8, 32, C), 0.0).astype(BF16)
    level1[...] = lev1
    for half in range(2):
        slot[8 * half : 8 * half + 8] = dot(v["pool4"][...], lev1[4 * half : 4 * half + 4].reshape(128, C)).astype(BF16)

    forth = Spectral(slot, *spec1[:5], *spec1[5:])
    forth.begin()
    edges[:, 0] = dot(v["pick"][...], a1[...].reshape(256, C).astype(BF16)).astype(BF16).reshape(4, 16, C)
    edges[:, 1] = dot(v["pick"][...], p1[...].reshape(256, C).astype(BF16)).astype(BF16).reshape(4, 16, C)
    edge = edge_copies(edges, ring, edge_s, edge_r)
    for copy in edge:
        copy.start()
    for n in ("gain", "table", "synth", "mixing", "place", "up4", "up2", "up8"):
        loads[n].wait()
    for b in range(3):
        x3c[:, :, b * C : (b + 1) * C] = fs[2:20, 15 + b : 63 + b, :].astype(BF16)
    forth.spread(table, gain, 1.0, v["synth"], sc, coef)
    for copy in edge:
        copy.wait()
    g1s[:, 8:40, :] = dot(v["place"][...], ring[:, 0].reshape(160, C)).reshape(10, 32, C)
    g1s[1:9, 8:40, :] += a1[...]
    slope[...] = dot(v["place"][...], ring[:, 1].reshape(160, C)).reshape(10, 32, C)
    slope[1:9] += p1[...]
    _, grad1 = gelu_both(slope[...])
    slope[...] = grad1
    filt = forth.collect()
    mixed = dot(filt, mixing[...])
    act, grad = gelu_both(mixed)
    cell = lax.rem(lax.broadcasted_iota(jnp.int32, (16, C), 0), 8)
    gm = jnp.where((cell >= 1) & (cell < 7), gl2[...] * grad, 0.0).astype(BF16)
    slot2[...] = dot_cols(gm, mixing[...]).astype(BF16)

    sum1 = Reduce(32, *red1[:12], red1[12:])
    sum0 = Reduce(48, *red0[:12], red0[12:])

    back_way = Spectral(slot2, *spec2[:5], *spec2[5:])
    back_way.begin()
    level2[...] = (slot[...].astype(F32) + act).astype(BF16)
    mix = dot_rows(filt, gm)
    mixes[...] = mix
    sum1.out[HALF : HALF + 128, :] = mixes[pl.ds(pl.multiple_of(128 - 128 * sum1.core, 128), 128), :].astype(BF16)
    sum1.total1[HALF : HALF + 128, :] = mixes[pl.ds(pl.multiple_of(128 * sum1.core, 128), 128), :]
    spec_own = forth.collect_modes()

    def predict(r):
        low = dot(v["up2"][...], level1[r]) + dot(v["up8"][...], level2[8 * (r // 4) : 8 * (r // 4) + 8])
        high = level0[2 * r + 2 : 2 * r + 4].astype(F32) + low.reshape(2, 48, C)
        pred[2 * r : 2 * r + 2] = high.astype(BF16)

    for r in range(4):
        predict(r)
    back_way.spread(table, gain, -1.0, v["synth"], sc, coef)
    for r in range(4, 8):
        predict(r)
    pred_out = pltpu.make_async_copy(pred, out_pred, pred_sem)
    pred_out.start()

    back = back_way.collect()
    gl1 = g1s[:, 8:40, :] + dot(v["up4"][...], back).reshape(10, 32, C)
    col = lax.broadcasted_iota(jnp.int32, (10, 32, C), 1)
    row = lax.broadcasted_iota(jnp.int32, (10, 32, C), 0)
    first = jnp.where(edge_top, 1, 0)
    last = jnp.where(edge_bot, 9, 10)
    valid = (col >= 3) & (col < 29) & (row >= first) & (row < last)
    gp1 = jnp.where(valid, gl1 * slope[...], 0.0)
    g1s[:, 8:40, :] = gp1
    gown = jnp.where((col[1:9] >= 4) & (col[1:9] < 28), gp1[1:9], 0.0).astype(BF16).reshape(256, C)
    sum1.halves(x13, gown)
    sum1.one[3][1].start()

    gc1 = gl1[1:9].reshape(256, C)
    for b in range(3):
        xg[...] = g1s[:, 7 + b : 39 + b, :].astype(BF16)
        for a in range(3):
            gc1 += dot_cols(xg[a : a + 8].reshape(256, C), k1[2 - a, (2 - b) * C : (3 - b) * C, :])
    high = gc1.astype(BF16)
    low = (gc1 - high.astype(F32)).astype(BF16)
    for r in range(8):
        up = dot(v["up2"][...], high[32 * r : 32 * r + 32]) + dot(v["up2"][...], low[32 * r : 32 * r + 32])
        gl0 = cot[2 * r : 2 * r + 2].astype(F32) + 0.25 * up.reshape(2, 48, C)
        gp0[2 * r : 2 * r + 2] = (gl0 * da0[2 * r + 2 : 2 * r + 4].astype(F32)).astype(BF16)
    sum1.first_axis()
    sum0.halves(x3c, gp0[...].reshape(768, C))

    grads = back_way.collect_modes()
    m = lax.rem(4 * lon + lax.broadcasted_iota(jnp.int32, (4, C), 0), 32)
    weight = jnp.where(m == 0, 1.0, 2.0)
    ar, ai, br, bi = spec_own[0:4], spec_own[4:8], grads[0:4], grads[4:8]
    rest = jnp.zeros((4, C), F32)
    gain_in[:, :C] = jnp.concatenate([weight * (ar * br + ai * bi), rest], axis=0)
    gain_in[:, C:] = jnp.concatenate([weight * (ar * bi - ai * br), rest], axis=0)
    swap = remote(gain_in, gain_got, gain_s, gain_r, lat, lon, 1 - batch)
    swap.start()

    sum0.first_axis()
    sum1.second_axis()
    swap.wait()
    gain_in[...] = gain_in[...] + gain_got[...]
    for batch_at in range(2):

        @pl.when(batch == batch_at)
        def _():
            for i in range(2):
                for j in range(4):
                    row = 2 * batch_at + i
                    outg[4 * i + j : 4 * i + j + 1, :] = gain_in[row : row + 1, 128 * j : 128 * j + 128]

    sum0.second_axis()
    sum1.to_owners()
    sum0.to_owners()
    t1 = sum1.finish()
    for r in range(9):
        for j in range(2):
            out1[2 * r + j : 2 * r + j + 1, :] = scales[1] * t1[r : r + 1, 128 * j : 128 * j + 128]
    for j in range(2):
        outm[j : j + 1, :] = scales[2] * t1[9:10, 128 * j : 128 * j + 128]
    t0 = sum0.finish()
    for r in range(9):
        for j in range(2):
            out0[2 * r + j : 2 * r + j + 1, :] = scales[0] * t0[r : r + 1, 128 * j : 128 * j + 128]
    forth.close()
    back_way.close()
    pred_out.wait()


def dma(*n):
    return pltpu.SemaphoreType.DMA(n)


def vmem(*shape, dtype=BF16):
    return pltpu.VMEM(shape, dtype)


def reduce_scratch(rows, x_rows):
    y_rows = 80 - x_rows
    return (
        vmem(rows, C), vmem(rows, C), vmem(rows, C, dtype=F32), vmem(4, 4, 80, C),
        vmem(3, 4, x_rows, C), vmem(3, 4, y_rows, C), vmem(4, x_rows, C), vmem(4, y_rows, C),
        vmem(3, x_rows, C), vmem(3, y_rows, C), vmem(8, 16, C), vmem(8, 16, C),
        dma(4), dma(4), dma(2, 3), dma(2, 3), dma(2, 3), dma(2, 3), dma(8), dma(8),
    )


def hand_over(*arrays):
    n = len(arrays)

    def body(*refs):
        src, dst, buf, (come, go) = refs[:n], refs[n : 2 * n], refs[2 * n : 3 * n], refs[3 * n :]
        inward = [pltpu.make_async_copy(src[i], buf[i], come.at[i]) for i in range(n)]
        outward = [pltpu.make_async_copy(buf[i], dst[i], go.at[i]) for i in range(n)]
        for copy in inward:
            copy.start()
        for i in range(n):
            inward[i].wait()
            outward[i].start()
        for copy in outward:
            copy.wait()

    anywhere = pl.BlockSpec(memory_space=pl.ANY)
    return pl.pallas_call(
        body, out_shape=[jax.ShapeDtypeStruct(a.shape, a.dtype) for a in arrays], in_specs=[anywhere] * n,
        out_specs=[anywhere] * n, scratch_shapes=[vmem(*a.shape, dtype=a.dtype) for a in arrays] + [dma(n), dma(n)],
    )(*arrays)


def on_device(tables, field, kernel0, kernel1, mixing, gain, cotangent):
    table, synth, small = tables
    args = {k: jnp.asarray(a) for k, a in small.items()}
    args |= dict(
        field=field[0], cot=cotangent[0], k0=kernel0.reshape(3, 3 * C, C), k1=kernel1.reshape(3, 3 * C, C),
        mixing=mixing, gain=gain, table=jnp.asarray(table), synth=jnp.asarray(synth),
    )
    cells0 = 2 * 128 * 768
    scales = (1.0 / math.sqrt(cells0), 1.0 / math.sqrt(cells0 // 4), 1.0 / math.sqrt(cells0 // 64))
    names = INPUTS
    scratch = [
        vmem(*args[n].shape[1:]) if n in ("synth", "table") else vmem(*args[n].shape, dtype=args[n].dtype) for n in names
    ]

    def spectral_scratch(rows):
        sems = (dma(7), dma(8), dma(15), dma(15), dma(15), dma(15))
        modes = vmem(NLON, 8, C, dtype=F32)
        return (vmem(NLAT, 16, C), vmem(NLON, rows, C), vmem(NLON, rows, C), modes, modes, *sems)

    scratch += [
        dma(len(names)), vmem(160, C), vmem(160, C), vmem(3, 48, C), vmem(3, 48, C), vmem(22, 80, C, dtype=F32), vmem(22, 64, 3 * C), vmem(18, 48, 3 * C),
        vmem(20, 64, C), vmem(10, 48, C, dtype=F32), vmem(10, 32, 3 * C), vmem(20, 48, C), vmem(20, 48, C),
        vmem(8, 32, C), vmem(8, 32, C, dtype=F32), vmem(8, 32, C, dtype=F32), vmem(16, C), vmem(16, C, dtype=F32),
        vmem(4, 2, 16, C), vmem(10, 2, 16, C), dma(8), dma(8), dma(8), dma(8),
        spectral_scratch(16), spectral_scratch(32), vmem(1024, C, dtype=F32), vmem(1024, C),
        vmem(16, C), vmem(16, C), vmem(ROWS, COLS, C), dma(),
        vmem(10, 48, C, dtype=F32), vmem(10, 32, C, dtype=F32), vmem(10, 32, C), vmem(16, 48, C),
        vmem(C, C, dtype=F32), reduce_scratch(HALF, 48), reduce_scratch(HALF + 128, 32), vmem(8, 2 * C, dtype=F32), vmem(8, 2 * C, dtype=F32), dma(), dma(),
    ]
    anywhere = pl.BlockSpec(memory_space=pl.ANY)
    here = pl.BlockSpec(memory_space=pltpu.VMEM)
    predicted, grad0, grad1, gradm, gradg = pl.pallas_call(
        functools.partial(kernel, scales, len(INPUTS)),
        out_shape=[jax.ShapeDtypeStruct((ROWS, COLS, C), BF16)]
        + [jax.ShapeDtypeStruct((n, 128), F32) for n in (18, 18, 2, 8)],
        in_specs=[anywhere] * len(INPUTS),
        out_specs=[anywhere] + [here] * 4,
        scratch_shapes=scratch,
        compiler_params=pltpu.CompilerParams(collective_id=0, has_side_effects=True, vmem_limit_bytes=VMEM_BYTES),
    )(*[args[n] for n in INPUTS])
    predicted, grad0, grad1, gradm, gradg = hand_over(predicted, grad0, grad1, gradm, gradg)
    return predicted[None], grad0.reshape(-1), grad1.reshape(-1), gradm.reshape(-1), gradg.reshape(-1)


def solution(mesh):
    tables = (*spectral_tables(), cell_tables())
    tile = P("batch", "lat", "lon", None)
    split = P(("lat", "lon", "batch"))
    return jax.shard_map(
        functools.partial(on_device, tables), mesh=mesh, in_specs=(tile, P(), P(), P(), P(), tile),
        out_specs=(tile, split, split, split, split), check_vma=False,
    )
```

```python
import functools
import math

import jax
import jax.numpy as jnp
import ml_dtypes
import numpy as np
from jax import lax
from jax.experimental import pallas as pl
from jax.experimental.pallas import tpu as pltpu
from jax.sharding import PartitionSpec as P

MESH = pl.DeviceIdType.MESH
F32 = jnp.float32
BF16 = jnp.bfloat16
C = 256
NLAT, NLON = 8, 16
ROWS, COLS = 16, 48
VMEM_BYTES = 56 * 2**20


def spectral_tables():
    lat_n, lon_n, kl, km = 16, 96, 16, 32
    freq = np.repeat(np.arange(kl) - kl // 2, km)
    mode = np.tile(np.arange(km), kl)
    norm = 1.0 / math.sqrt(lat_n * lon_n)

    def phase(i, j):
        whole = (freq[:, None] * i[None] * lon_n + mode[:, None] * j[None] * lat_n) % (lat_n * lon_n)
        return 2.0 * np.pi * whole / (lat_n * lon_n)

    forward = np.zeros((2, kl * km, NLON, NLAT, 2, 8))
    for lon in range(NLON):
        for lat in range(NLAT):
            for r in range(2):
                j = lon * 6 + np.arange(6)
                ph = phase(np.full(6, lat * 2 + r), j)
                forward[0, :, lon, lat, r, 1:7] = np.cos(ph) * norm
                forward[1, :, lon, lat, r, 1:7] = -np.sin(ph) * norm
    forward = forward.reshape(2 * kl * km, NLON * NLAT * 16)
    weight = np.where(mode == 0, 1.0, 2.0) * norm
    back = np.zeros((NLAT * NLON, 32, 2, kl * km))
    for lat in range(NLAT):
        for lon in range(NLON):
            i = np.repeat(lat * 2 + np.array([0, 1, -1, 2]), 8)
            j = np.tile(lon * 6 - 1 + np.arange(8), 4)
            ph = phase(i, j).T
            back[lat * NLON + lon, :, 0] = np.cos(ph) * weight
            back[lat * NLON + lon, :, 1] = -np.sin(ph) * weight
    back = back.reshape(NLAT, NLON, 32, 2 * kl * km)
    forward = forward.reshape(2 * kl * km, NLON, NLAT * 16).transpose(1, 0, 2)
    return forward.astype(ml_dtypes.bfloat16), back.astype(ml_dtypes.bfloat16)


def cell_tables():
    pool2 = np.zeros((32, 2, 64))
    for j in range(32):
        pool2[j, :, 2 * j : 2 * j + 2] = 0.25
    pool4 = np.zeros((8, 4, 32))
    for j in range(1, 7):
        pool4[j, :, 4 * j : 4 * j + 4] = 1 / 16
    dec = np.zeros((4, 32, 8, 48))
    for r in range(4):
        for j in range(24):
            dec[r, 4 + j, :, 8 * (j // 4) : 8 * (j // 4) + 8] += 1 / 16
            dec[r, 4 + j, 2 * r : 2 * r + 2, 2 * j : 2 * j + 2] += 1
    sum8 = np.zeros((8, 8, 48))
    for j in range(6):
        sum8[1 + j, :, 8 * j : 8 * j + 8] = 1
    pick = np.zeros((64, 8, 32))
    for half, row, col in ((0, 0, 4), (32, 7, 27)):
        for i in range(24):
            pick[half + i, row, 4 + i] = 1
        for r in range(8):
            pick[half + 24 + r, r, col] = 1
    place = np.zeros((10, 32, 10, 16))
    for j in range(24):
        place[0, 4 + j, j // 16, j % 16] = 1
        place[9, 4 + j, 2 + j // 16, j % 16] = 1
    for r in range(8):
        place[1 + r, 3, 4, 8 + r] = 1
        place[1 + r, 28, 5, 8 + r] = 1
    place[0, 3, 6, 7] = 1
    place[0, 28, 7, 0] = 1
    place[9, 3, 8, 7] = 1
    place[9, 28, 9, 0] = 1
    up4 = np.zeros((10, 32, 4, 8))
    for r in range(10):
        for j in range(32):
            up4[r, j, (2, 0, 1, 3)[(r + 3) // 4], j // 4] = 1 / 16
    up2 = np.zeros((2, 48, 32))
    up8 = np.zeros((2, 48, 8))
    for j in range(48):
        up2[:, j, 4 + j // 2] = 1
        up8[:, j, 1 + j // 8] = 1
    hpick = np.zeros((160, 16, 48))
    hplace = np.zeros((22, 32, 160))
    for j in range(3):
        for r in range(16):
            hpick[3 * r + j, r, j] = 1
            hpick[48 + 3 * r + j, r, 45 + j] = 1
            hplace[3 + r, 16 + j, 3 * r + j] = 1
            hplace[3 + r, 13 + j, 48 + 3 * r + j] = 1
        for i in range(3):
            for seg, row, col, to_row, to_col in (
                (96, 0, 0, 19, 16), (112, 0, 45, 19, 13), (128, 13, 0, 0, 16), (144, 13, 45, 0, 13)
            ):
                hpick[seg + 3 * i + j, row + i, col + j] = 1
                hplace[to_row + i, to_col + j, seg + 3 * i + j] = 1
    shapes = dict(
        hpick=(hpick, (160, 768)), hplace=(hplace, (704, 160)),
        pool2=(pool2, (32, 128)), pool4=(pool4, (8, 128)), dec=(dec, (128, 384)), sum8=(sum8, (8, 384)),
        pick=(pick, (64, 256)), place=(place, (320, 160)), up4=(up4, (320, 32)), up2=(up2, (96, 32)),
        up8=(up8, (96, 8)),
    )
    return {k: v.reshape(s).astype(ml_dtypes.bfloat16) for k, (v, s) in shapes.items()}


def dot(a, b):
    return jnp.dot(a, b, preferred_element_type=F32)


def dot_rows(a, b):
    return lax.dot_general(a, b, (((0,), (0,)), ((), ())), preferred_element_type=F32)


def dot_cols(a, b):
    return lax.dot_general(a, b, (((1,), (1,)), ((), ())), preferred_element_type=F32)


def gelu_both(v):
    k, q = 0.7978845608028654, 0.044715
    sq = v * v
    t = jnp.tanh(k * (v * (1.0 + q * sq)))
    half = 0.5 * (1.0 + t)
    return v * half, half + (0.5 * v) * (1.0 - t * t) * (k * (1.0 + (3.0 * q) * sq))


def place():
    return lax.axis_index("lat"), lax.axis_index("lon"), lax.axis_index("batch")


def step(pos, by, n):
    return lax.rem(pos + (by + n), n)


def signal(lat, lon, batch):
    pl.semaphore_signal(
        pltpu.get_barrier_semaphore(), inc=1, device_id={"lat": lat, "lon": lon, "batch": batch}, device_id_type=MESH
    )


def remote(src, dst, send, recv, lat, lon, batch):
    return pltpu.make_async_remote_copy(
        src_ref=src, dst_ref=dst, send_sem=send, recv_sem=recv,
        device_id={"lat": lat, "lon": lon, "batch": batch}, device_id_type=MESH,
    )


NEIGHBOURS = ((1, 0), (-1, 0), (0, 1), (0, -1), (1, 1), (1, -1), (-1, 1), (-1, -1))


HALO_SENDS = (
    ((0, -1), 0, 48), ((0, 1), 48, 48), ((-1, -1), 96, 16), ((-1, 1), 112, 16), ((1, -1), 128, 16), ((1, 1), 144, 16),
)


def halo_copies(field, rows_top, rows_bot, packed, halo, send, recv):
    lat, lon, batch = place()
    copies = [
        remote(packed.at[pl.ds(at, n)], halo.at[pl.ds(at, n)], send.at[i], recv.at[i],
               step(lat, dlat, NLAT), step(lon, dlon, NLON), batch)
        for i, ((dlat, dlon), at, n) in enumerate(HALO_SENDS)
    ]
    copies.append(remote(field.at[pl.ds(13, 3)], rows_top, send.at[6], recv.at[6], step(lat, 1, NLAT), lon, batch))
    copies.append(remote(field.at[pl.ds(0, 3)], rows_bot, send.at[7], recv.at[7], step(lat, -1, NLAT), lon, batch))
    return copies


EDGE_SENDS = (
    ((1, 0), 2, 2, 0), ((-1, 0), 0, 2, 2), ((0, 1), 3, 1, 4), ((0, -1), 1, 1, 5),
    ((1, 1), 3, 1, 6), ((1, -1), 2, 1, 7), ((-1, 1), 1, 1, 8), ((-1, -1), 0, 1, 9),
)


def edge_copies(edges, ring, send, recv):
    lat, lon, batch = place()
    return [
        remote(
            edges.at[pl.ds(seg, n)], ring.at[pl.ds(at, n)], send.at[i], recv.at[i],
            step(lat, dlat, NLAT), step(lon, dlon, NLON), batch,
        )
        for i, ((dlat, dlon), seg, n, at) in enumerate(EDGE_SENDS)
    ]


def greet_all():
    lat, lon, batch = place()
    for dlat, dlon in NEIGHBOURS[4:]:
        signal(step(lat, dlat, NLAT), step(lon, dlon, NLON), batch)
    for k in (4, 3, 5, 2, 6, 1, 7):
        signal(step(lat, k, NLAT), lon, batch)
    for k in Spectral.FAR_FIRST:
        signal(lat, step(lon, k, NLON), batch)
    signal(lat, lon + 2 - 4 * lax.rem(lon // 2, 2), 1 - batch)
    signal(lat, lon, 1 - batch)
    return 28


class Spectral:
    FAR_FIRST = (10, 6, 9, 7, 11, 5, 8, 12, 4, 3, 13, 2, 14, 1, 15)

    def __init__(self, slot, cells, share, got, modes, got_modes, send1, recv1, send2, recv2, send3, recv3):
        lat, lon, batch = place()
        self.lat, self.lon, self.cells = lat, lon, cells
        self.share, self.got, self.modes, self.got_modes = share, got, modes, got_modes
        self.own = pltpu.make_async_copy(slot, cells.at[lat], recv1.at[lat])
        self.first = [
            remote(slot, cells.at[lat], send1.at[k - 1], recv1.at[lat], step(lat, k, NLAT), lon, batch)
            for k in range(1, NLAT)
        ]
        self.arrived = [pltpu.make_async_copy(slot, cells.at[l], recv1.at[l]) for l in range(NLAT)]
        self.second, self.third = [], []
        for k in self.FAR_FIRST:
            to = step(lon, k, NLON)
            self.second.append(remote(share.at[to], got.at[lon], send2.at[k - 1], recv2.at[k - 1], lat, to, batch))
            self.third.append(remote(modes.at[to], got_modes.at[lon], send3.at[k - 1], recv3.at[k - 1], lat, to, batch))

    def begin(self):
        for k in (4, 3, 5, 2, 6, 1, 7):
            self.first[k - 1].start()
        self.own.start()

    def spread(self, table, gain, sign, synth, sc, coef):
        for copy in self.arrived:
            copy.wait()
        sc[...] = dot(table[...], self.cells[...].reshape(NLAT * 16, C))
        gr, gi = gain[:, :C], gain[:, C:] * sign
        sr, si = sc[0:512], sc[512:1024]
        coef[0:512] = (gr * sr - gi * si).astype(BF16)
        coef[512:1024] = (gr * si + gi * sr).astype(BF16)
        rows = self.share.shape[1]
        weights = synth[:, 0:rows].reshape(NLON * rows, 1024)
        self.share[...] = dot(weights, coef[...]).astype(BF16).reshape(NLON, rows, C)
        for copy in self.second:
            copy.start()
        self.got[self.lon] = self.share[self.lon]
        re = sc[pl.ds(pl.multiple_of(64 * self.lat, 8), 64), :]
        im = sc[pl.ds(pl.multiple_of(512 + 64 * self.lat, 8), 64), :]
        for to in range(NLON):
            self.modes[to] = jnp.concatenate([re[4 * to : 4 * to + 4], im[4 * to : 4 * to + 4]], axis=0)
        for copy in self.third:
            copy.start()
        self.got_modes[self.lon] = self.modes[self.lon]

    def collect(self):
        for copy in self.second:
            copy.wait_recv()
        total = self.got[0].astype(F32)
        for h in range(1, NLON):
            total += self.got[h].astype(F32)
        return total.astype(BF16)

    def collect_modes(self):
        for copy in self.third:
            copy.wait_recv()
        total = self.got_modes[0]
        for h in range(1, NLON):
            total += self.got_modes[h]
        return total

    def close(self):
        for copy in self.first + self.second + self.third:
            copy.wait_send()


HALF = 1152


PIECE = 384


class Reduce:
    def __init__(self, x_rows, out, got1, total1, acc1, got2x, got2y, acc2x, acc2y, got3x, got3y, blocks, got4, sems):
        s1, r1, s2, r2, s3, r3, s4, r4 = sems
        self.out, self.got1, self.total1, self.acc1 = out, got1, total1, acc1
        self.blocks, self.got4 = blocks, got4
        lat, lon, batch = place()
        self.lat, self.core = lat, lax.rem(lon, 2)
        self.x = lon // 4
        self.y = lax.rem(lon // 2, 2) * 2 + batch
        core, x, y = self.core, self.x, self.y
        self.one = []
        for i, at in enumerate(range(0, out.shape[0], PIECE)):
            part = pl.ds(at, min(PIECE, out.shape[0] - at))
            self.one.append((part, remote(out.at[part], got1.at[part], s1.at[i], r1.at[i], lat, lon + 1 - 2 * core, batch)))

        def peer(along_x, k):
            if along_x:
                return lax.rem(x + k, 4), (lat, step(lon, 4 * k, NLON), batch)
            to = lax.rem(y + k, 4)
            return to, (lat, x * 4 + (to // 2) * 2 + core, lax.rem(to, 2))

        self.ways = []
        for way, (rows, got2, acc2, got3) in enumerate((
            (pl.ds(0, x_rows), got2x, acc2x, got3x), (pl.ds(x_rows, 80 - x_rows), got2y, acc2y, got3y)
        )):
            two, three = [], []
            for k in (2, 1, 3):
                to, device = peer(way == 0, k)
                src = acc1.at[:, to, rows] if way == 0 else acc1.at[to, :, rows]
                two.append(remote(src, got2.at[k - 1], s2.at[way, k - 1], r2.at[way, k - 1], *device))
                to, device = peer(way == 1, k)
                three.append(remote(acc2.at[to], got3.at[k - 1], s3.at[way, k - 1], r3.at[way, k - 1], *device))
            self.ways.append((rows, got2, acc2, got3, two, three))
        self.is_own = lat // 4 == core
        self.e_own = lax.rem(lat, 4) * 2 + core
        self.four = [
            remote(blocks.at[e], got4.at[lat], s4.at[e], r4.at[lat], core * 4 + e // 2, lon - core + e % 2, batch)
            for e in range(8)
        ]
        self.arrive = [remote(blocks.at[0], got4.at[h], s4.at[0], r4.at[h], lat, lon + 1 - 2 * core, batch) for h in range(8)]

    def halves(self, windows, grad):
        n = grad.shape[0]
        height = n // windows.shape[1]

        def piece(i):
            tap, side = i // 2, lax.rem(i, 2)
            cols = pl.ds(pl.multiple_of(side * PIECE, 128), PIECE)
            return dot_rows(windows[pl.ds(tap, height), :, cols].reshape(n, PIECE), grad)

        for i in range(3):
            self.out[PIECE * i : PIECE * i + PIECE, :] = piece(i + 3 - 3 * self.core).astype(BF16)
            self.one[i][1].start()
        for i in range(3):
            self.total1[PIECE * i : PIECE * i + PIECE, :] = piece(i + 3 * self.core)

    def first_axis(self):
        total1, acc1 = self.total1, self.acc1
        for part, copy in self.one:
            copy.wait_recv()
            total1[part, :] += self.got1[part, :].astype(F32)
        for x in range(4):
            for y in range(4):
                pieces = []
                for e in range(8):
                    w = x * 8 + (y // 2) * 4 + (e % 2) * 2 + y % 2
                    at = 288 * (e // 2) + 9 * w
                    pieces.append(total1[at : at + 9])
                for e in range(8):
                    w = x * 8 + (y // 2) * 4 + (e % 2) * 2 + y % 2
                    at = HALF + 32 * (e // 2) + w
                    pieces.append(total1[at : at + 1] if total1.shape[0] > HALF else jnp.zeros((1, C), F32))
                acc1[y, x] = jnp.concatenate(pieces, axis=0).astype(BF16)
        for i in range(3):
            for way in range(2):
                self.ways[way][4][i].start()

    def second_axis(self):
        for way, (rows, got2, acc2, _, two, three) in enumerate(self.ways):
            for copy in two:
                copy.wait_recv()
            for i in range(4):
                mine = self.acc1[i, self.x, rows] if way == 0 else self.acc1[self.y, i, rows]
                acc2[i] = (
                    mine.astype(F32) + got2[0, i].astype(F32) + got2[1, i].astype(F32) + got2[2, i].astype(F32)
                ).astype(BF16)
            for copy in three:
                copy.start()

    def to_owners(self):
        blocks, got4 = self.blocks, self.got4
        totals = []
        for way, (_, _, acc2, got3, _, three) in enumerate(self.ways):
            for copy in three:
                copy.wait_recv()
            mine = acc2[self.y if way == 0 else self.x]
            totals.append(mine.astype(F32) + got3[0].astype(F32) + got3[1].astype(F32) + got3[2].astype(F32))
        total = jnp.concatenate(totals, axis=0)
        for e in range(8):
            rows = [total[9 * e : 9 * e + 9], total[72 + e : 73 + e], jnp.zeros((6, C), F32)]
            blocks[e] = jnp.concatenate(rows, axis=0).astype(BF16)
        for e in range(8):
            mine = self.is_own & (self.e_own == e)

            @pl.when(jnp.logical_not(mine))
            def _():
                self.four[e].start()

            @pl.when(mine)
            def _():
                got4[self.lat] = blocks[e]

    def finish(self):
        got4 = self.got4
        total = None
        for h in range(8):

            @pl.when(jnp.logical_not(self.is_own & (self.lat == h)))
            def _():
                self.arrive[h].wait_recv()

        for h in range(8):
            total = got4[h].astype(F32) if h == 0 else total + got4[h].astype(F32)
        for e in range(8):

            @pl.when(jnp.logical_not(self.is_own & (self.e_own == e)))
            def _():
                self.four[e].wait_send()

        for copy in [c for _, c in self.one] + [c for way in self.ways for c in way[4] + way[5]]:
            copy.wait_send()
        return total


INPUTS = (
    "field", "hpick", "cot", "dec", "sum8", "hplace", "k0", "pool2", "k1", "pool4", "pick", "gain", "table", "synth", "mixing", "place",
    "up4", "up2", "up8",
)


def kernel(scales, n_in, *refs):
    src = dict(zip(INPUTS, refs[:n_in]))
    out_pred, out0, out1, outm, outg = refs[n_in : n_in + 5]
    names = list(INPUTS)
    v = dict(zip(names, refs[n_in + 5 :]))
    (
        load_sem, packed, halo_in, rows_top, rows_bot, fs, x3, x3c, l0f, c1s, x13, level0, da0, level1, a1, p1, slot, gl2, edges, ring, halo_s, halo_r,
        edge_s, edge_r, spec1, spec2, sc, coef, slot2, level2, pred, pred_sem,
        g1s, slope, xg, gp0, mixes, red0, red1, gain_in, gain_got, gain_s, gain_r,
    ) = refs[n_in + 5 + len(names) :]
    cot, k0, k1, gain, table, mixing = (v[n] for n in ("cot", "k0", "k1", "gain", "table", "mixing"))
    field = v["field"]
    lat, lon, batch = place()

    n_peers = greet_all()
    loads = {}
    for i, n in enumerate(names):
        ref = src[n].at[dict(synth=lat, table=lon)[n]] if n in ("synth", "table") else src[n]
        loads[n] = pltpu.make_async_copy(ref, v[n], load_sem.at[i])
    early = ("field", "hpick", "k0", "cot", "dec", "sum8")
    for n in early:
        loads[n].start()
    loads["field"].wait()
    loads["hpick"].wait()
    packed[...] = dot(v["hpick"][...], field[...].reshape(768, C)).astype(BF16)
    fs[3:19, 16:64] = field[...].astype(F32)
    loads["k0"].wait()

    def level_rows(y, n, c0, c1):
        size = n * (c1 - c0)
        acc = dot(x3[pl.ds(y, n), c0:c1].reshape(size, 3 * C), k0[0])
        acc += dot(x3[pl.ds(y + 1, n), c0:c1].reshape(size, 3 * C), k0[1])
        acc += dot(x3[pl.ds(y + 2, n), c0:c1].reshape(size, 3 * C), k0[2])
        act, grad = gelu_both(acc)
        out = fs[pl.ds(y + 1, n), 8 + c0 : 8 + c1, :] + act.reshape(n, c1 - c0, C)
        l0f[pl.ds(y, n), c0:c1] = out.astype(BF16)
        a, b = max(c0, 8), min(c1, 56)
        level0[pl.ds(y, n), a - 8 : b - 8] = out[:, a - c0 : b - c0].astype(BF16)
        da0[pl.ds(y, n), a - 8 : b - 8] = grad.reshape(n, c1 - c0, C)[:, a - c0 : b - c0].astype(BF16)

    for b in range(3):
        x3[3:19, 16:48, b * C : (b + 1) * C] = fs[3:19, 23 + b : 55 + b, :].astype(BF16)
    lax.fori_loop(0, 2, lambda i, _: (level_rows(4 + 6 * i, 6, 16, 48), 0)[1], 0)
    pl.semaphore_wait(pltpu.get_barrier_semaphore(), n_peers)
    halo = halo_copies(field, rows_top, rows_bot, packed, halo_in, halo_s, halo_r)
    for copy in halo:
        copy.start()
    for n in names:
        if n not in early:
            loads[n].start()

    for n in ("cot", "dec", "sum8"):
        loads[n].wait()
    for half in range(2):
        part = cot[8 * half : 8 * half + 8].reshape(384, C)
        a1[4 * half : 4 * half + 4] = dot(v["dec"][...], part).reshape(4, 32, C)
        gl2[8 * half : 8 * half + 8] = dot(v["sum8"][...], part)
    c1s[...] = jnp.zeros_like(c1s)
    g1s[...] = jnp.zeros_like(g1s)
    for n in ("hplace", "pool2", "k1", "pool4", "pick"):
        loads[n].wait()

    for copy in halo:
        copy.wait()

    edge_top = lat == 0
    edge_bot = lat == NLAT - 1
    fs[0:3, 16:64] = jnp.where(edge_top, 0.0, rows_top[...].astype(F32))
    fs[19:22, 16:64] = jnp.where(edge_bot, 0.0, rows_bot[...].astype(F32))
    sides = dot(v["hplace"][...], halo_in[...]).reshape(22, 32, C)
    for half, at in ((0, 0), (16, 64)):
        fs[0:3, at : at + 16] = jnp.where(edge_top, 0.0, sides[0:3, half : half + 16])
        fs[3:19, at : at + 16] = sides[3:19, half : half + 16]
        fs[19:22, at : at + 16] = jnp.where(edge_bot, 0.0, sides[19:22, half : half + 16])
    for b in range(3):
        lane = slice(b * C, (b + 1) * C)
        x3[0:3, :, lane] = fs[0:3, 7 + b : 71 + b, :].astype(BF16)
        x3[19:22, :, lane] = fs[19:22, 7 + b : 71 + b, :].astype(BF16)
        x3[3:19, 0:16, lane] = fs[3:19, 7 + b : 23 + b, :].astype(BF16)
        x3[3:19, 48:64, lane] = fs[3:19, 55 + b : 71 + b, :].astype(BF16)
    lax.fori_loop(0, 2, lambda i, _: (level_rows(16 * i, 4, 0, 64), 0)[1], 0)
    level_rows(4, 12, 0, 16)
    level_rows(4, 12, 48, 64)

    for y in range(10):
        row = dot(v["pool2"][...], l0f[2 * y : 2 * y + 2].reshape(128, C)).astype(BF16).astype(F32)
        if y == 0:
            row = jnp.where(edge_top, 0.0, row)
        if y == 9:
            row = jnp.where(edge_bot, 0.0, row)
        c1s[y, 8:40, :] = row
    for b in range(3):
        x13[:, :, b * C : (b + 1) * C] = c1s[:, 7 + b : 39 + b, :].astype(BF16)
    pre = dot(x13[0:8].reshape(256, 3 * C), k1[0])
    pre += dot(x13[1:9].reshape(256, 3 * C), k1[1])
    pre += dot(x13[2:10].reshape(256, 3 * C), k1[2])
    act, _ = gelu_both(pre)
    col = lax.broadcasted_iota(jnp.int32, (8, 32, C), 1)
    mine = (col >= 4) & (col < 28)
    p1[...] = jnp.where(mine, pre.reshape(8, 32, C), 0.0)
    lev1 = jnp.where(mine, c1s[1:9, 8:40, :] + act.reshape(8, 32, C), 0.0).astype(BF16)
    level1[...] = lev1
    for half in range(2):
        slot[8 * half : 8 * half + 8] = dot(v["pool4"][...], lev1[4 * half : 4 * half + 4].reshape(128, C)).astype(BF16)

    forth = Spectral(slot, *spec1[:5], *spec1[5:])
    forth.begin()
    edges[:, 0] = dot(v["pick"][...], a1[...].reshape(256, C).astype(BF16)).astype(BF16).reshape(4, 16, C)
    edges[:, 1] = dot(v["pick"][...], p1[...].reshape(256, C).astype(BF16)).astype(BF16).reshape(4, 16, C)
    edge = edge_copies(edges, ring, edge_s, edge_r)
    for copy in edge:
        copy.start()
    for n in ("gain", "table", "synth", "mixing", "place", "up4", "up2", "up8"):
        loads[n].wait()
    for b in range(3):
        x3c[:, :, b * C : (b + 1) * C] = fs[2:20, 15 + b : 63 + b, :].astype(BF16)
    forth.spread(table, gain, 1.0, v["synth"], sc, coef)
    for copy in edge:
        copy.wait()
    g1s[:, 8:40, :] = dot(v["place"][...], ring[:, 0].reshape(160, C)).reshape(10, 32, C)
    g1s[1:9, 8:40, :] += a1[...]
    slope[...] = dot(v["place"][...], ring[:, 1].reshape(160, C)).reshape(10, 32, C)
    slope[1:9] += p1[...]
    _, grad1 = gelu_both(slope[...])
    slope[...] = grad1
    filt = forth.collect()
    mixed = dot(filt, mixing[...])
    act, grad = gelu_both(mixed)
    cell = lax.rem(lax.broadcasted_iota(jnp.int32, (16, C), 0), 8)
    gm = jnp.where((cell >= 1) & (cell < 7), gl2[...] * grad, 0.0).astype(BF16)
    slot2[...] = dot_cols(gm, mixing[...]).astype(BF16)

    sum1 = Reduce(32, *red1[:12], red1[12:])
    sum0 = Reduce(48, *red0[:12], red0[12:])

    back_way = Spectral(slot2, *spec2[:5], *spec2[5:])
    back_way.begin()
    level2[...] = (slot[...].astype(F32) + act).astype(BF16)
    mix = dot_rows(filt, gm)
    mixes[...] = mix
    sum1.out[HALF : HALF + 128, :] = mixes[pl.ds(pl.multiple_of(128 - 128 * sum1.core, 128), 128), :].astype(BF16)
    sum1.total1[HALF : HALF + 128, :] = mixes[pl.ds(pl.multiple_of(128 * sum1.core, 128), 128), :]
    sum1.one[3][1].start()
    spec_own = forth.collect_modes()

    def predict(r):
        low = dot(v["up2"][...], level1[r]) + dot(v["up8"][...], level2[8 * (r // 4) : 8 * (r // 4) + 8])
        high = level0[2 * r + 2 : 2 * r + 4].astype(F32) + low.reshape(2, 48, C)
        pred[2 * r : 2 * r + 2] = high.astype(BF16)

    for r in range(4):
        predict(r)
    back_way.spread(table, gain, -1.0, v["synth"], sc, coef)
    for r in range(4, 8):
        predict(r)
    pred_out = pltpu.make_async_copy(pred, out_pred, pred_sem)
    pred_out.start()

    back = back_way.collect()
    gl1 = g1s[:, 8:40, :] + dot(v["up4"][...], back).reshape(10, 32, C)
    col = lax.broadcasted_iota(jnp.int32, (10, 32, C), 1)
    row = lax.broadcasted_iota(jnp.int32, (10, 32, C), 0)
    first = jnp.where(edge_top, 1, 0)
    last = jnp.where(edge_bot, 9, 10)
    valid = (col >= 3) & (col < 29) & (row >= first) & (row < last)
    gp1 = jnp.where(valid, gl1 * slope[...], 0.0)
    g1s[:, 8:40, :] = gp1
    gown = jnp.where((col[1:9] >= 4) & (col[1:9] < 28), gp1[1:9], 0.0).astype(BF16).reshape(256, C)
    sum1.halves(x13, gown)

    gc1 = gl1[1:9].reshape(256, C)
    for b in range(3):
        xg[...] = g1s[:, 7 + b : 39 + b, :].astype(BF16)
        for a in range(3):
            gc1 += dot_cols(xg[a : a + 8].reshape(256, C), k1[2 - a, (2 - b) * C : (3 - b) * C, :])
    high = gc1.astype(BF16)
    low = (gc1 - high.astype(F32)).astype(BF16)
    for r in range(8):
        up = dot(v["up2"][...], high[32 * r : 32 * r + 32]) + dot(v["up2"][...], low[32 * r : 32 * r + 32])
        gl0 = cot[2 * r : 2 * r + 2].astype(F32) + 0.25 * up.reshape(2, 48, C)
        gp0[2 * r : 2 * r + 2] = (gl0 * da0[2 * r + 2 : 2 * r + 4].astype(F32)).astype(BF16)
    sum1.first_axis()
    sum0.halves(x3c, gp0[...].reshape(768, C))

    sum0.first_axis()

    grads = back_way.collect_modes()
    m = lax.rem(4 * lon + lax.broadcasted_iota(jnp.int32, (4, C), 0), 32)
    weight = jnp.where(m == 0, 1.0, 2.0)
    ar, ai, br, bi = spec_own[0:4], spec_own[4:8], grads[0:4], grads[4:8]
    rest = jnp.zeros((4, C), F32)
    gain_in[:, :C] = jnp.concatenate([weight * (ar * br + ai * bi), rest], axis=0)
    gain_in[:, C:] = jnp.concatenate([weight * (ar * bi - ai * br), rest], axis=0)
    swap = remote(gain_in, gain_got, gain_s, gain_r, lat, lon, 1 - batch)
    swap.start()

    sum1.second_axis()
    sum0.second_axis()
    sum1.to_owners()
    swap.wait()
    gain_in[...] = gain_in[...] + gain_got[...]
    for batch_at in range(2):

        @pl.when(batch == batch_at)
        def _():
            for i in range(2):
                for j in range(4):
                    row = 2 * batch_at + i
                    outg[4 * i + j : 4 * i + j + 1, :] = gain_in[row : row + 1, 128 * j : 128 * j + 128]

    sum0.to_owners()
    t1 = sum1.finish()
    for r in range(9):
        for j in range(2):
            out1[2 * r + j : 2 * r + j + 1, :] = scales[1] * t1[r : r + 1, 128 * j : 128 * j + 128]
    for j in range(2):
        outm[j : j + 1, :] = scales[2] * t1[9:10, 128 * j : 128 * j + 128]
    t0 = sum0.finish()
    for r in range(9):
        for j in range(2):
            out0[2 * r + j : 2 * r + j + 1, :] = scales[0] * t0[r : r + 1, 128 * j : 128 * j + 128]
    forth.close()
    back_way.close()
    pred_out.wait()


def dma(*n):
    return pltpu.SemaphoreType.DMA(n)


def vmem(*shape, dtype=BF16):
    return pltpu.VMEM(shape, dtype)


def reduce_scratch(rows, x_rows):
    y_rows = 80 - x_rows
    return (
        vmem(rows, C), vmem(rows, C), vmem(rows, C, dtype=F32), vmem(4, 4, 80, C),
        vmem(3, 4, x_rows, C), vmem(3, 4, y_rows, C), vmem(4, x_rows, C), vmem(4, y_rows, C),
        vmem(3, x_rows, C), vmem(3, y_rows, C), vmem(8, 16, C), vmem(8, 16, C),
        dma(4), dma(4), dma(2, 3), dma(2, 3), dma(2, 3), dma(2, 3), dma(8), dma(8),
    )


def hand_over(*arrays):
    n = len(arrays)

    def body(*refs):
        src, dst, buf, (come, go) = refs[:n], refs[n : 2 * n], refs[2 * n : 3 * n], refs[3 * n :]
        inward = [pltpu.make_async_copy(src[i], buf[i], come.at[i]) for i in range(n)]
        outward = [pltpu.make_async_copy(buf[i], dst[i], go.at[i]) for i in range(n)]
        for copy in inward:
            copy.start()
        for i in range(n):
            inward[i].wait()
            outward[i].start()
        for copy in outward:
            copy.wait()

    anywhere = pl.BlockSpec(memory_space=pl.ANY)
    return pl.pallas_call(
        body, out_shape=[jax.ShapeDtypeStruct(a.shape, a.dtype) for a in arrays], in_specs=[anywhere] * n,
        out_specs=[anywhere] * n, scratch_shapes=[vmem(*a.shape, dtype=a.dtype) for a in arrays] + [dma(n), dma(n)],
    )(*arrays)


def on_device(tables, field, kernel0, kernel1, mixing, gain, cotangent):
    table, synth, small = tables
    args = {k: jnp.asarray(a) for k, a in small.items()}
    args |= dict(
        field=field[0], cot=cotangent[0], k0=kernel0.reshape(3, 3 * C, C), k1=kernel1.reshape(3, 3 * C, C),
        mixing=mixing, gain=gain, table=jnp.asarray(table), synth=jnp.asarray(synth),
    )
    cells0 = 2 * 128 * 768
    scales = (1.0 / math.sqrt(cells0), 1.0 / math.sqrt(cells0 // 4), 1.0 / math.sqrt(cells0 // 64))
    names = INPUTS
    scratch = [
        vmem(*args[n].shape[1:]) if n in ("synth", "table") else vmem(*args[n].shape, dtype=args[n].dtype) for n in names
    ]

    def spectral_scratch(rows):
        sems = (dma(7), dma(8), dma(15), dma(15), dma(15), dma(15))
        modes = vmem(NLON, 8, C, dtype=F32)
        return (vmem(NLAT, 16, C), vmem(NLON, rows, C), vmem(NLON, rows, C), modes, modes, *sems)

    scratch += [
        dma(len(names)), vmem(160, C), vmem(160, C), vmem(3, 48, C), vmem(3, 48, C), vmem(22, 80, C, dtype=F32), vmem(22, 64, 3 * C), vmem(18, 48, 3 * C),
        vmem(20, 64, C), vmem(10, 48, C, dtype=F32), vmem(10, 32, 3 * C), vmem(20, 48, C), vmem(20, 48, C),
        vmem(8, 32, C), vmem(8, 32, C, dtype=F32), vmem(8, 32, C, dtype=F32), vmem(16, C), vmem(16, C, dtype=F32),
        vmem(4, 2, 16, C), vmem(10, 2, 16, C), dma(8), dma(8), dma(8), dma(8),
        spectral_scratch(16), spectral_scratch(32), vmem(1024, C, dtype=F32), vmem(1024, C),
        vmem(16, C), vmem(16, C), vmem(ROWS, COLS, C), dma(),
        vmem(10, 48, C, dtype=F32), vmem(10, 32, C, dtype=F32), vmem(10, 32, C), vmem(16, 48, C),
        vmem(C, C, dtype=F32), reduce_scratch(HALF, 48), reduce_scratch(HALF + 128, 32), vmem(8, 2 * C, dtype=F32), vmem(8, 2 * C, dtype=F32), dma(), dma(),
    ]
    anywhere = pl.BlockSpec(memory_space=pl.ANY)
    here = pl.BlockSpec(memory_space=pltpu.VMEM)
    predicted, grad0, grad1, gradm, gradg = pl.pallas_call(
        functools.partial(kernel, scales, len(INPUTS)),
        out_shape=[jax.ShapeDtypeStruct((ROWS, COLS, C), BF16)]
        + [jax.ShapeDtypeStruct((n, 128), F32) for n in (18, 18, 2, 8)],
        in_specs=[anywhere] * len(INPUTS),
        out_specs=[anywhere] + [here] * 4,
        scratch_shapes=scratch,
        compiler_params=pltpu.CompilerParams(collective_id=0, has_side_effects=True, vmem_limit_bytes=VMEM_BYTES),
    )(*[args[n] for n in INPUTS])
    predicted, grad0, grad1, gradm, gradg = hand_over(predicted, grad0, grad1, gradm, gradg)
    return predicted[None], grad0.reshape(-1), grad1.reshape(-1), gradm.reshape(-1), gradg.reshape(-1)


def solution(mesh):
    tables = (*spectral_tables(), cell_tables())
    tile = P("batch", "lat", "lon", None)
    split = P(("lat", "lon", "batch"))
    return jax.shard_map(
        functools.partial(on_device, tables), mesh=mesh, in_specs=(tile, P(), P(), P(), P(), tile),
        out_specs=(tile, split, split, split, split), check_vma=False,
    )
```
